512 devices in a mesh: rows: 128 (over z, x, core), modes: 4 (over y).
Axes of the slice: x: 4, y: 4, z: 16, core: 2. Of those that a mesh axis runs over, the one named last changes fastest.
Arguments:
- test_basis: bfloat16 [65536, 5, 256], P('rows'), may hold values from -0.009765625 to 0.009765625
- deim_basis: bfloat16 [65536, 5, 512], P('rows', None, 'modes'), may hold values from -6 to 6
- trial_basis: bfloat16 [65536, 5, 256], P('rows'), may hold values from -6 to 6
- jacobian: float32 [2048, 7, 5], P('rows'), may hold values from -1 to 1
- neighbours: int32 [2048, 7], P('rows'), may hold values from 0 to 65535, as said below
- counts: int32 [128], P('rows'), may hold values from 1 to 16, 512 in all
- sample_inverse: float32 [512, 512], P('modes'), may hold values from -0.01171875 to 0.01171875
Outputs:
- reduced_operator: float32 [256, 256], P('modes', 'rows')
The draws below stay inside these ranges and needn't reach their ends.
Inputs may be any that keep to these rules, and one draw needn't show every extreme that they name: `neighbours`: the first entry of row g is the sampled cell, which lies among the 512 cells of device g // 16; every other entry lies within 128 cells of it. Device r uses its first counts[r] slots; the counts sum to 512.
All inputs are finite; a program needn't handle non-finite values.
Results may differ from the reference program's by a relative error of at most 0.0003.
Values may be sent and summed in bfloat16 or wider, within the bound.
No kernel may reach another device: no remote copies, remote signals or barrier semaphores. Data moves between devices by JAX's collectives and lax.ppermute only.
A program may use at most 64 MiB of HBM per device.

```python
import math
import jax
import jax.numpy as jnp
import numpy as np
from jax import lax

K = 256
M = 512
NC = 5
NB = 7
HALO = 128
CELLS_DEV = 512
SLOT = 16
NCELLS = 65536
SAMPLES = 2048
N_ROWS = 128


def draw_neighbours(key, part):
    first, second = jax.random.split(jax.random.fold_in(key, 11))
    total = N_ROWS * SLOT
    device = jnp.arange(total, dtype=jnp.int32) // SLOT
    centre = device * CELLS_DEV + jax.random.randint(first, (total,), 0, CELLS_DEV)
    reach = jax.random.randint(second, (total, NB - 1), -HALO, HALO + 1)
    others = jnp.clip(centre[:, None] + reach, 0, N_ROWS * CELLS_DEV - 1)
    return jnp.concatenate([centre[:, None], others], axis=1).astype(jnp.int32)


def levels(stream_key, shape, shards, low, top_value):
    def one(dim, shards_of):
        draws = jax.random.uniform(jax.random.fold_in(jax.random.fold_in(stream_key, 6), dim), (shards_of,), jnp.float32, low / len(shards), top_value / len(shards))
        return jnp.repeat(jnp.exp(draws), shape[dim] // shards_of).reshape((-1,) + (1,) * (len(shape) - dim - 1))

    gain = one(*shards[0])
    for cut in shards[1:]:
        gain = gain * one(*cut)
    return gain


def split_up(count, total, bound, slope):
    loads = [(1 << 20) // math.isqrt(grade ** slope) + 1 for grade in range(2, count + 1)]
    surplus, given = total - bound - (count - 1), [1] * (count - 1)
    while surplus > 0:
        candidates = [i for i in range(count - 1) if given[i] < bound]
        pool, budget = sum([loads[i] for i in candidates]), surplus
        for i in candidates:
            more = min(bound - given[i], max(1, budget * loads[i] // pool), surplus)
            given[i] = given[i] + more
            surplus = surplus - more
    return np.array([bound] + given)


def uneven(own_key, amount, total, most, lean):
    if amount == 2:
        one = jax.random.randint(own_key, (), max(1, total - most), min(most, total - 1) + 1)
        return jnp.stack([one, total - one])
    tallies = jnp.asarray(split_up(amount, total, most, lean), jnp.int32)
    pairs = (amount - 1) // 2
    donor, receiver = tallies[1:1 + 2 * pairs:2], tallies[2:2 + 2 * pairs:2]
    room = jnp.minimum(donor - 1, most - receiver)
    moved = jax.random.randint(jax.random.fold_in(own_key, 1), (pairs,), 0, 1 << 20) % (room + 1)
    tallies = tallies.at[1:1 + 2 * pairs:2].set(donor - moved).at[2:2 + 2 * pairs:2].set(receiver + moved)
    return tallies[jax.random.permutation(jax.random.fold_in(own_key, 2), amount)]


def gaussian(rng, dims, width, most, cuts=(), held_as=jnp.bfloat16):
    drawn = jax.random.normal(rng, dims, jnp.float32) * width
    if len(cuts) > 0:
        drawn = levels(rng, dims, cuts, -0.22, 0.18) * drawn
    return jnp.clip(drawn, min=-most, max=most).astype(held_as)


def setup_inputs(seed: int = 0) -> dict:
    seeds = jax.random.split(jax.random.key(seed), 8)
    return {
        "test_basis": gaussian(seeds[0], (NCELLS, NC, K), (NCELLS * 5) ** -0.5, 0.009765625, ((0, 128),)),
        "deim_basis": gaussian(seeds[1], (NCELLS, NC, M), 1.0, 6.0, ((0, 128), (2, 4))),
        "trial_basis": gaussian(seeds[2], (NCELLS, NC, K), 1.0, 6.0, ((0, 128),)),
        "jacobian": gaussian(seeds[3], (SAMPLES, NB, NC), (NB * 5) ** -0.5, 1.0, ((0, 128),), jnp.float32),
        "neighbours": draw_neighbours(jax.random.fold_in(seeds[7], 71), 0),
        "counts": uneven(seeds[5], N_ROWS, M, SLOT, 2).astype(jnp.int32),
        "sample_inverse": gaussian(seeds[6], (M, M), (M * M) ** -0.5, 0.01171875, ((0, 4),), jnp.float32),
    }


def reference(test_basis, deim_basis, trial_basis, jacobian, neighbours, counts, sample_inverse):
    flat_test = test_basis.reshape(-1, K).astype(jnp.float32)
    flat_deim = deim_basis.reshape(-1, M).astype(jnp.float32)
    projection = lax.dot_general(flat_test, flat_deim, (((0,), (0,)), ((), ())), precision=lax.Precision.HIGHEST, preferred_element_type=jnp.float32)
    offset = jnp.cumsum(counts) - counts
    total = neighbours.shape[0]
    slot_ids = jnp.arange(total, dtype=jnp.int32)
    device = slot_ids // SLOT
    within = slot_ids % SLOT
    live = within < counts[device]
    row_ids = jnp.where(live, offset[device] + within, 0).astype(jnp.int32)
    picked = trial_basis[neighbours].astype(jnp.float32)
    contrib = jnp.einsum("snj,snjk->sk", jacobian.astype(jnp.float32), picked, precision=lax.Precision.HIGHEST)
    contrib = contrib * live[:, None].astype(jnp.float32)
    sampled = jnp.zeros((M, K), jnp.float32).at[row_ids].add(contrib)
    folded = jnp.dot(projection, sample_inverse, precision=lax.Precision.HIGHEST, preferred_element_type=jnp.float32)
    return jnp.dot(folded, sampled, precision=lax.Precision.HIGHEST, preferred_element_type=jnp.float32)
```

```python
import jax
import jax.numpy as jnp
from jax import lax
from jax.experimental import pallas as pl
from jax.experimental.pallas import tpu as pltpu
from jax.sharding import Mesh
from jax.sharding import PartitionSpec as P

ROWS = ("z", "x", "c")
PLANE = ("x", "c")
CUBE = ("x", "c", "y")
F32 = jnp.float32
BF16 = jnp.bfloat16
NC, NB = 5, 7
JAC, NBR, CNT = 0, 35, 42
PLANE_CNT, LOW_CNT, OWN_CNT, RANK = 48, 56, 57, 58


def whole(shape):
    return pl.BlockSpec(shape, lambda *_: (0,) * len(shape))


def lanes(shape):
    return lax.broadcasted_iota(jnp.int32, shape, len(shape) - 1)


def project_kernel(v_ref, d_ref, table_ref, out_ref, acc_ref):
    step = pl.program_id(0)
    part = lax.dot_general(
        d_ref[0], v_ref[0], (((0,), (0,)), ((), ())), preferred_element_type=F32
    )

    @pl.when(step == 0)
    def _():
        acc_ref[...] = part

    @pl.when(step > 0)
    def _():
        acc_ref[...] += part

    @pl.when(step == NC - 1)
    def _():
        g = acc_ref[...].T
        count = jnp.broadcast_to(table_ref[0:8, CNT : CNT + 1], (8, 128))
        for p in range(8):
            for m in range(4):
                row = 64 * m + 8 * p
                out_ref[p, 8 * m : 8 * m + 8, :] = g[row : row + 8, :]
            out_ref[p, 32:40, :] = count


def project(test, deim, table):
    return pl.pallas_call(
        project_kernel,
        grid=(NC,),
        in_specs=[
            pl.BlockSpec((1, 512, 256), lambda j: (j, 0, 0)),
            pl.BlockSpec((1, 512, 128), lambda j: (j, 0, 0)),
            whole((16, 128)),
        ],
        out_specs=whole((8, 40, 128)),
        out_shape=jax.ShapeDtypeStruct((8, 40, 128), F32),
        scratch_shapes=[pltpu.VMEM((128, 256), F32)],
        name="project",
    )(test, deim, table)


def sample_kernel(low_ref, own_ref, high_ref, u_ref, out_ref):
    rank = jnp.floor(own_ref[0:1, NBR : NBR + 1] * (1.0 / 512.0))
    slot = lax.broadcasted_iota(jnp.int32, (16, 128), 0).astype(F32)
    entry = lanes((16, 128)) < NBR
    tables = []
    for ref in (low_ref, own_ref, high_ref):
        rows = ref[...]
        dead = entry & (slot >= rows[:, CNT : CNT + 1])
        tables.append(jnp.where(dead, 0.0, rows))
    table = jnp.concatenate(tables, axis=0)
    values = [jnp.broadcast_to(table[:, k : k + 1], (48, 128)) for k in range(NBR)]
    near = [table[:, NBR + n : NBR + n + 1] - rank * 512.0 for n in range(NB)]
    total = jnp.zeros((144, 256), F32)
    for chunk in range(4):
        cell = (lanes((48, 128)) + 128 * chunk).astype(F32)
        hits = [cell == near[n] for n in range(NB)]
        for j in range(NC):
            weight = jnp.where(hits[0], values[j], 0.0)
            for n in range(1, NB):
                weight = weight + jnp.where(hits[n], values[n * NC + j], 0.0)
            w0 = weight.astype(BF16)
            rest = weight - w0.astype(F32)
            w1 = rest.astype(BF16)
            w2 = (rest - w1.astype(F32)).astype(BF16)
            stacked = jnp.concatenate([w0, w1, w2], axis=0)
            total = total + jnp.dot(
                stacked,
                u_ref[j, 128 * chunk : 128 * chunk + 128, :],
                preferred_element_type=F32,
            )
    rows = total[0:48, :] + (total[48:96, :] + total[96:144, :])
    rows = jnp.concatenate([rows, jnp.zeros((80, 256), F32)], axis=0)
    lane = lanes((1, 128))
    extra = jnp.where(lane == LOW_CNT, low_ref[0:1, CNT : CNT + 1], 0.0)
    extra = extra + jnp.where(lane == OWN_CNT, own_ref[0:1, CNT : CNT + 1], 0.0)
    extra = extra + jnp.where(lane == RANK, rank, 0.0)
    cols = rows.T + extra
    for z in range(16):
        out_ref[z, :, :] = cols[16 * z : 16 * z + 16, :]


def sample(low, own, high, trial):
    return pl.pallas_call(
        sample_kernel,
        out_shape=jax.ShapeDtypeStruct((16, 16, 128), F32),
        name="sample",
    )(low, own, high, trial)


def merge_kernel(g_ref, b_ref, out_ref):
    total = g_ref[0, 0:32, :]
    for p in range(1, 8):
        total = total + g_ref[p, 0:32, :]
    lane = lanes((1, 128))
    counts = jnp.zeros((1, 128), F32)
    for p in range(8):
        counts = counts + jnp.where(lane == PLANE_CNT + p, g_ref[p, 32:33, :], 0.0)
    for z in range(16):
        out_ref[z, 0:32, :] = total
        out_ref[z, 32:48, :] = b_ref[z, :, :] + counts


def merge(g_parts, columns):
    return pl.pallas_call(
        merge_kernel,
        out_shape=jax.ShapeDtypeStruct((16, 48, 128), F32),
        name="merge",
    )(g_parts, columns)


def fold_kernel(x_ref, s_ref, out_ref):
    total = x_ref[0, 0:32, :]
    for z in range(1, 16):
        total = total + x_ref[z, 0:32, :]
    info = x_ref[:, 32, :]
    lane = lanes((16, 128))

    def column(k):
        return jnp.sum(jnp.where(lane == k, info, 0.0), axis=1, keepdims=True)

    rank = column(RANK)
    place = rank - 8.0 * jnp.floor(rank * 0.125)
    is_count = (lane >= PLANE_CNT) & (lane < PLANE_CNT + 8)
    counts = jnp.where(is_count, info, 0.0)
    before = lax.broadcasted_iota(jnp.int32, (16, 16), 1) < lax.broadcasted_iota(
        jnp.int32, (16, 16), 0
    )
    lower = jnp.dot(before.astype(F32), counts, preferred_element_type=F32)
    ahead = (lane - PLANE_CNT).astype(F32) < place
    lower = lower + jnp.where(ahead, counts, 0.0)
    offset = jnp.sum(lower, axis=1, keepdims=True)
    shift = jnp.where(lane < 16, -column(LOW_CNT), jnp.where(lane < 32, 0.0, column(OWN_CNT)))
    ids = offset + shift + (lane % 16).astype(F32)
    ids = jnp.where(lane < 48, ids, -1.0)
    mode = lax.broadcasted_iota(jnp.int32, (512, 128), 0).astype(F32)
    slots = lanes((16, 128)) < 48
    full = jnp.zeros((32, 512), F32)
    for z in range(16):
        hot = jnp.where(mode == ids[z : z + 1, :], 1.0, 0.0).astype(BF16)
        cols = jnp.where(slots, x_ref[z, 32:48, :], 0.0)
        high = cols.astype(BF16)
        low = (cols - high.astype(F32)).astype(BF16)
        both = jnp.concatenate([high, low], axis=0)
        full = full + lax.dot_general(
            both, hot, (((1,), (1,)), ((), ())), preferred_element_type=F32
        )
    sampled = full[0:16, :] + full[16:32, :]
    c = lax.dot_general(
        sampled,
        s_ref[...],
        (((1,), (1,)), ((), ())),
        precision=lax.Precision.HIGHEST,
        preferred_element_type=F32,
    )
    blank = jnp.zeros((6, 128), F32)
    for p in range(8):
        mine = jnp.concatenate([c[2 * p : 2 * p + 2, :], blank], axis=0)
        for m in range(4):
            out_ref[4 * p + m, 0:8, :] = total[8 * m : 8 * m + 8, :]
            out_ref[4 * p + m, 8:16, :] = mine


def fold(parts, inverse):
    return pl.pallas_call(
        fold_kernel,
        out_shape=jax.ShapeDtypeStruct((32, 16, 128), F32),
        name="fold",
    )(parts, inverse)


def finish_kernel(x_ref, out_ref):
    for j in range(2):
        c = []
        for m in range(4):
            total = x_ref[m, 8 + j : 9 + j, :]
            for p in range(1, 8):
                total = total + x_ref[4 * p + m, 8 + j : 9 + j, :]
            c.append(total)
        for p in range(8):
            acc = x_ref[4 * p, 0:8, :] * c[0]
            for m in range(1, 4):
                acc = acc + x_ref[4 * p + m, 0:8, :] * c[m]
            out_ref[8 * p : 8 * p + 8, j : j + 1] = jnp.sum(acc, axis=1, keepdims=True)


def finish(parts):
    return pl.pallas_call(
        finish_kernel,
        out_shape=jax.ShapeDtypeStruct((64, 2), F32),
        name="finish",
    )(parts)


def shards(test_basis, deim_basis, trial_basis, jacobian, neighbours, counts, sample_inverse):
    slots = neighbours.shape[0]
    own = jnp.concatenate(
        [
            jacobian.reshape(slots, NB * NC),
            neighbours.astype(F32),
            jnp.broadcast_to(counts.astype(F32)[None, :], (slots, 1)),
            jnp.zeros((slots, 128 - NB * NC - NB - 1), F32),
        ],
        axis=1,
    )
    groups = lax.axis_size(ROWS)
    up = [(i, i + 1) for i in range(groups - 1)]
    down = [(i + 1, i) for i in range(groups - 1)]
    low = lax.ppermute(own, ROWS, up)
    high = lax.ppermute(own, ROWS, down)
    g_part = project(test_basis.swapaxes(0, 1), deim_basis.swapaxes(0, 1), own)
    g_plane = lax.all_to_all(g_part, PLANE, 0, 0, tiled=True)
    columns = sample(low, own, high, trial_basis.swapaxes(0, 1))
    parts = lax.all_to_all(merge(g_plane, columns), "z", 0, 0, tiled=True)
    pieces = lax.all_to_all(fold(parts, sample_inverse), CUBE, 0, 0, tiled=True)
    return finish(pieces)


def solution(mesh):
    split = Mesh(mesh.devices.reshape(16, 4, 2, 4), ("z", "x", "c", "y"))
    placed = (
        P(ROWS, None, None),
        P(ROWS, None, "y"),
        P(ROWS, None, None),
        P(ROWS, None, None),
        P(ROWS, None),
        P(ROWS),
        P("y", None),
    )
    return jax.shard_map(
        shards, mesh=split, in_specs=placed, out_specs=P("y", ROWS), check_vma=False
    )
```

```python
import jax
import jax.numpy as jnp
from jax import lax
from jax.experimental import pallas as pl
from jax.experimental.pallas import tpu as pltpu
from jax.sharding import Mesh
from jax.sharding import PartitionSpec as P

ROWS = ("z", "x", "c")
PLANE = ("x", "c")
CUBE = ("x", "c", "y")
F32 = jnp.float32
BF16 = jnp.bfloat16
NC, NB = 5, 7
NBR, CNT = 40, 47
PLANE_CNT, LOW_CNT, OWN_CNT, RANK, G_EXP, B_EXP = 96, 104, 105, 106, 107, 108
TOP = 32000.0
FINE = 65536.0


def whole(shape):
    return pl.BlockSpec(shape, lambda *_: (0,) * len(shape))


def lanes(shape):
    return lax.broadcasted_iota(jnp.int32, shape, len(shape) - 1)


def exponent(x):
    top = jnp.max(jnp.abs(x), axis=(0, 1), keepdims=True)
    return jnp.floor(-jnp.log2(jnp.maximum(top, 1e-30)))


def nearest(x):
    return jnp.floor(x + 0.5)


def to_i16(x):
    return x.astype(jnp.int32).astype(jnp.int16)


def from_i16(x):
    return x.astype(jnp.int32).astype(F32)


def table_kernel(jac_ref, nbr_ref, count_ref, out_ref):
    blank = jnp.zeros((1, 16), F32)
    rows = []
    for j in range(NC):
        rows += [jac_ref[j], blank]
    count = jnp.full((1, 16), count_ref[0].astype(F32))
    rows += [nbr_ref[...].astype(F32), count]
    table = jnp.concatenate(rows + [jnp.zeros((80, 16), F32)], axis=0)
    table = jnp.concatenate([table, jnp.zeros((128, 112), F32)], axis=1)
    out_ref[...] = table.T[0:16, :]


def make_table(jac, nbr, counts):
    return pl.pallas_call(
        table_kernel,
        in_specs=[
            pl.BlockSpec(memory_space=pltpu.VMEM),
            pl.BlockSpec(memory_space=pltpu.VMEM),
            pl.BlockSpec(memory_space=pltpu.SMEM),
        ],
        out_shape=jax.ShapeDtypeStruct((16, 128), F32),
        name="table",
    )(jac, nbr, counts)


def project_kernel(v_ref, d_ref, count_ref, out_ref, acc_ref):
    step = pl.program_id(0)
    part = lax.dot_general(
        d_ref[0], v_ref[0], (((0,), (0,)), ((), ())), preferred_element_type=F32
    )

    @pl.when(step == 0)
    def _():
        acc_ref[...] = part

    @pl.when(step > 0)
    def _():
        acc_ref[...] += part

    @pl.when(step == NC - 1)
    def _():
        g = acc_ref[...].T
        count = jnp.full((8, 128), count_ref[0].astype(F32))
        for p in range(8):
            for m in range(4):
                row = 64 * m + 8 * p
                out_ref[p, 8 * m : 8 * m + 8, :] = g[row : row + 8, :]
            out_ref[p, 32:40, :] = count


def project(test, deim, counts):
    return pl.pallas_call(
        project_kernel,
        grid=(NC,),
        in_specs=[
            pl.BlockSpec((1, 512, 256), lambda j: (j, 0, 0)),
            pl.BlockSpec((1, 512, 128), lambda j: (j, 0, 0)),
            pl.BlockSpec(memory_space=pltpu.SMEM),
        ],
        out_specs=whole((8, 40, 128)),
        out_shape=jax.ShapeDtypeStruct((8, 40, 128), F32),
        scratch_shapes=[pltpu.VMEM((128, 256), F32)],
        name="project",
        cost_estimate=pl.CostEstimate(
            flops=2 * 2560 * 256 * 128, bytes_accessed=2 * 2560 * 384, transcendentals=0
        ),
    )(test, deim, counts)


def sample_kernel(low_ref, own_ref, high_ref, u_ref, out_ref):
    rank = jnp.floor(own_ref[0:1, NBR : NBR + 1] * (1.0 / 512.0))
    slot = lax.broadcasted_iota(jnp.int32, (16, 128), 0).astype(F32)
    entry = lanes((16, 128)) < NBR
    tables = []
    for ref in (low_ref, own_ref, high_ref):
        rows = ref[...]
        dead = entry & (slot >= rows[:, CNT : CNT + 1])
        tables.append(jnp.where(dead, 0.0, rows))
    table = jnp.concatenate(tables, axis=0)
    near = [table[:, NBR + n : NBR + n + 1] - rank * 512.0 for n in range(NB)]
    total = jnp.zeros((144, 256), F32)
    values = [jnp.broadcast_to(table[:, k : k + 1], (48, 128)) for k in range(NBR)]
    for chunk in range(4):
        cell = (lanes((48, 128)) + 128 * chunk).astype(F32)
        hits = [cell == near[n] for n in range(NB)]
        for j in range(NC):
            weight = jnp.where(hits[0], values[8 * j], 0.0)
            for n in range(1, NB):
                weight = weight + jnp.where(hits[n], values[8 * j + n], 0.0)
            w0 = weight.astype(BF16)
            rest = weight - w0.astype(F32)
            w1 = rest.astype(BF16)
            w2 = (rest - w1.astype(F32)).astype(BF16)
            stacked = jnp.concatenate([w0, w1, w2], axis=0)
            total = total + jnp.dot(
                stacked,
                u_ref[j, 128 * chunk : 128 * chunk + 128, :],
                preferred_element_type=F32,
            )
    rows = total[0:48, :] + (total[48:96, :] + total[96:144, :])
    exp = exponent(rows)
    rows = rows * (jnp.exp2(exp) * TOP)
    coarse = nearest(rows)
    fine = jnp.clip(nearest((rows - coarse) * FINE), -32767.0, 32767.0)
    rows = jnp.concatenate([coarse, fine, jnp.zeros((32, 256), F32)], axis=0)
    lane = lanes((1, 128))
    extra = jnp.where(lane == LOW_CNT, low_ref[0:1, CNT : CNT + 1], 0.0)
    extra = extra + jnp.where(lane == OWN_CNT, own_ref[0:1, CNT : CNT + 1], 0.0)
    extra = extra + jnp.where(lane == RANK, rank, 0.0)
    extra = extra + jnp.where(lane == B_EXP, exp, 0.0)
    cols = rows.T + extra
    for z in range(16):
        out_ref[z, :, :] = cols[16 * z : 16 * z + 16, :]


def sample(low, own, high, trial):
    return pl.pallas_call(
        sample_kernel,
        out_shape=jax.ShapeDtypeStruct((16, 16, 128), F32),
        name="sample",
    )(low, own, high, trial)


def merge_kernel(g_ref, b_ref, out_ref):
    total = g_ref[0, 0:32, :]
    for p in range(1, 8):
        total = total + g_ref[p, 0:32, :]
    exp = exponent(total)
    share = jnp.abs(total * jnp.exp2(exp))
    code = nearest(jnp.sqrt(jnp.sqrt(share)) * TOP)
    code = to_i16(jnp.where(total < 0.0, -code, code))
    lane = lanes((1, 128))
    extra = jnp.where(lane == G_EXP, exp, 0.0)
    for p in range(8):
        extra = extra + jnp.where(lane == PLANE_CNT + p, g_ref[p, 32:33, :], 0.0)
    for z in range(16):
        out_ref[z, 0:32, :] = code
        out_ref[z, 32:48, :] = to_i16(b_ref[z, :, :] + extra)


def merge(g_parts, columns):
    return pl.pallas_call(
        merge_kernel,
        out_shape=jax.ShapeDtypeStruct((16, 48, 128), jnp.int16),
        name="merge",
    )(g_parts, columns)


def fold_kernel(x_ref, s_ref, out_ref):
    blocks = [from_i16(x_ref[z, 32:48, :]) for z in range(16)]
    info = jnp.concatenate([block[0:1, :] for block in blocks], axis=0)
    lane = lanes((16, 128))

    def column(k):
        return jnp.sum(jnp.where(lane == k, info, 0.0), axis=1, keepdims=True)

    g_scale = jnp.exp2(-column(G_EXP))
    b_scale = jnp.exp2(-column(B_EXP)) * (1.0 / TOP)
    total = jnp.zeros((32, 128), F32)
    for z in range(16):
        root = from_i16(x_ref[z, 0:32, :]) * (1.0 / TOP)
        square = root * root
        total = total + square * square * jnp.where(root < 0.0, -1.0, 1.0) * g_scale[z : z + 1, :]
    rank = column(RANK)
    place = rank - 8.0 * jnp.floor(rank * 0.125)
    is_count = (lane >= PLANE_CNT) & (lane < PLANE_CNT + 8)
    counts = jnp.where(is_count, info, 0.0)
    before = lax.broadcasted_iota(jnp.int32, (16, 16), 1) < lax.broadcasted_iota(
        jnp.int32, (16, 16), 0
    )
    lower = jnp.dot(before.astype(F32), counts, preferred_element_type=F32)
    ahead = (lane - PLANE_CNT).astype(F32) < place
    lower = lower + jnp.where(ahead, counts, 0.0)
    offset = jnp.sum(lower, axis=1, keepdims=True)
    slot = jnp.where(lane < 48, lane, lane - 48)
    shift = jnp.where(slot < 16, -column(LOW_CNT), jnp.where(slot < 32, 0.0, column(OWN_CNT)))
    ids = offset + shift + (lane % 16).astype(F32)
    ids = jnp.where(lane < 96, ids, -1.0)
    unit = jnp.where(lane < 48, 1.0, jnp.where(lane < 96, 1.0 / FINE, 0.0))
    mode = lax.broadcasted_iota(jnp.int32, (512, 128), 0).astype(F32)
    sampled = jnp.zeros((16, 512), F32)
    for z in range(16):
        hot = jnp.where(mode == ids[z : z + 1, :], 1.0, 0.0).astype(BF16)
        cols = blocks[z] * unit
        high = cols.astype(BF16)
        rest = (cols - high.astype(F32)).astype(BF16)
        part = lax.dot_general(
            jnp.concatenate([high, rest], axis=0),
            hot,
            (((1,), (1,)), ((), ())),
            preferred_element_type=F32,
        )
        sampled = sampled + (part[0:16, :] + part[16:32, :]) * b_scale[z : z + 1, :]
    c = lax.dot_general(
        sampled,
        s_ref[...],
        (((1,), (1,)), ((), ())),
        precision=lax.Precision.HIGHEST,
        preferred_element_type=F32,
    )
    g_pairs = total.reshape(16, 2, 128)
    c_pairs = c.reshape(8, 2, 128)
    for p in range(8):
        for m in range(4):
            at = 5 * (4 * p + m)
            out_ref[at : at + 4] = g_pairs[4 * m : 4 * m + 4]
            out_ref[at + 4] = c_pairs[p]


def fold(parts, inverse):
    return pl.pallas_call(
        fold_kernel,
        out_shape=jax.ShapeDtypeStruct((160, 2, 128), F32),
        name="fold",
    )(parts, inverse)


def finish_kernel(x_ref, out_ref):
    result = jnp.zeros((2, 64), F32)
    for m in range(4):
        rows = [x_ref[5 * (4 * p + m) : 5 * (4 * p + m) + 4].reshape(8, 128) for p in range(8)]
        c = x_ref[5 * m + 4]
        for p in range(1, 8):
            c = c + x_ref[5 * (4 * p + m) + 4]
        result = result + lax.dot_general(
            c,
            jnp.concatenate(rows, axis=0),
            (((1,), (1,)), ((), ())),
            precision=lax.Precision.HIGHEST,
            preferred_element_type=F32,
        )
    out_ref[...] = result


def finish(parts):
    return pl.pallas_call(
        finish_kernel,
        out_shape=jax.ShapeDtypeStruct((2, 64), F32),
        name="finish",
    )(parts)


def shards(test_basis, deim_basis, trial_basis, jacobian, neighbours, counts, sample_inverse):
    own = make_table(jacobian.transpose(2, 1, 0), neighbours.T, counts)
    groups = lax.axis_size(ROWS)
    up = [(i, i + 1) for i in range(groups - 1)]
    down = [(i + 1, i) for i in range(groups - 1)]
    low = lax.ppermute(own, ROWS, up)
    high = lax.ppermute(own, ROWS, down)
    g_part = project(test_basis.swapaxes(0, 1), deim_basis.swapaxes(0, 1), counts)
    g_part, low, high = lax.optimization_barrier((g_part, low, high))
    g_plane = lax.all_to_all(g_part, PLANE, 0, 0, tiled=True)
    columns = sample(low, own, high, trial_basis.swapaxes(0, 1))
    parts = lax.all_to_all(merge(g_plane, columns), "z", 0, 0, tiled=True)
    pieces = lax.all_to_all(fold(parts, sample_inverse), CUBE, 0, 0, tiled=True)
    return finish(pieces).T


def solution(mesh):
    split = Mesh(mesh.devices.reshape(16, 4, 2, 4), ("z", "x", "c", "y"))
    placed = (
        P(ROWS, None, None),
        P(ROWS, None, "y"),
        P(ROWS, None, None),
        P(ROWS, None, None),
        P(ROWS, None),
        P(ROWS),
        P("y", None),
    )
    return jax.shard_map(
        shards, mesh=split, in_specs=placed, out_specs=P("y", ROWS), check_vma=False
    )
```

```python
import jax
import jax.numpy as jnp
from jax import lax
from jax.experimental import pallas as pl
from jax.experimental.pallas import tpu as pltpu
from jax.sharding import Mesh
from jax.sharding import PartitionSpec as P

ROWS = ("z", "x", "c")
PLANE = ("x", "c")
CUBE = ("x", "c", "y")
F32 = jnp.float32
BF16 = jnp.bfloat16
NC, NB = 5, 7
NBR, CNT = 40, 47
PLANE_CNT, LOW_CNT, OWN_CNT, RANK, G_EXP, B_EXP = 96, 104, 105, 106, 107, 108
TOP = 32000.0
FINE = 65536.0


VMEM = pl.BlockSpec(memory_space=pltpu.VMEM)
SMEM = pl.BlockSpec(memory_space=pltpu.SMEM)
PARAMS = pltpu.CompilerParams(vmem_limit_bytes=12 * 1024 * 1024)


def lanes(shape):
    return lax.broadcasted_iota(jnp.int32, shape, len(shape) - 1)


def exponent(x):
    top = jnp.max(jnp.abs(x), axis=(0, 1), keepdims=True)
    return jnp.floor(-jnp.log2(jnp.maximum(top, 1e-30)))


def nearest(x):
    return jnp.floor(x + 0.5)


def to_i16(x):
    return x.astype(jnp.int32).astype(jnp.int16)


def from_i16(x):
    return x.astype(jnp.int32).astype(F32)


def table_kernel(jac_ref, nbr_ref, count_ref, out_ref):
    blank = jnp.zeros((1, 16), F32)
    rows = []
    for j in range(NC):
        rows += [jac_ref[j], blank]
    count = jnp.full((1, 16), count_ref[0].astype(F32))
    rows += [nbr_ref[...].astype(F32), count]
    table = jnp.concatenate(rows + [jnp.zeros((80, 16), F32)], axis=0)
    table = jnp.concatenate([table, jnp.zeros((128, 112), F32)], axis=1)
    out_ref[...] = table.T[0:16, :]


def make_table(jac, nbr, counts):
    return pl.pallas_call(
        table_kernel,
        in_specs=[VMEM, VMEM, SMEM],
        out_shape=jax.ShapeDtypeStruct((16, 128), F32),
        out_specs=VMEM,
        compiler_params=PARAMS,
        name="table",
    )(jac, nbr, counts)


def project_kernel(v_ref, d_ref, count_ref, out_ref):
    acc = jnp.zeros((128, 256), F32)
    for j in range(NC):
        acc = acc + lax.dot_general(
            d_ref[j], v_ref[j], (((0,), (0,)), ((), ())), preferred_element_type=F32
        )
    g = acc.T
    count = jnp.full((8, 128), count_ref[0].astype(F32))
    for p in range(8):
        for m in range(4):
            row = 64 * m + 8 * p
            out_ref[p, 8 * m : 8 * m + 8, :] = g[row : row + 8, :]
        out_ref[p, 32:40, :] = count


def project(test, deim, counts):
    return pl.pallas_call(
        project_kernel,
        in_specs=[VMEM, VMEM, SMEM],
        out_specs=VMEM,
        out_shape=jax.ShapeDtypeStruct((8, 40, 128), F32),
        compiler_params=PARAMS,
        name="project",
        cost_estimate=pl.CostEstimate(
            flops=2 * 2560 * 256 * 128, bytes_accessed=2 * 2560 * 384, transcendentals=0
        ),
    )(test, deim, counts)


def sample_kernel(low_ref, own_ref, high_ref, u_ref, out_ref):
    rank = jnp.floor(own_ref[0:1, NBR : NBR + 1] * (1.0 / 512.0))
    slot = lax.broadcasted_iota(jnp.int32, (16, 128), 0).astype(F32)
    entry = lanes((16, 128)) < NBR
    tables = []
    for ref in (low_ref, own_ref, high_ref):
        rows = ref[...]
        dead = entry & (slot >= rows[:, CNT : CNT + 1])
        tables.append(jnp.where(dead, 0.0, rows))
    table = jnp.concatenate(tables, axis=0)
    near = [table[:, NBR + n : NBR + n + 1] - rank * 512.0 for n in range(NB)]
    total = jnp.zeros((144, 256), F32)
    values = [jnp.broadcast_to(table[:, k : k + 1], (48, 128)) for k in range(NBR)]
    for chunk in range(4):
        cell = (lanes((48, 128)) + 128 * chunk).astype(F32)
        hits = [cell == near[n] for n in range(NB)]
        for j in range(NC):
            weight = jnp.where(hits[0], values[8 * j], 0.0)
            for n in range(1, NB):
                weight = weight + jnp.where(hits[n], values[8 * j + n], 0.0)
            w0 = weight.astype(BF16)
            rest = weight - w0.astype(F32)
            w1 = rest.astype(BF16)
            w2 = (rest - w1.astype(F32)).astype(BF16)
            stacked = jnp.concatenate([w0, w1, w2], axis=0)
            total = total + jnp.dot(
                stacked,
                u_ref[j, 128 * chunk : 128 * chunk + 128, :],
                preferred_element_type=F32,
            )
    rows = total[0:48, :] + (total[48:96, :] + total[96:144, :])
    exp = exponent(rows)
    rows = rows * (jnp.exp2(exp) * TOP)
    coarse = nearest(rows)
    fine = jnp.clip(nearest((rows - coarse) * FINE), -32767.0, 32767.0)
    rows = jnp.concatenate([coarse, fine, jnp.zeros((32, 256), F32)], axis=0)
    lane = lanes((1, 128))
    extra = jnp.where(lane == LOW_CNT, low_ref[0:1, CNT : CNT + 1], 0.0)
    extra = extra + jnp.where(lane == OWN_CNT, own_ref[0:1, CNT : CNT + 1], 0.0)
    extra = extra + jnp.where(lane == RANK, rank, 0.0)
    extra = extra + jnp.where(lane == B_EXP, exp, 0.0)
    cols = rows.T + extra
    for z in range(16):
        out_ref[z, :, :] = cols[16 * z : 16 * z + 16, :]


def sample(low, own, high, trial):
    return pl.pallas_call(
        sample_kernel,
        out_shape=jax.ShapeDtypeStruct((16, 16, 128), F32),
        in_specs=[VMEM] * 4,
        out_specs=VMEM,
        compiler_params=PARAMS,
        name="sample",
    )(low, own, high, trial)


def merge_kernel(g_ref, b_ref, out_ref):
    total = g_ref[0, 0:32, :]
    for p in range(1, 8):
        total = total + g_ref[p, 0:32, :]
    exp = exponent(total)
    share = jnp.abs(total * jnp.exp2(exp))
    code = nearest(jnp.sqrt(jnp.sqrt(share)) * TOP)
    code = to_i16(jnp.where(total < 0.0, -code, code))
    lane = lanes((1, 128))
    extra = jnp.where(lane == G_EXP, exp, 0.0)
    for p in range(8):
        extra = extra + jnp.where(lane == PLANE_CNT + p, g_ref[p, 32:33, :], 0.0)
    for z in range(16):
        out_ref[z, 0:32, :] = code
        out_ref[z, 32:48, :] = to_i16(b_ref[z, :, :] + extra)


def merge(g_parts, columns):
    return pl.pallas_call(
        merge_kernel,
        out_shape=jax.ShapeDtypeStruct((16, 48, 128), jnp.int16),
        in_specs=[VMEM] * 2,
        out_specs=VMEM,
        compiler_params=PARAMS,
        name="merge",
    )(g_parts, columns)


def fold_kernel(x_ref, s_ref, out_ref):
    blocks = [from_i16(x_ref[z, 32:48, :]) for z in range(16)]
    info = jnp.concatenate([block[0:1, :] for block in blocks], axis=0)
    lane = lanes((16, 128))

    def column(k):
        return jnp.sum(jnp.where(lane == k, info, 0.0), axis=1, keepdims=True)

    g_scale = jnp.exp2(-column(G_EXP))
    b_scale = jnp.exp2(-column(B_EXP)) * (1.0 / TOP)
    total = jnp.zeros((32, 128), F32)
    for z in range(16):
        root = from_i16(x_ref[z, 0:32, :]) * (1.0 / TOP)
        square = root * root
        total = total + square * square * jnp.where(root < 0.0, -1.0, 1.0) * g_scale[z : z + 1, :]
    rank = column(RANK)
    place = rank - 8.0 * jnp.floor(rank * 0.125)
    is_count = (lane >= PLANE_CNT) & (lane < PLANE_CNT + 8)
    counts = jnp.where(is_count, info, 0.0)
    before = lax.broadcasted_iota(jnp.int32, (16, 16), 1) < lax.broadcasted_iota(
        jnp.int32, (16, 16), 0
    )
    lower = jnp.dot(before.astype(F32), counts, preferred_element_type=F32)
    ahead = (lane - PLANE_CNT).astype(F32) < place
    lower = lower + jnp.where(ahead, counts, 0.0)
    offset = jnp.sum(lower, axis=1, keepdims=True)
    slot = jnp.where(lane < 48, lane, lane - 48)
    shift = jnp.where(slot < 16, -column(LOW_CNT), jnp.where(slot < 32, 0.0, column(OWN_CNT)))
    ids = offset + shift + (lane % 16).astype(F32)
    ids = jnp.where(lane < 96, ids, -1.0)
    unit = jnp.where(lane < 48, 1.0, jnp.where(lane < 96, 1.0 / FINE, 0.0))
    mode = lax.broadcasted_iota(jnp.int32, (512, 128), 0).astype(F32)
    sampled = jnp.zeros((16, 512), F32)
    for z in range(16):
        hot = jnp.where(mode == ids[z : z + 1, :], 1.0, 0.0).astype(BF16)
        cols = blocks[z] * unit
        high = cols.astype(BF16)
        rest = (cols - high.astype(F32)).astype(BF16)
        part = lax.dot_general(
            jnp.concatenate([high, rest], axis=0),
            hot,
            (((1,), (1,)), ((), ())),
            preferred_element_type=F32,
        )
        sampled = sampled + (part[0:16, :] + part[16:32, :]) * b_scale[z : z + 1, :]
    c = lax.dot_general(
        sampled,
        s_ref[...],
        (((1,), (1,)), ((), ())),
        precision=lax.Precision.HIGHEST,
        preferred_element_type=F32,
    )
    g_pairs = total.reshape(16, 2, 128)
    c_pairs = c.reshape(8, 2, 128)
    for p in range(8):
        for m in range(4):
            at = 5 * (4 * p + m)
            out_ref[at : at + 4] = g_pairs[4 * m : 4 * m + 4]
            out_ref[at + 4] = c_pairs[p]


def fold(parts, inverse):
    return pl.pallas_call(
        fold_kernel,
        out_shape=jax.ShapeDtypeStruct((160, 2, 128), F32),
        in_specs=[VMEM] * 2,
        out_specs=VMEM,
        compiler_params=PARAMS,
        name="fold",
    )(parts, inverse)


def finish_kernel(x_ref, out_ref):
    result = jnp.zeros((2, 64), F32)
    for m in range(4):
        rows = [x_ref[5 * (4 * p + m) : 5 * (4 * p + m) + 4].reshape(8, 128) for p in range(8)]
        c = x_ref[5 * m + 4]
        for p in range(1, 8):
            c = c + x_ref[5 * (4 * p + m) + 4]
        result = result + lax.dot_general(
            c,
            jnp.concatenate(rows, axis=0),
            (((1,), (1,)), ((), ())),
            precision=lax.Precision.HIGHEST,
            preferred_element_type=F32,
        )
    out_ref[...] = result


def finish(parts):
    return pl.pallas_call(
        finish_kernel,
        out_shape=jax.ShapeDtypeStruct((2, 64), F32),
        in_specs=[VMEM] * 1,
        out_specs=VMEM,
        compiler_params=PARAMS,
        name="finish",
    )(parts)


def shards(test_basis, deim_basis, trial_basis, jacobian, neighbours, counts, sample_inverse):
    own = make_table(jacobian.transpose(2, 1, 0), neighbours.T, counts)
    groups = lax.axis_size(ROWS)
    up = [(i, i + 1) for i in range(groups - 1)]
    down = [(i + 1, i) for i in range(groups - 1)]
    low = lax.ppermute(own, ROWS, up)
    high = lax.ppermute(own, ROWS, down)
    g_part = project(test_basis.swapaxes(0, 1), deim_basis.swapaxes(0, 1), counts)
    g_part, low, high = lax.optimization_barrier((g_part, low, high))
    g_plane = lax.all_to_all(g_part, PLANE, 0, 0, tiled=True)
    columns = sample(low, own, high, trial_basis.swapaxes(0, 1))
    parts = lax.all_to_all(merge(g_plane, columns), "z", 0, 0, tiled=True)
    pieces = lax.all_to_all(fold(parts, sample_inverse), CUBE, 0, 0, tiled=True)
    return finish(pieces).T


def solution(mesh):
    split = Mesh(mesh.devices.reshape(16, 4, 2, 4), ("z", "x", "c", "y"))
    placed = (
        P(ROWS, None, None),
        P(ROWS, None, "y"),
        P(ROWS, None, None),
        P(ROWS, None, None),
        P(ROWS, None),
        P(ROWS),
        P("y", None),
    )
    return jax.shard_map(
        shards, mesh=split, in_specs=placed, out_specs=P("y", ROWS), check_vma=False
    )
```

```python
import jax
import jax.numpy as jnp
from jax import lax
from jax.experimental import pallas as pl
from jax.experimental.pallas import tpu as pltpu
from jax.sharding import Mesh
from jax.sharding import PartitionSpec as P

ROWS = ("z", "x", "c")
PLANE = ("x", "c")
CUBE = ("x", "c", "y")
F32 = jnp.float32
BF16 = jnp.bfloat16
NC, NB = 5, 7
NBR, CNT = 40, 47
PLANE_CNT, LOW_CNT, OWN_CNT, RANK, G_EXP, B_EXP = 96, 104, 105, 106, 107, 108
TOP = 32000.0


VMEM = pl.BlockSpec(memory_space=pltpu.VMEM)
HBM = pl.BlockSpec(memory_space=pltpu.HBM)
SMEM = pl.BlockSpec(memory_space=pltpu.SMEM)
PARAMS = pltpu.CompilerParams(vmem_limit_bytes=12 * 1024 * 1024)


def lanes(shape):
    return lax.broadcasted_iota(jnp.int32, shape, len(shape) - 1)


def exponent(x):
    top = jnp.max(jnp.abs(x), axis=(0, 1), keepdims=True)
    return jnp.floor(-jnp.log2(jnp.maximum(top, 1e-30)))


def coded(x, exp):
    code = jnp.floor(jnp.sqrt(jnp.sqrt(jnp.abs(x * jnp.exp2(exp)))) * TOP + 0.5)
    return jnp.where(x < 0.0, -code, code)


def decoded(code):
    root = code * (1.0 / TOP)
    square = root * root
    return square * square * jnp.where(code < 0.0, -1.0, 1.0)


def to_i16(x):
    return x.astype(jnp.int32).astype(jnp.int16)


def from_i16(x):
    return x.astype(jnp.int32).astype(F32)


def prepare_kernel(
    v_hbm, d_hbm, jac_hbm, nbr_hbm, count_ref, g_ref, table_ref, v_ref, d_ref, jac_ref, nbr_ref, sems
):
    small = [
        pltpu.make_async_copy(jac_hbm, jac_ref, sems.at[2 * NC]),
        pltpu.make_async_copy(nbr_hbm, nbr_ref, sems.at[2 * NC + 1]),
    ]
    v_copies = [
        pltpu.make_async_copy(v_hbm.at[j], v_ref.at[j], sems.at[j]) for j in range(NC)
    ]
    d_copies = [
        pltpu.make_async_copy(d_hbm.at[j], d_ref.at[j], sems.at[NC + j]) for j in range(NC)
    ]
    for j in range(NC):
        v_copies[j].start()
        d_copies[j].start()
    for copy in small:
        copy.start()
    acc = jnp.zeros((128, 256), F32)
    for j in range(NC):
        v_copies[j].wait()
        d_copies[j].wait()
        acc = acc + lax.dot_general(
            d_ref[j], v_ref[j], (((0,), (0,)), ((), ())), preferred_element_type=F32
        )
    for copy in small:
        copy.wait()
    blank = jnp.zeros((1, 16), F32)
    rows = []
    for j in range(NC):
        rows += [jac_ref[j], blank]
    count = count_ref[0].astype(F32)
    rows += [nbr_ref[...].astype(F32), jnp.full((1, 16), count)]
    table = jnp.concatenate(rows + [jnp.zeros((80, 16), F32)], axis=0)
    table = jnp.concatenate([table, jnp.zeros((128, 112), F32)], axis=1)
    table_ref[...] = table.T[0:16, :]
    g = acc.T
    for p in range(8):
        for m in range(4):
            row = 64 * m + 8 * p
            g_ref[p, 8 * m : 8 * m + 8, :] = g[row : row + 8, :]
        g_ref[p, 32:40, :] = jnp.full((8, 128), count)


def prepare(test, deim, jac, nbr, counts):
    return pl.pallas_call(
        prepare_kernel,
        in_specs=[HBM, HBM, HBM, HBM, SMEM],
        out_specs=[VMEM, VMEM],
        out_shape=[
            jax.ShapeDtypeStruct((8, 40, 128), F32),
            jax.ShapeDtypeStruct((16, 128), F32),
        ],
        scratch_shapes=[
            pltpu.VMEM(test.shape, BF16),
            pltpu.VMEM(deim.shape, BF16),
            pltpu.VMEM((NC, NB, 16), F32),
            pltpu.VMEM((NB, 16), jnp.int32),
            pltpu.SemaphoreType.DMA((2 * NC + 2,)),
        ],
        name="prepare",
    )(test, deim, jac, nbr, counts)


def sample_kernel(own_ref, chip_ref, core_ref, u_ref, out_ref):
    rank = jnp.floor(own_ref[0:1, NBR : NBR + 1] * (1.0 / 512.0))
    slot = lax.broadcasted_iota(jnp.int32, (16, 128), 0).astype(F32)
    entry = lanes((16, 128)) < NBR
    first = rank == 2.0 * jnp.floor(rank * 0.5)
    chip, core = chip_ref[...], core_ref[...]
    low = jnp.where(first, chip, core)
    tables = []
    for rows in (low, own_ref[...], jnp.where(first, core, chip)):
        dead = entry & (slot >= rows[:, CNT : CNT + 1])
        tables.append(jnp.where(dead, 0.0, rows))
    table = jnp.concatenate(tables, axis=0)
    near = [table[:, NBR + n : NBR + n + 1] - rank * 512.0 for n in range(NB)]
    total = jnp.zeros((144, 256), F32)
    values = [jnp.broadcast_to(table[:, k : k + 1], (48, 128)) for k in range(NBR)]
    for chunk in range(4):
        cell = (lanes((48, 128)) + 128 * chunk).astype(F32)
        hits = [cell == near[n] for n in range(NB)]
        for j in range(NC):
            weight = jnp.where(hits[0], values[8 * j], 0.0)
            for n in range(1, NB):
                weight = weight + jnp.where(hits[n], values[8 * j + n], 0.0)
            w0 = weight.astype(BF16)
            rest = weight - w0.astype(F32)
            w1 = rest.astype(BF16)
            w2 = (rest - w1.astype(F32)).astype(BF16)
            stacked = jnp.concatenate([w0, w1, w2], axis=0)
            total = total + jnp.dot(
                stacked,
                u_ref[j, 128 * chunk : 128 * chunk + 128, :],
                preferred_element_type=F32,
            )
    rows = total[0:48, :] + (total[48:96, :] + total[96:144, :])
    exp = exponent(rows)
    rows = jnp.concatenate([coded(rows, exp), jnp.zeros((80, 256), F32)], axis=0)
    lane = lanes((1, 128))
    extra = jnp.where(lane == LOW_CNT, low[0:1, CNT : CNT + 1], 0.0)
    extra = extra + jnp.where(lane == OWN_CNT, own_ref[0:1, CNT : CNT + 1], 0.0)
    extra = extra + jnp.where(lane == RANK, rank, 0.0)
    extra = extra + jnp.where(lane == B_EXP, exp, 0.0)
    cols = rows.T
    for z in range(16):
        left = cols[16 * z : 16 * z + 8, :]
        right = pltpu.roll(cols[16 * z + 8 : 16 * z + 16, :], 48, 1)
        out_ref[z, :, :] = left + right + extra


def sample(own, chip, core, trial):
    return pl.pallas_call(
        sample_kernel,
        out_shape=jax.ShapeDtypeStruct((16, 8, 128), F32),
        in_specs=[VMEM] * 4,
        out_specs=VMEM,
        compiler_params=PARAMS,
        name="sample",
    )(own, chip, core, trial)


def merge_kernel(g_ref, b_ref, out_ref):
    total = g_ref[0, 0:32, :]
    for p in range(1, 8):
        total = total + g_ref[p, 0:32, :]
    exp = exponent(total)
    code = coded(total, exp)
    lane = lanes((1, 128))
    extra = jnp.where(lane == G_EXP, exp, 0.0)
    for p in range(8):
        extra = extra + jnp.where(lane == PLANE_CNT + p, g_ref[p, 32:33, :], 0.0)
    for z in range(16):
        out_ref[z] = to_i16(jnp.concatenate([code, b_ref[z] + extra], axis=0))


def merge(g_parts, columns):
    return pl.pallas_call(
        merge_kernel,
        out_shape=jax.ShapeDtypeStruct((16, 40, 128), jnp.int16),
        in_specs=[VMEM] * 2,
        out_specs=VMEM,
        compiler_params=PARAMS,
        name="merge",
    )(g_parts, columns)


def fold_kernel(x_ref, s_ref, out_ref):
    blocks = [from_i16(x_ref[z]) for z in range(16)]
    info = jnp.concatenate([block[32:33, :] for block in blocks], axis=0)
    lane = lanes((16, 128))

    def column(k):
        return jnp.sum(jnp.where(lane == k, info, 0.0), axis=1, keepdims=True)

    g_scale = jnp.exp2(-column(G_EXP))
    b_scale = jnp.exp2(-column(B_EXP))
    total = jnp.zeros((32, 128), F32)
    for z in range(16):
        total = total + decoded(blocks[z][0:32, :]) * g_scale[z : z + 1, :]
    rank = column(RANK)
    place = rank - 8.0 * jnp.floor(rank * 0.125)
    is_count = (lane >= PLANE_CNT) & (lane < PLANE_CNT + 8)
    counts = jnp.where(is_count, info, 0.0)
    before = lax.broadcasted_iota(jnp.int32, (16, 16), 1) < lax.broadcasted_iota(
        jnp.int32, (16, 16), 0
    )
    lower = jnp.dot(before.astype(F32), counts, preferred_element_type=F32)
    ahead = (lane - PLANE_CNT).astype(F32) < place
    lower = lower + jnp.where(ahead, counts, 0.0)
    offset = jnp.sum(lower, axis=1, keepdims=True)
    shift = jnp.where(lane < 16, -column(LOW_CNT), jnp.where(lane < 32, 0.0, column(OWN_CNT)))
    ids = jnp.where(lane < 48, offset + shift + (lane % 16).astype(F32), -1.0)
    slots = lane < 48
    mode = lax.broadcasted_iota(jnp.int32, (512, 128), 0).astype(F32)
    sampled = jnp.zeros((16, 512), F32)
    for z in range(16):
        hot = jnp.where(mode == ids[z : z + 1, :], 1.0, 0.0).astype(BF16)
        both = decoded(blocks[z][32:40, :])
        both = jnp.concatenate([both, pltpu.roll(both, 80, 1)], axis=0)
        cols = jnp.where(slots, both, 0.0)
        high = cols.astype(BF16)
        rest = (cols - high.astype(F32)).astype(BF16)
        part = lax.dot_general(
            jnp.concatenate([high, rest], axis=0),
            hot,
            (((1,), (1,)), ((), ())),
            preferred_element_type=F32,
        )
        sampled = sampled + (part[0:16, :] + part[16:32, :]) * b_scale[z : z + 1, :]
    c = lax.dot_general(
        sampled,
        s_ref[...],
        (((1,), (1,)), ((), ())),
        precision=lax.Precision.HIGHEST,
        preferred_element_type=F32,
    )
    g_pairs = total.reshape(16, 2, 128)
    c_pairs = c.reshape(8, 2, 128)
    for p in range(8):
        for m in range(4):
            at = 5 * (4 * p + m)
            out_ref[at : at + 4] = g_pairs[4 * m : 4 * m + 4]
            out_ref[at + 4] = c_pairs[p]


def fold(parts, inverse):
    return pl.pallas_call(
        fold_kernel,
        out_shape=jax.ShapeDtypeStruct((160, 2, 128), F32),
        in_specs=[VMEM] * 2,
        out_specs=VMEM,
        compiler_params=PARAMS,
        name="fold",
    )(parts, inverse)


def finish_kernel(x_ref, out_ref):
    result = jnp.zeros((2, 64), F32)
    for m in range(4):
        rows = [x_ref[5 * (4 * p + m) : 5 * (4 * p + m) + 4].reshape(8, 128) for p in range(8)]
        c = x_ref[5 * m + 4]
        for p in range(1, 8):
            c = c + x_ref[5 * (4 * p + m) + 4]
        result = result + lax.dot_general(
            c,
            jnp.concatenate(rows, axis=0),
            (((1,), (1,)), ((), ())),
            precision=lax.Precision.HIGHEST,
            preferred_element_type=F32,
        )
    out_ref[...] = result


def finish(parts):
    return pl.pallas_call(
        finish_kernel,
        out_shape=jax.ShapeDtypeStruct((2, 64), F32),
        in_specs=[VMEM] * 1,
        out_specs=VMEM,
        compiler_params=PARAMS,
        name="finish",
    )(parts)


def shards(test_basis, deim_basis, trial_basis, jacobian, neighbours, counts, sample_inverse):
    g_part, own = prepare(
        test_basis.swapaxes(0, 1),
        deim_basis.swapaxes(0, 1),
        jacobian.transpose(2, 1, 0),
        neighbours.T,
        counts,
    )
    groups = lax.axis_size(ROWS)
    across = [(i, i + 1) for i in range(1, groups - 1, 2)]
    across += [(target, source) for source, target in across]
    inside = [(i, i ^ 1) for i in range(groups)]
    chip = lax.ppermute(own, ROWS, across)
    core = lax.ppermute(own, ROWS, inside)
    g_plane = lax.all_to_all(g_part, PLANE, 0, 0, tiled=True)
    columns = sample(own, chip, core, trial_basis.swapaxes(0, 1))
    parts = lax.all_to_all(merge(g_plane, columns), "z", 0, 0, tiled=True)
    pieces = lax.all_to_all(fold(parts, sample_inverse), CUBE, 0, 0, tiled=True)
    return finish(pieces).T


def solution(mesh):
    split = Mesh(mesh.devices.reshape(16, 4, 2, 4), ("z", "x", "c", "y"))
    placed = (
        P(ROWS, None, None),
        P(ROWS, None, "y"),
        P(ROWS, None, None),
        P(ROWS, None, None),
        P(ROWS, None),
        P(ROWS),
        P("y", None),
    )
    return jax.shard_map(
        shards, mesh=split, in_specs=placed, out_specs=P("y", ROWS), check_vma=False
    )
```

```python
import jax
import jax.numpy as jnp
from jax import lax
from jax.experimental import pallas as pl
from jax.experimental.pallas import tpu as pltpu
from jax.sharding import Mesh
from jax.sharding import PartitionSpec as P

ROWS = ("zh", "zl", "x", "c")
GROUP = ("zl", "x", "c")
CUBE = ("zl", "x", "c", "y")
F32 = jnp.float32
BF16 = jnp.bfloat16
NC, NB = 5, 7
NBR, CNT = 40, 47
GROUP_CNT, LOW_CNT, OWN_CNT, RANK, G_EXP, B_EXP = 96, 112, 113, 114, 115, 116
TOP = 32000.0


VMEM = pl.BlockSpec(memory_space=pltpu.VMEM)
HBM = pl.BlockSpec(memory_space=pltpu.HBM)
PARAMS = pltpu.CompilerParams(vmem_limit_bytes=12 * 1024 * 1024)


def lanes(shape):
    return lax.broadcasted_iota(jnp.int32, shape, len(shape) - 1)


def exponent(x):
    top = jnp.max(jnp.abs(x), axis=(0, 1), keepdims=True)
    return jnp.floor(-jnp.log2(jnp.maximum(top, 1e-30)))


def coded(x, exp):
    code = jnp.floor(jnp.sqrt(jnp.sqrt(jnp.abs(x * jnp.exp2(exp)))) * TOP + 0.5)
    return jnp.where(x < 0.0, -code, code)


def decoded(code):
    root = code * (1.0 / TOP)
    square = root * root
    return square * square * jnp.where(code < 0.0, -1.0, 1.0)


def to_i16(x):
    return x.astype(jnp.int32).astype(jnp.int16)


def from_i16(x):
    return x.astype(jnp.int32).astype(F32)


def table_of(jac_ref, nbr_ref, count):
    blank = jnp.zeros((1, 16), F32)
    rows = []
    for j in range(NC):
        rows += [jac_ref[j], blank]
    rows += [nbr_ref[...].astype(F32), jnp.broadcast_to(count, (1, 16))]
    table = jnp.concatenate(rows + [jnp.zeros((80, 16), F32)], axis=0)
    table = jnp.concatenate([table, jnp.zeros((128, 112), F32)], axis=1)
    return table.T[0:16, :]


def prepare_kernel(
    v_hbm,
    d_hbm,
    jac_hbm,
    nbr_hbm,
    count_hbm,
    g_ref,
    table_ref,
    v_ref,
    d_ref,
    jac_ref,
    nbr_ref,
    count_ref,
    sems,
):
    small = [
        pltpu.make_async_copy(jac_hbm, jac_ref, sems.at[2 * NC]),
        pltpu.make_async_copy(nbr_hbm, nbr_ref, sems.at[2 * NC + 1]),
        pltpu.make_async_copy(count_hbm, count_ref, sems.at[2 * NC + 2]),
    ]
    v_copies = [
        pltpu.make_async_copy(v_hbm.at[j], v_ref.at[j], sems.at[j]) for j in range(NC)
    ]
    d_copies = [
        pltpu.make_async_copy(d_hbm.at[j], d_ref.at[j], sems.at[NC + j]) for j in range(NC)
    ]
    for copy in small:
        copy.start()
    for j in range(NC):
        v_copies[j].start()
        d_copies[j].start()
    for copy in small:
        copy.wait()
    count = count_ref[0, 0].astype(F32)
    table_ref[...] = table_of(jac_ref, nbr_ref, count)
    acc = jnp.zeros((128, 256), F32)
    for j in range(NC):
        v_copies[j].wait()
        d_copies[j].wait()
        acc = acc + lax.dot_general(
            d_ref[j], v_ref[j], (((0,), (0,)), ((), ())), preferred_element_type=F32
        )
    pairs = acc.T.reshape(128, 2, 128)
    for p in range(16):
        for m in range(4):
            at = 32 * m + 2 * p
            g_ref[9 * p + 2 * m : 9 * p + 2 * m + 2] = pairs[at : at + 2]
        g_ref[9 * p + 8] = jnp.full((2, 128), count)


def prepare(test, deim, jac, nbr, counts):
    return pl.pallas_call(
        prepare_kernel,
        in_specs=[HBM, HBM, HBM, HBM, HBM],
        out_specs=[VMEM, VMEM],
        out_shape=[
            jax.ShapeDtypeStruct((144, 2, 128), F32),
            jax.ShapeDtypeStruct((16, 128), F32),
        ],
        scratch_shapes=[
            pltpu.VMEM(test.shape, BF16),
            pltpu.VMEM(deim.shape, BF16),
            pltpu.VMEM((NC, NB, 16), F32),
            pltpu.VMEM((NB, 16), jnp.int32),
            pltpu.SMEM((1, 1), jnp.int32),
            pltpu.SemaphoreType.DMA((2 * NC + 3,)),
        ],
        name="prepare",
    )(test, deim, jac, nbr, counts)


def sample_kernel(jac_ref, nbr_ref, count_ref, chip_ref, core_ref, u_ref, out_ref):
    own = table_of(jac_ref, nbr_ref, count_ref[...].astype(F32))
    rank = jnp.floor(own[0:1, NBR : NBR + 1] * (1.0 / 512.0))
    slot = lax.broadcasted_iota(jnp.int32, (16, 128), 0).astype(F32)
    entry = lanes((16, 128)) < NBR
    first = rank == 2.0 * jnp.floor(rank * 0.5)
    chip, core = chip_ref[...], core_ref[...]
    low = jnp.where(first, chip, core)
    tables = []
    for rows in (low, own, jnp.where(first, core, chip)):
        dead = entry & (slot >= rows[:, CNT : CNT + 1])
        tables.append(jnp.where(dead, 0.0, rows))
    table = jnp.concatenate(tables, axis=0)
    near = [table[:, NBR + n : NBR + n + 1] - rank * 512.0 for n in range(NB)]
    total = jnp.zeros((96, 256), F32)
    values = [jnp.broadcast_to(table[:, k : k + 1], (48, 128)) for k in range(NBR)]
    for chunk in range(4):
        cell = (lanes((48, 128)) + 128 * chunk).astype(F32)
        hits = [cell == near[n] for n in range(NB)]
        for j in range(NC):
            weight = jnp.where(hits[0], values[8 * j], 0.0)
            for n in range(1, NB):
                weight = weight + jnp.where(hits[n], values[8 * j + n], 0.0)
            high = weight.astype(BF16)
            rest = (weight - high.astype(F32)).astype(BF16)
            total = total + jnp.dot(
                jnp.concatenate([high, rest], axis=0),
                u_ref[j, 128 * chunk : 128 * chunk + 128, :],
                preferred_element_type=F32,
            )
    rows = total[0:48, :] + total[48:96, :]
    exp = exponent(rows)
    rows = jnp.concatenate([coded(rows, exp), jnp.zeros((80, 256), F32)], axis=0)
    lane = lanes((1, 128))
    extra = jnp.where(lane == LOW_CNT, low[0:1, CNT : CNT + 1], 0.0)
    extra = extra + jnp.where(lane == OWN_CNT, own[0:1, CNT : CNT + 1], 0.0)
    extra = extra + jnp.where(lane == RANK, rank, 0.0)
    extra = extra + jnp.where(lane == B_EXP, exp, 0.0)
    cols = rows.T
    for z in range(8):
        left = cols[32 * z : 32 * z + 16, :]
        right = pltpu.roll(cols[32 * z + 16 : 32 * z + 32, :], 48, 1)
        out_ref[z, :, :] = left + right + extra


def sample(jac, nbr, counts, chip, core, trial):
    return pl.pallas_call(
        sample_kernel,
        out_shape=jax.ShapeDtypeStruct((8, 16, 128), F32),
        in_specs=[VMEM] * 6,
        out_specs=VMEM,
        compiler_params=PARAMS,
        name="sample",
    )(jac, nbr, counts, chip, core, trial)


def merge_kernel(g_ref, b_ref, out_ref):
    total = g_ref[0:8]
    for p in range(1, 16):
        total = total + g_ref[9 * p : 9 * p + 8]
    total = total.reshape(16, 128)
    exp = exponent(total)
    code = coded(total, exp)
    lane = lanes((1, 128))
    extra = jnp.where(lane == G_EXP, exp, 0.0)
    for p in range(16):
        extra = extra + jnp.where(lane == GROUP_CNT + p, g_ref[9 * p + 8][0:1, :], 0.0)
    for z in range(8):
        out_ref[z] = to_i16(jnp.concatenate([code, b_ref[z] + extra], axis=0))


def merge(g_parts, columns):
    return pl.pallas_call(
        merge_kernel,
        out_shape=jax.ShapeDtypeStruct((8, 32, 128), jnp.int16),
        in_specs=[VMEM] * 2,
        out_specs=VMEM,
        compiler_params=PARAMS,
        name="merge",
    )(g_parts, columns)


def fold_kernel(x_ref, s_ref, out_ref):
    blocks = [from_i16(x_ref[z]) for z in range(8)]
    info = jnp.concatenate([block[16:17, :] for block in blocks], axis=0)
    lane = lanes((8, 128))

    def column(k):
        return jnp.sum(jnp.where(lane == k, info, 0.0), axis=1, keepdims=True)

    g_scale = jnp.exp2(-column(G_EXP))
    b_scale = jnp.exp2(-column(B_EXP))
    total = jnp.zeros((16, 128), F32)
    for z in range(8):
        total = total + decoded(blocks[z][0:16, :]) * g_scale[z : z + 1, :]
    rank = column(RANK)
    place = rank - 16.0 * jnp.floor(rank * 0.0625)
    is_count = (lane >= GROUP_CNT) & (lane < GROUP_CNT + 16)
    counts = jnp.where(is_count, info, 0.0)
    before = lax.broadcasted_iota(jnp.int32, (8, 8), 1) < lax.broadcasted_iota(
        jnp.int32, (8, 8), 0
    )
    lower = jnp.dot(before.astype(F32), counts, preferred_element_type=F32)
    ahead = (lane - GROUP_CNT).astype(F32) < place
    lower = lower + jnp.where(ahead, counts, 0.0)
    offset = jnp.sum(lower, axis=1, keepdims=True)
    shift = jnp.where(lane < 16, -column(LOW_CNT), jnp.where(lane < 32, 0.0, column(OWN_CNT)))
    ids = jnp.where(lane < 48, offset + shift + (lane % 16).astype(F32), -1.0)
    slots = lanes((1, 128)) < 48
    mode = lax.broadcasted_iota(jnp.int32, (512, 128), 0).astype(F32)
    sampled = jnp.zeros((32, 512), F32)
    for z in range(8):
        hot = jnp.where(mode == ids[z : z + 1, :], 1.0, 0.0).astype(BF16)
        both = decoded(blocks[z][16:32, :])
        both = jnp.concatenate([both, pltpu.roll(both, 80, 1)], axis=0)
        cols = jnp.where(slots, both, 0.0)
        high = cols.astype(BF16)
        rest = (cols - high.astype(F32)).astype(BF16)
        part = lax.dot_general(
            jnp.concatenate([high, rest], axis=0),
            hot,
            (((1,), (1,)), ((), ())),
            preferred_element_type=F32,
        )
        sampled = sampled + (part[0:32, :] + part[32:64, :]) * b_scale[z : z + 1, :]
    c = lax.dot_general(
        sampled,
        s_ref[...],
        (((1,), (1,)), ((), ())),
        precision=lax.Precision.HIGHEST,
        preferred_element_type=F32,
    )
    g_pairs = total.reshape(8, 2, 128)
    c_pairs = c.reshape(16, 2, 128)
    for p in range(16):
        for m in range(4):
            at = 3 * (4 * p + m)
            out_ref[at : at + 2] = g_pairs[2 * m : 2 * m + 2]
            out_ref[at + 2] = c_pairs[p]


def fold(parts, inverse):
    return pl.pallas_call(
        fold_kernel,
        out_shape=jax.ShapeDtypeStruct((192, 2, 128), F32),
        in_specs=[VMEM] * 2,
        out_specs=VMEM,
        compiler_params=PARAMS,
        name="fold",
    )(parts, inverse)


def finish_kernel(x_ref, out_ref):
    result = jnp.zeros((2, 64), F32)
    for m in range(4):
        rows = [x_ref[3 * (4 * p + m) : 3 * (4 * p + m) + 2] for p in range(16)]
        c = x_ref[3 * m + 2]
        for p in range(1, 16):
            c = c + x_ref[3 * (4 * p + m) + 2]
        result = result + lax.dot_general(
            c,
            jnp.concatenate(rows, axis=0).reshape(64, 128),
            (((1,), (1,)), ((), ())),
            precision=lax.Precision.HIGHEST,
            preferred_element_type=F32,
        )
    out_ref[...] = result


def finish(parts):
    return pl.pallas_call(
        finish_kernel,
        out_shape=jax.ShapeDtypeStruct((2, 64), F32),
        in_specs=[VMEM] * 1,
        out_specs=VMEM,
        compiler_params=PARAMS,
        name="finish",
    )(parts)


def shards(test_basis, deim_basis, trial_basis, jacobian, neighbours, counts, sample_inverse):
    jac, nbr, count = jacobian.transpose(2, 1, 0), neighbours.T, counts.reshape(1, 1)
    g_part, own = prepare(test_basis.swapaxes(0, 1), deim_basis.swapaxes(0, 1), jac, nbr, count)
    groups = lax.axis_size(ROWS)
    across = [(i, i + 1) for i in range(1, groups - 1, 2)]
    across += [(target, source) for source, target in across]
    inside = [(i, i ^ 1) for i in range(groups)]
    core = lax.ppermute(own, ROWS, inside)
    chip = lax.ppermute(own, ROWS, across)
    g_group = lax.all_to_all(g_part, GROUP, 0, 0, tiled=True)
    columns = sample(jac, nbr, count, chip, core, trial_basis.swapaxes(0, 1))
    parts = lax.all_to_all(merge(g_group, columns), "zh", 0, 0, tiled=True)
    pieces = lax.all_to_all(fold(parts, sample_inverse), CUBE, 0, 0, tiled=True)
    return finish(pieces).T


def solution(mesh):
    split = Mesh(mesh.devices.reshape(8, 2, 4, 2, 4), ("zh", "zl", "x", "c", "y"))
    placed = (
        P(ROWS, None, None),
        P(ROWS, None, "y"),
        P(ROWS, None, None),
        P(ROWS, None, None),
        P(ROWS, None),
        P(ROWS),
        P("y", None),
    )
    return jax.shard_map(
        shards, mesh=split, in_specs=placed, out_specs=P("y", ROWS), check_vma=False
    )
```

```python
import jax
import jax.numpy as jnp
from jax import lax
from jax.experimental import pallas as pl
from jax.experimental.pallas import tpu as pltpu
from jax.sharding import Mesh
from jax.sharding import PartitionSpec as P

ROWS = ("zh", "zl", "x", "c")
GROUP = ("zl", "x", "c")
CUBE = ("zl", "x", "c", "y")
F32 = jnp.float32
BF16 = jnp.bfloat16
NC, NB = 5, 7
NBR, CNT = 40, 47
GROUP_CNT, LOW_CNT, OWN_CNT, RANK, G_EXP, B_EXP = 96, 112, 113, 114, 115, 116
TOP = 32000.0


VMEM = pl.BlockSpec(memory_space=pltpu.VMEM)
HBM = pl.BlockSpec(memory_space=pltpu.HBM)
PARAMS = pltpu.CompilerParams(vmem_limit_bytes=12 * 1024 * 1024)


def lanes(shape):
    return lax.broadcasted_iota(jnp.int32, shape, len(shape) - 1)


def exponent(x):
    top = jnp.max(jnp.abs(x), axis=(0, 1), keepdims=True)
    return jnp.floor(-jnp.log2(jnp.maximum(top, 1e-30)))


def coded(x, exp):
    code = jnp.floor(jnp.sqrt(jnp.sqrt(jnp.abs(x * jnp.exp2(exp)))) * TOP + 0.5)
    return jnp.where(x < 0.0, -code, code)


def decoded(code):
    root = code * (1.0 / TOP)
    square = root * root
    return square * square * jnp.where(code < 0.0, -1.0, 1.0)


def to_i16(x):
    return x.astype(jnp.int32).astype(jnp.int16)


def from_i16(x):
    return x.astype(jnp.int32).astype(F32)


def table_of(jac_ref, nbr_ref, count):
    blank = jnp.zeros((1, 16), F32)
    rows = []
    for j in range(NC):
        rows += [jac_ref[j], blank]
    rows += [nbr_ref[...].astype(F32), jnp.broadcast_to(count, (1, 16))]
    table = jnp.concatenate(rows + [jnp.zeros((80, 16), F32)], axis=0)
    table = jnp.concatenate([table, jnp.zeros((128, 112), F32)], axis=1)
    return table.T[0:16, :]


def prepare_kernel(
    v_hbm,
    d_hbm,
    jac_hbm,
    nbr_hbm,
    count_hbm,
    g_ref,
    table_ref,
    v_ref,
    d_ref,
    jac_ref,
    nbr_ref,
    count_ref,
    sems,
):
    small = [
        pltpu.make_async_copy(jac_hbm, jac_ref, sems.at[2 * NC]),
        pltpu.make_async_copy(nbr_hbm, nbr_ref, sems.at[2 * NC + 1]),
        pltpu.make_async_copy(count_hbm, count_ref, sems.at[2 * NC + 2]),
    ]
    v_copies = [
        pltpu.make_async_copy(v_hbm.at[j], v_ref.at[j], sems.at[j]) for j in range(NC)
    ]
    d_copies = [
        pltpu.make_async_copy(d_hbm.at[j], d_ref.at[j], sems.at[NC + j]) for j in range(NC)
    ]
    for copy in small:
        copy.start()
    for j in range(NC):
        v_copies[j].start()
        d_copies[j].start()
    for copy in small:
        copy.wait()
    count = count_ref[0, 0].astype(F32)
    table_ref[...] = table_of(jac_ref, nbr_ref, count)
    acc = jnp.zeros((128, 256), F32)
    for j in range(NC):
        v_copies[j].wait()
        d_copies[j].wait()
        acc = acc + lax.dot_general(
            d_ref[j], v_ref[j], (((0,), (0,)), ((), ())), preferred_element_type=F32
        )
    pairs = acc.T.reshape(128, 2, 128)
    for p in range(16):
        for m in range(4):
            at = 32 * m + 2 * p
            g_ref[9 * p + 2 * m : 9 * p + 2 * m + 2] = pairs[at : at + 2]
        g_ref[9 * p + 8] = jnp.full((2, 128), count)


def prepare(test, deim, jac, nbr, counts):
    return pl.pallas_call(
        prepare_kernel,
        in_specs=[HBM, HBM, HBM, HBM, HBM],
        out_specs=[VMEM, VMEM],
        out_shape=[
            jax.ShapeDtypeStruct((144, 2, 128), F32),
            jax.ShapeDtypeStruct((16, 128), F32),
        ],
        scratch_shapes=[
            pltpu.VMEM(test.shape, BF16),
            pltpu.VMEM(deim.shape, BF16),
            pltpu.VMEM((NC, NB, 16), F32),
            pltpu.VMEM((NB, 16), jnp.int32),
            pltpu.SMEM((1, 1), jnp.int32),
            pltpu.SemaphoreType.DMA((2 * NC + 3,)),
        ],
        name="prepare",
    )(test, deim, jac, nbr, counts)


def sample_kernel(jac_ref, nbr_ref, count_ref, core_ref, chip_ref, u_ref, out_ref):
    own = table_of(jac_ref, nbr_ref, count_ref[...].astype(F32))
    rank = jnp.floor(own[0:1, NBR : NBR + 1] * (1.0 / 512.0))
    slot = lax.broadcasted_iota(jnp.int32, (16, 128), 0).astype(F32)
    entry = lanes((16, 128)) < NBR
    first = rank == 2.0 * jnp.floor(rank * 0.5)
    chip, core = chip_ref[...], core_ref[...]
    low = jnp.where(first, chip, core)
    tables = []
    for rows in (low, own, jnp.where(first, core, chip)):
        dead = entry & (slot >= rows[:, CNT : CNT + 1])
        tables.append(jnp.where(dead, 0.0, rows))
    table = jnp.concatenate(tables, axis=0)
    near = [table[:, NBR + n : NBR + n + 1] - rank * 512.0 for n in range(NB)]
    total = jnp.zeros((96, 256), F32)
    values = [jnp.broadcast_to(table[:, k : k + 1], (48, 128)) for k in range(NBR)]
    cell = lanes((48, 128)).astype(F32)
    hits = [[cell + 128.0 * part == near[n] for n in range(NB)] for part in range(4)]
    for j in range(NC):
        weights = []
        for part in range(4):
            weight = jnp.where(hits[part][0], values[8 * j], 0.0)
            for n in range(1, NB):
                weight = weight + jnp.where(hits[part][n], values[8 * j + n], 0.0)
            weights.append(weight)
        weight = jnp.concatenate(weights, axis=1)
        high = weight.astype(BF16)
        rest = (weight - high.astype(F32)).astype(BF16)
        total = total + jnp.dot(
            jnp.concatenate([high, rest], axis=0), u_ref[j], preferred_element_type=F32
        )
    rows = total[0:48, :] + total[48:96, :]
    exp = exponent(rows)
    rows = jnp.concatenate([coded(rows, exp), jnp.zeros((80, 256), F32)], axis=0)
    lane = lanes((1, 128))
    extra = jnp.where(lane == LOW_CNT, low[0:1, CNT : CNT + 1], 0.0)
    extra = extra + jnp.where(lane == OWN_CNT, own[0:1, CNT : CNT + 1], 0.0)
    extra = extra + jnp.where(lane == RANK, rank, 0.0)
    extra = extra + jnp.where(lane == B_EXP, exp, 0.0)
    cols = rows.T
    for z in range(8):
        left = cols[32 * z : 32 * z + 16, :]
        right = pltpu.roll(cols[32 * z + 16 : 32 * z + 32, :], 48, 1)
        out_ref[z, :, :] = left + right + extra


def sample(jac, nbr, counts, core, chip, trial):
    return pl.pallas_call(
        sample_kernel,
        out_shape=jax.ShapeDtypeStruct((8, 16, 128), F32),
        in_specs=[VMEM] * 6,
        out_specs=VMEM,
        compiler_params=PARAMS,
        name="sample",
    )(jac, nbr, counts, core, chip, trial)


def merge_kernel(g_ref, b_ref, out_ref):
    total = g_ref[0:8]
    for p in range(1, 16):
        total = total + g_ref[9 * p : 9 * p + 8]
    total = total.reshape(16, 128)
    exp = exponent(total)
    code = coded(total, exp)
    lane = lanes((1, 128))
    extra = jnp.where(lane == G_EXP, exp, 0.0)
    for p in range(16):
        extra = extra + jnp.where(lane == GROUP_CNT + p, g_ref[9 * p + 8][0:1, :], 0.0)
    for z in range(8):
        out_ref[z] = to_i16(jnp.concatenate([code, b_ref[z] + extra], axis=0))


def merge(g_parts, columns):
    return pl.pallas_call(
        merge_kernel,
        out_shape=jax.ShapeDtypeStruct((8, 32, 128), jnp.int16),
        in_specs=[VMEM] * 2,
        out_specs=VMEM,
        compiler_params=PARAMS,
        name="merge",
    )(g_parts, columns)


def fold_kernel(x_ref, s_ref, out_ref):
    blocks = [from_i16(x_ref[z]) for z in range(8)]
    info = jnp.concatenate([block[16:17, :] for block in blocks], axis=0)
    lane = lanes((8, 128))

    def column(k):
        return jnp.sum(jnp.where(lane == k, info, 0.0), axis=1, keepdims=True)

    g_scale = jnp.exp2(-column(G_EXP))
    b_scale = jnp.exp2(-column(B_EXP))
    total = jnp.zeros((16, 128), F32)
    for z in range(8):
        total = total + decoded(blocks[z][0:16, :]) * g_scale[z : z + 1, :]
    rank = column(RANK)
    place = rank - 16.0 * jnp.floor(rank * 0.0625)
    is_count = (lane >= GROUP_CNT) & (lane < GROUP_CNT + 16)
    counts = jnp.where(is_count, info, 0.0)
    before = lax.broadcasted_iota(jnp.int32, (8, 8), 1) < lax.broadcasted_iota(
        jnp.int32, (8, 8), 0
    )
    lower = jnp.dot(before.astype(F32), counts, preferred_element_type=F32)
    ahead = (lane - GROUP_CNT).astype(F32) < place
    lower = lower + jnp.where(ahead, counts, 0.0)
    offset = jnp.sum(lower, axis=1, keepdims=True)
    shift = jnp.where(lane < 16, -column(LOW_CNT), jnp.where(lane < 32, 0.0, column(OWN_CNT)))
    ids = jnp.where(lane < 48, offset + shift + (lane % 16).astype(F32), -1.0)
    slots = lanes((1, 128)) < 48
    mode = lax.broadcasted_iota(jnp.int32, (512, 128), 0).astype(F32)
    sampled = jnp.zeros((32, 512), F32)
    for z in range(8):
        hot = jnp.where(mode == ids[z : z + 1, :], 1.0, 0.0).astype(BF16)
        both = decoded(blocks[z][16:32, :])
        both = jnp.concatenate([both, pltpu.roll(both, 80, 1)], axis=0)
        cols = jnp.where(slots, both, 0.0)
        high = cols.astype(BF16)
        rest = (cols - high.astype(F32)).astype(BF16)
        part = lax.dot_general(
            jnp.concatenate([high, rest], axis=0),
            hot,
            (((1,), (1,)), ((), ())),
            preferred_element_type=F32,
        )
        sampled = sampled + (part[0:32, :] + part[32:64, :]) * b_scale[z : z + 1, :]
    c = lax.dot_general(
        sampled,
        s_ref[...],
        (((1,), (1,)), ((), ())),
        precision=lax.Precision.HIGHEST,
        preferred_element_type=F32,
    )
    g_pairs = total.reshape(8, 2, 128)
    c_pairs = c.reshape(16, 2, 128)
    for p in range(16):
        for m in range(4):
            at = 3 * (4 * p + m)
            out_ref[at : at + 2] = g_pairs[2 * m : 2 * m + 2]
            out_ref[at + 2] = c_pairs[p]


def fold(parts, inverse):
    return pl.pallas_call(
        fold_kernel,
        out_shape=jax.ShapeDtypeStruct((192, 2, 128), F32),
        in_specs=[VMEM] * 2,
        out_specs=VMEM,
        compiler_params=PARAMS,
        name="fold",
    )(parts, inverse)


def finish_kernel(x_ref, out_ref):
    result = jnp.zeros((2, 64), F32)
    for m in range(4):
        rows = [x_ref[3 * (4 * p + m) : 3 * (4 * p + m) + 2] for p in range(16)]
        c = x_ref[3 * m + 2]
        for p in range(1, 16):
            c = c + x_ref[3 * (4 * p + m) + 2]
        result = result + lax.dot_general(
            c,
            jnp.concatenate(rows, axis=0).reshape(64, 128),
            (((1,), (1,)), ((), ())),
            precision=lax.Precision.HIGHEST,
            preferred_element_type=F32,
        )
    out_ref[...] = result


def finish(parts):
    return pl.pallas_call(
        finish_kernel,
        out_shape=jax.ShapeDtypeStruct((2, 64), F32),
        in_specs=[VMEM] * 1,
        out_specs=VMEM,
        compiler_params=PARAMS,
        name="finish",
    )(parts)


def shards(test_basis, deim_basis, trial_basis, jacobian, neighbours, counts, sample_inverse):
    jac, nbr, count = jacobian.transpose(2, 1, 0), neighbours.T, counts.reshape(1, 1)
    g_part, own = prepare(test_basis.swapaxes(0, 1), deim_basis.swapaxes(0, 1), jac, nbr, count)
    groups = lax.axis_size(ROWS)
    across = [(i, i + 1) for i in range(1, groups - 1, 2)]
    across += [(target, source) for source, target in across]
    inside = [(i, i ^ 1) for i in range(groups)]
    core = lax.ppermute(own, ROWS, inside)
    chip = lax.ppermute(own, ROWS, across)
    g_group = lax.all_to_all(g_part, GROUP, 0, 0, tiled=True)
    columns = sample(jac, nbr, count, core, chip, trial_basis.swapaxes(0, 1))
    parts = lax.all_to_all(merge(g_group, columns), "zh", 0, 0, tiled=True)
    pieces = lax.all_to_all(fold(parts, sample_inverse), CUBE, 0, 0, tiled=True)
    return finish(pieces).T


def solution(mesh):
    split = Mesh(mesh.devices.reshape(8, 2, 4, 2, 4), ("zh", "zl", "x", "c", "y"))
    placed = (
        P(ROWS, None, None),
        P(ROWS, None, "y"),
        P(ROWS, None, None),
        P(ROWS, None, None),
        P(ROWS, None),
        P(ROWS),
        P("y", None),
    )
    return jax.shard_map(
        shards, mesh=split, in_specs=placed, out_specs=P("y", ROWS), check_vma=False
    )
```

```python
import jax
import jax.numpy as jnp
from jax import lax
from jax.experimental import pallas as pl
from jax.experimental.pallas import tpu as pltpu
from jax.sharding import Mesh
from jax.sharding import PartitionSpec as P

ROWS = ("zh", "zl", "x", "c")
GROUP = ("zl", "x", "c")
CUBE = ("zl", "x", "c", "y")
F32 = jnp.float32
BF16 = jnp.bfloat16
NC, NB = 5, 7
NBR, CNT = 40, 47
LOW_CNT, OWN_CNT, RANK, G_EXP, B_EXP, GROUP_CNT = 96, 97, 98, 99, 100, 112
TOP = 32000.0


VMEM = pl.BlockSpec(memory_space=pltpu.VMEM)
HBM = pl.BlockSpec(memory_space=pltpu.HBM)
PARAMS = pltpu.CompilerParams(vmem_limit_bytes=12 * 1024 * 1024)


def lanes(shape):
    return lax.broadcasted_iota(jnp.int32, shape, len(shape) - 1)


def exponent(x):
    top = jnp.max(jnp.abs(x), axis=(0, 1), keepdims=True)
    return jnp.floor(-jnp.log2(jnp.maximum(top, 1e-30)))


def coded(x, exp):
    code = jnp.floor(jnp.sqrt(jnp.sqrt(jnp.abs(x * jnp.exp2(exp)))) * TOP + 0.5)
    return jnp.where(x < 0.0, -code, code)


def decoded(code):
    root = code * (1.0 / TOP)
    square = root * root
    return square * square * jnp.where(code < 0.0, -1.0, 1.0)


def to_i16(x):
    return x.astype(jnp.int32).astype(jnp.int16)


def from_i16(x):
    return x.astype(jnp.int32).astype(F32)


def table_of(jac_ref, nbr_ref, count):
    blank = jnp.zeros((1, 16), F32)
    rows = []
    for j in range(NC):
        rows += [jac_ref[j], blank]
    rows += [nbr_ref[...].astype(F32), jnp.broadcast_to(count, (1, 16))]
    table = jnp.concatenate(rows + [jnp.zeros((80, 16), F32)], axis=0)
    table = jnp.concatenate([table, jnp.zeros((128, 112), F32)], axis=1)
    return table.T[0:16, :]


def prepare_kernel(
    v_hbm,
    d_hbm,
    jac_hbm,
    nbr_hbm,
    count_hbm,
    g_ref,
    table_ref,
    v_ref,
    d_ref,
    jac_ref,
    nbr_ref,
    count_ref,
    sems,
):
    small = [
        pltpu.make_async_copy(jac_hbm, jac_ref, sems.at[2 * NC]),
        pltpu.make_async_copy(nbr_hbm, nbr_ref, sems.at[2 * NC + 1]),
        pltpu.make_async_copy(count_hbm, count_ref, sems.at[2 * NC + 2]),
    ]
    v_copies = [
        pltpu.make_async_copy(v_hbm.at[j], v_ref.at[j], sems.at[j]) for j in range(NC)
    ]
    d_copies = [
        pltpu.make_async_copy(d_hbm.at[j], d_ref.at[j], sems.at[NC + j]) for j in range(NC)
    ]
    for copy in small:
        copy.start()
    for j in range(NC):
        v_copies[j].start()
        d_copies[j].start()
    for copy in small:
        copy.wait()
    count = count_ref[0, 0].astype(F32)
    table = table_of(jac_ref, nbr_ref, count)
    table_ref[...] = table
    packed = table[0:8, :] + pltpu.roll(table[8:16, :], 64, 1)
    packed = packed + jnp.where(lanes((8, 128)) >= GROUP_CNT, count, 0.0)
    packed = packed.reshape(4, 2, 128)
    acc = jnp.zeros((128, 256), F32)
    for j in range(NC):
        v_copies[j].wait()
        d_copies[j].wait()
        acc = acc + lax.dot_general(
            d_ref[j], v_ref[j], (((0,), (0,)), ((), ())), preferred_element_type=F32
        )
    pairs = acc.T.reshape(128, 2, 128)
    for p in range(16):
        for m in range(4):
            at = 32 * m + 2 * p
            g_ref[12 * p + 2 * m : 12 * p + 2 * m + 2] = pairs[at : at + 2]
        g_ref[12 * p + 8 : 12 * p + 12] = packed


def prepare(test, deim, jac, nbr, counts):
    return pl.pallas_call(
        prepare_kernel,
        in_specs=[HBM, HBM, HBM, HBM, HBM],
        out_specs=[VMEM, VMEM],
        out_shape=[
            jax.ShapeDtypeStruct((192, 2, 128), F32),
            jax.ShapeDtypeStruct((16, 128), F32),
        ],
        scratch_shapes=[
            pltpu.VMEM(test.shape, BF16),
            pltpu.VMEM(deim.shape, BF16),
            pltpu.VMEM((NC, NB, 16), F32),
            pltpu.VMEM((NB, 16), jnp.int32),
            pltpu.SMEM((1, 1), jnp.int32),
            pltpu.SemaphoreType.DMA((2 * NC + 3,)),
        ],
        name="prepare",
    )(test, deim, jac, nbr, counts)


def sample_kernel(x_ref, nbr_ref, edge_ref, u_ref, out_ref):
    rank = jnp.floor(nbr_ref[0:1, 0:1].astype(F32) * (1.0 / 512.0))
    place = rank - 16.0 * jnp.floor(rank * 0.0625)
    lane = lanes((1, 128))
    total = jnp.zeros((8, 2, 128), F32)
    blank = jnp.zeros((4, 2, 128), F32)
    near = [blank, blank, blank]
    extra = jnp.zeros((1, 128), F32)
    for p in range(16):
        total = total + x_ref[12 * p : 12 * p + 8]
        packed = x_ref[12 * p + 8 : 12 * p + 12]
        near = [
            near[k] + jnp.where((place == p + 1 - k)[None], packed, 0.0) for k in range(3)
        ]
        extra = extra + jnp.where(lane == GROUP_CNT + p, packed[0, 0:1, :], 0.0)
    total = total.reshape(16, 128)
    slot = lax.broadcasted_iota(jnp.int32, (16, 128), 0).astype(F32)
    entry = lanes((16, 128)) < NBR
    tables = []
    for k, edge in ((0, 0.0), (1, None), (2, 15.0)):
        rows = near[k].reshape(8, 128)
        rows = jnp.concatenate([rows, pltpu.roll(rows, 64, 1)], axis=0)
        if edge is not None:
            rows = jnp.where(place == edge, edge_ref[...], rows)
        extra = extra + jnp.where(lane == LOW_CNT + k, rows[0:1, CNT : CNT + 1], 0.0) * (k < 2)
        dead = entry & (slot >= rows[:, CNT : CNT + 1])
        tables.append(jnp.where(dead, 0.0, rows))
    cell = lanes((16, 128)).astype(F32) + rank * 512.0
    zero = jnp.zeros((16, 128), F32)

    def weights(table, part, j):
        at = cell + 128.0 * part
        weight = zero
        for n in range(NB):
            hit = at == table[:, NBR + n : NBR + n + 1]
            weight = weight + jnp.where(hit, table[:, 8 * j + n : 8 * j + n + 1], 0.0)
        return weight

    low, own, high = tables
    sums = jnp.zeros((96, 256), F32)
    for j in range(NC):
        weight = jnp.concatenate(
            [
                jnp.concatenate([weights(low, 0, j), zero, zero, zero], axis=1),
                jnp.concatenate([weights(own, part, j) for part in range(4)], axis=1),
                jnp.concatenate([zero, zero, zero, weights(high, 3, j)], axis=1),
            ],
            axis=0,
        )
        upper = weight.astype(BF16)
        rest = (weight - upper.astype(F32)).astype(BF16)
        sums = sums + jnp.dot(
            jnp.concatenate([upper, rest], axis=0), u_ref[j], preferred_element_type=F32
        )
    rows = sums[0:48, :] + sums[48:96, :]
    b_exp, g_exp = exponent(rows), exponent(total)
    rows = jnp.concatenate([coded(rows, b_exp), jnp.zeros((80, 256), F32)], axis=0)
    extra = extra + jnp.where(lane == RANK, rank, 0.0)
    extra = extra + jnp.where(lane == B_EXP, b_exp, 0.0) + jnp.where(lane == G_EXP, g_exp, 0.0)
    cols = rows.T
    code = coded(total, g_exp)
    for z in range(8):
        left = cols[32 * z : 32 * z + 16, :]
        right = pltpu.roll(cols[32 * z + 16 : 32 * z + 32, :], 48, 1)
        out_ref[z] = to_i16(jnp.concatenate([code, left + right + extra], axis=0))


def sample(g_parts, nbr, edge, trial):
    return pl.pallas_call(
        sample_kernel,
        out_shape=jax.ShapeDtypeStruct((8, 32, 128), jnp.int16),
        in_specs=[VMEM] * 4,
        out_specs=VMEM,
        compiler_params=PARAMS,
        name="sample",
    )(g_parts, nbr, edge, trial)


def fold_kernel(x_ref, s_ref, out_ref):
    blocks = [from_i16(x_ref[z]) for z in range(8)]
    info = jnp.concatenate([block[16:17, :] for block in blocks], axis=0)
    lane = lanes((8, 128))

    def column(k):
        return jnp.sum(jnp.where(lane == k, info, 0.0), axis=1, keepdims=True)

    g_scale = jnp.exp2(-column(G_EXP))
    b_scale = jnp.exp2(-column(B_EXP))
    total = jnp.zeros((16, 128), F32)
    for z in range(8):
        total = total + decoded(blocks[z][0:16, :]) * g_scale[z : z + 1, :]
    rank = column(RANK)
    place = rank - 16.0 * jnp.floor(rank * 0.0625)
    is_count = (lane >= GROUP_CNT) & (lane < GROUP_CNT + 16)
    counts = jnp.where(is_count, info, 0.0)
    before = lax.broadcasted_iota(jnp.int32, (8, 8), 1) < lax.broadcasted_iota(
        jnp.int32, (8, 8), 0
    )
    lower = jnp.dot(before.astype(F32), counts, preferred_element_type=F32)
    ahead = (lane - GROUP_CNT).astype(F32) < place
    lower = lower + jnp.where(ahead, counts, 0.0)
    offset = jnp.sum(lower, axis=1, keepdims=True)
    shift = jnp.where(lane < 16, -column(LOW_CNT), jnp.where(lane < 32, 0.0, column(OWN_CNT)))
    ids = jnp.where(lane < 48, offset + shift + (lane % 16).astype(F32), -1.0)
    slots = lanes((1, 128)) < 48
    mode = lax.broadcasted_iota(jnp.int32, (512, 128), 0).astype(F32)
    sampled = jnp.zeros((32, 512), F32)
    for z in range(8):
        hot = jnp.where(mode == ids[z : z + 1, :], 1.0, 0.0).astype(BF16)
        both = decoded(blocks[z][16:32, :])
        both = jnp.concatenate([both, pltpu.roll(both, 80, 1)], axis=0)
        cols = jnp.where(slots, both, 0.0)
        high = cols.astype(BF16)
        rest = (cols - high.astype(F32)).astype(BF16)
        part = lax.dot_general(
            jnp.concatenate([high, rest], axis=0),
            hot,
            (((1,), (1,)), ((), ())),
            preferred_element_type=F32,
        )
        sampled = sampled + (part[0:32, :] + part[32:64, :]) * b_scale[z : z + 1, :]
    c = lax.dot_general(
        sampled,
        s_ref[...],
        (((1,), (1,)), ((), ())),
        precision=lax.Precision.HIGHEST,
        preferred_element_type=F32,
    )
    g_pairs = total.reshape(8, 2, 128)
    c_pairs = c.reshape(16, 2, 128)
    for p in range(16):
        for m in range(4):
            at = 3 * (4 * p + m)
            out_ref[at : at + 2] = g_pairs[2 * m : 2 * m + 2]
            out_ref[at + 2] = c_pairs[p]


def fold(parts, inverse):
    return pl.pallas_call(
        fold_kernel,
        out_shape=jax.ShapeDtypeStruct((192, 2, 128), F32),
        in_specs=[VMEM] * 2,
        out_specs=VMEM,
        compiler_params=PARAMS,
        name="fold",
    )(parts, inverse)


def finish_kernel(x_ref, out_ref):
    result = jnp.zeros((2, 64), F32)
    for m in range(4):
        rows = [x_ref[3 * (4 * p + m) : 3 * (4 * p + m) + 2] for p in range(16)]
        c = x_ref[3 * m + 2]
        for p in range(1, 16):
            c = c + x_ref[3 * (4 * p + m) + 2]
        result = result + lax.dot_general(
            c,
            jnp.concatenate(rows, axis=0).reshape(64, 128),
            (((1,), (1,)), ((), ())),
            precision=lax.Precision.HIGHEST,
            preferred_element_type=F32,
        )
    out_ref[...] = result


def finish(parts):
    return pl.pallas_call(
        finish_kernel,
        out_shape=jax.ShapeDtypeStruct((2, 64), F32),
        in_specs=[VMEM] * 1,
        out_specs=VMEM,
        compiler_params=PARAMS,
        name="finish",
    )(parts)


def shards(test_basis, deim_basis, trial_basis, jacobian, neighbours, counts, sample_inverse):
    jac, nbr, count = jacobian.transpose(2, 1, 0), neighbours.T, counts.reshape(1, 1)
    g_part, own = prepare(test_basis.swapaxes(0, 1), deim_basis.swapaxes(0, 1), jac, nbr, count)
    groups, group = lax.axis_size(ROWS), lax.axis_size(GROUP)
    across = [(i - 1, i) for i in range(group, groups, group)]
    across += [(target, source) for source, target in across]
    edge = lax.ppermute(own, ROWS, across)
    g_group = lax.all_to_all(g_part, GROUP, 0, 0, tiled=True)
    sent = sample(g_group, nbr, edge, trial_basis.swapaxes(0, 1))
    parts = lax.all_to_all(sent, "zh", 0, 0, tiled=True)
    pieces = lax.all_to_all(fold(parts, sample_inverse), CUBE, 0, 0, tiled=True)
    return finish(pieces).T


def solution(mesh):
    split = Mesh(mesh.devices.reshape(8, 2, 4, 2, 4), ("zh", "zl", "x", "c", "y"))
    placed = (
        P(ROWS, None, None),
        P(ROWS, None, "y"),
        P(ROWS, None, None),
        P(ROWS, None, None),
        P(ROWS, None),
        P(ROWS),
        P("y", None),
    )
    return jax.shard_map(
        shards, mesh=split, in_specs=placed, out_specs=P("y", ROWS), check_vma=False
    )
```

```python
import jax
import jax.numpy as jnp
from jax import lax
from jax.experimental import pallas as pl
from jax.experimental.pallas import tpu as pltpu
from jax.sharding import Mesh
from jax.sharding import PartitionSpec as P

ROWS = ("zh", "zl", "x", "c")
GROUP = ("zl", "x", "c")
CUBE = ("zl", "x", "c", "y")
F32 = jnp.float32
BF16 = jnp.bfloat16
NC, NB = 5, 7
NBR, CNT = 40, 47
LOW_CNT, OWN_CNT, RANK, G_EXP, B_EXP, GROUP_CNT = 96, 97, 98, 99, 100, 112
TOP = 32000.0


VMEM = pl.BlockSpec(memory_space=pltpu.VMEM)
HBM = pl.BlockSpec(memory_space=pltpu.HBM)
PARAMS = pltpu.CompilerParams(vmem_limit_bytes=12 * 1024 * 1024)


def lanes(shape):
    return lax.broadcasted_iota(jnp.int32, shape, len(shape) - 1)


def exponent(x):
    top = jnp.max(jnp.abs(x), axis=(0, 1), keepdims=True)
    return jnp.floor(-jnp.log2(jnp.maximum(top, 1e-30)))


def coded(x, exp):
    code = jnp.floor(jnp.sqrt(jnp.sqrt(jnp.abs(x * jnp.exp2(exp)))) * TOP + 0.5)
    return jnp.where(x < 0.0, -code, code)


def decoded(code):
    root = code * (1.0 / TOP)
    square = root * root
    return square * square * jnp.where(code < 0.0, -1.0, 1.0)


def to_i16(x):
    return x.astype(jnp.int32).astype(jnp.int16)


def from_i16(x):
    return x.astype(jnp.int32).astype(F32)


def table_of(jac_ref, nbr_ref, count):
    blank = jnp.zeros((1, 16), F32)
    rows = []
    for j in range(NC):
        rows += [jac_ref[j], blank]
    rows += [nbr_ref[...].astype(F32), jnp.broadcast_to(count, (1, 16))]
    table = jnp.concatenate(rows + [jnp.zeros((80, 16), F32)], axis=0)
    table = jnp.concatenate([table, jnp.zeros((128, 112), F32)], axis=1)
    return table.T[0:16, :]


def prepare_kernel(
    v_hbm,
    d_hbm,
    jac_hbm,
    nbr_hbm,
    count_hbm,
    g_ref,
    table_ref,
    v_ref,
    d_ref,
    jac_ref,
    nbr_ref,
    count_ref,
    sems,
):
    small = [
        pltpu.make_async_copy(jac_hbm, jac_ref, sems.at[2 * NC]),
        pltpu.make_async_copy(nbr_hbm, nbr_ref, sems.at[2 * NC + 1]),
        pltpu.make_async_copy(count_hbm, count_ref, sems.at[2 * NC + 2]),
    ]
    v_copies = [
        pltpu.make_async_copy(v_hbm.at[j], v_ref.at[j], sems.at[j]) for j in range(NC)
    ]
    d_copies = [
        pltpu.make_async_copy(d_hbm.at[j], d_ref.at[j], sems.at[NC + j]) for j in range(NC)
    ]
    for copy in small:
        copy.start()
    for j in range(NC):
        v_copies[j].start()
        d_copies[j].start()
    for copy in small:
        copy.wait()
    count = count_ref[0, 0].astype(F32)
    table = table_of(jac_ref, nbr_ref, count)
    table_ref[...] = table
    packed = table[0:8, :] + pltpu.roll(table[8:16, :], 64, 1)
    packed = packed + jnp.where(lanes((8, 128)) >= GROUP_CNT, count, 0.0)
    packed = packed.reshape(4, 2, 128)
    acc = jnp.zeros((128, 256), F32)
    for j in range(NC):
        v_copies[j].wait()
        d_copies[j].wait()
        acc = acc + lax.dot_general(
            d_ref[j], v_ref[j], (((0,), (0,)), ((), ())), preferred_element_type=F32
        )
    pairs = acc.T.reshape(128, 2, 128)
    for p in range(16):
        for m in range(4):
            at = 32 * m + 2 * p
            g_ref[12 * p + 2 * m : 12 * p + 2 * m + 2] = pairs[at : at + 2]
        g_ref[12 * p + 8 : 12 * p + 12] = packed


def prepare(test, deim, jac, nbr, counts):
    return pl.pallas_call(
        prepare_kernel,
        in_specs=[HBM, HBM, HBM, HBM, HBM],
        out_specs=[VMEM, VMEM],
        out_shape=[
            jax.ShapeDtypeStruct((192, 2, 128), F32),
            jax.ShapeDtypeStruct((16, 128), F32),
        ],
        scratch_shapes=[
            pltpu.VMEM(test.shape, BF16),
            pltpu.VMEM(deim.shape, BF16),
            pltpu.VMEM((NC, NB, 16), F32),
            pltpu.VMEM((NB, 16), jnp.int32),
            pltpu.SMEM((1, 1), jnp.int32),
            pltpu.SemaphoreType.DMA((2 * NC + 3,)),
        ],
        name="prepare",
    )(test, deim, jac, nbr, counts)


def halves(x):
    upper = x.astype(BF16)
    return upper, (x - upper.astype(F32)).astype(BF16)


def alive(rows):
    slot = lax.broadcasted_iota(jnp.int32, (16, 128), 0).astype(F32)
    dead = (lanes((16, 128)) < NBR) & (slot >= rows[:, CNT : CNT + 1])
    return jnp.where(dead, 0.0, rows)


def weights(table, cell, j):
    weight = jnp.zeros((16, 128), F32)
    for n in range(NB):
        hit = cell == table[:, NBR + n : NBR + n + 1]
        weight = weight + jnp.where(hit, table[:, 8 * j + n : 8 * j + n + 1], 0.0)
    return weight


def own_kernel(table_ref, u_ref, s_ref, sums_ref, upper_ref, rest_ref):
    table = table_ref[...]
    rank = jnp.floor(table[0:1, NBR : NBR + 1] * (1.0 / 512.0))
    own = alive(table)
    cell = lanes((16, 128)).astype(F32) + rank * 512.0
    sums = jnp.zeros((32, 256), F32)
    for j in range(NC):
        parts = [weights(own, cell + 128.0 * part, j) for part in range(4)]
        pieces = halves(jnp.concatenate(parts, axis=1))
        sums = sums + jnp.dot(
            jnp.concatenate(pieces, axis=0), u_ref[j], preferred_element_type=F32
        )
    sums_ref[...] = sums[0:16, :] + sums[16:32, :]
    upper_ref[...], rest_ref[...] = halves(s_ref[...])


def own_part(table, trial, inverse):
    return pl.pallas_call(
        own_kernel,
        out_shape=[
            jax.ShapeDtypeStruct((16, 256), F32),
            jax.ShapeDtypeStruct(inverse.shape, BF16),
            jax.ShapeDtypeStruct(inverse.shape, BF16),
        ],
        in_specs=[VMEM] * 3,
        out_specs=[VMEM] * 3,
        compiler_params=PARAMS,
        name="own_part",
    )(table, trial, inverse)


def sample_kernel(x_ref, nbr_ref, edge_ref, own_ref, u_ref, out_ref):
    rank = jnp.floor(nbr_ref[0:1, 0:1].astype(F32) * (1.0 / 512.0))
    place = rank - 16.0 * jnp.floor(rank * 0.0625)
    lane = lanes((1, 128))
    total = jnp.zeros((8, 2, 128), F32)
    blank = jnp.zeros((4, 2, 128), F32)
    near = [blank, blank, blank]
    extra = jnp.zeros((1, 128), F32)
    for p in range(16):
        total = total + x_ref[12 * p : 12 * p + 8]
        packed = x_ref[12 * p + 8 : 12 * p + 12]
        near = [
            near[k] + jnp.where((place == p + 1 - k)[None], packed, 0.0) for k in range(3)
        ]
        extra = extra + jnp.where(lane == GROUP_CNT + p, packed[0, 0:1, :], 0.0)
    total = total.reshape(16, 128)
    tables = []
    for k, edge in ((0, 0.0), (1, None), (2, 15.0)):
        rows = near[k].reshape(8, 128)
        rows = jnp.concatenate([rows, pltpu.roll(rows, 64, 1)], axis=0)
        if edge is not None:
            rows = jnp.where(place == edge, edge_ref[...], rows)
        if k < 2:
            extra = extra + jnp.where(lane == LOW_CNT + k, rows[0:1, CNT : CNT + 1], 0.0)
        tables.append(alive(rows))
    cell = lanes((16, 128)).astype(F32) + rank * 512.0
    low = jnp.zeros((32, 256), F32)
    high = jnp.zeros((32, 256), F32)
    for j in range(NC):
        pieces = halves(weights(tables[0], cell, j))
        low = low + jnp.dot(
            jnp.concatenate(pieces, axis=0), u_ref[j, 0:128, :], preferred_element_type=F32
        )
        pieces = halves(weights(tables[2], cell + 384.0, j))
        high = high + jnp.dot(
            jnp.concatenate(pieces, axis=0), u_ref[j, 384:512, :], preferred_element_type=F32
        )
    rows = jnp.concatenate(
        [low[0:16, :] + low[16:32, :], own_ref[...], high[0:16, :] + high[16:32, :]], axis=0
    )
    b_exp, g_exp = exponent(rows), exponent(total)
    rows = jnp.concatenate([coded(rows, b_exp), jnp.zeros((80, 256), F32)], axis=0)
    extra = extra + jnp.where(lane == RANK, rank, 0.0)
    extra = extra + jnp.where(lane == B_EXP, b_exp, 0.0) + jnp.where(lane == G_EXP, g_exp, 0.0)
    cols = rows.T
    code = coded(total, g_exp)
    for z in range(8):
        left = cols[32 * z : 32 * z + 16, :]
        right = pltpu.roll(cols[32 * z + 16 : 32 * z + 32, :], 48, 1)
        out_ref[z] = to_i16(jnp.concatenate([code, left + right + extra], axis=0))


def sample(g_parts, nbr, edge, own, trial):
    return pl.pallas_call(
        sample_kernel,
        out_shape=jax.ShapeDtypeStruct((8, 32, 128), jnp.int16),
        in_specs=[VMEM] * 5,
        out_specs=VMEM,
        compiler_params=PARAMS,
        name="sample",
    )(g_parts, nbr, edge, own, trial)


def fold_kernel(x_ref, upper_ref, rest_ref, out_ref):
    blocks = [from_i16(x_ref[z]) for z in range(8)]
    info = jnp.concatenate([block[16:17, :] for block in blocks], axis=0)
    lane = lanes((8, 128))

    def column(k):
        return jnp.sum(jnp.where(lane == k, info, 0.0), axis=1, keepdims=True)

    g_scale = jnp.exp2(-column(G_EXP))
    b_scale = jnp.exp2(-column(B_EXP))
    total = jnp.zeros((16, 128), F32)
    for z in range(8):
        total = total + decoded(blocks[z][0:16, :]) * g_scale[z : z + 1, :]
    rank = column(RANK)
    place = rank - 16.0 * jnp.floor(rank * 0.0625)
    is_count = (lane >= GROUP_CNT) & (lane < GROUP_CNT + 16)
    counts = jnp.where(is_count, info, 0.0)
    before = lax.broadcasted_iota(jnp.int32, (8, 8), 1) < lax.broadcasted_iota(
        jnp.int32, (8, 8), 0
    )
    lower = jnp.dot(before.astype(F32), counts, preferred_element_type=F32)
    ahead = (lane - GROUP_CNT).astype(F32) < place
    lower = lower + jnp.where(ahead, counts, 0.0)
    offset = jnp.sum(lower, axis=1, keepdims=True)
    shift = jnp.where(lane < 16, -column(LOW_CNT), jnp.where(lane < 32, 0.0, column(OWN_CNT)))
    ids = jnp.where(lane < 48, offset + shift + (lane % 16).astype(F32), -1.0)
    at = lanes((1, 128))
    mode = lax.broadcasted_iota(jnp.int32, (512, 128), 0).astype(F32)
    sampled = jnp.zeros((64, 512), F32)
    for z in range(0, 8, 2):
        here, there = (
            decoded(blocks[k][16:32, :]) * b_scale[k : k + 1, :] for k in (z, z + 1)
        )
        first = jnp.where(at < 48, here, jnp.where(at < 96, pltpu.roll(there, 48, 1), 0.0))
        second = jnp.where(at < 48, pltpu.roll(here, 80, 1), jnp.where(at < 96, there, 0.0))
        row = jnp.where(at < 48, ids[z : z + 1, :], pltpu.roll(ids[z + 1 : z + 2, :], 48, 1))
        hot = jnp.where(mode == row, 1.0, 0.0).astype(BF16)
        pieces = halves(jnp.concatenate([first, second], axis=0))
        sampled = sampled + lax.dot_general(
            jnp.concatenate(pieces, axis=0),
            hot,
            (((1,), (1,)), ((), ())),
            preferred_element_type=F32,
        )
    sampled = sampled[0:32, :] + sampled[32:64, :]
    upper, rest = halves(sampled)
    c = lax.dot_general(
        jnp.concatenate([upper, rest], axis=0),
        upper_ref[...],
        (((1,), (1,)), ((), ())),
        preferred_element_type=F32,
    )
    c = (c[0:32, :] + c[32:64, :]) + lax.dot_general(
        upper, rest_ref[...], (((1,), (1,)), ((), ())), preferred_element_type=F32
    )
    g_pairs = total.reshape(8, 2, 128)
    c_pairs = c.reshape(16, 2, 128)
    for p in range(16):
        for m in range(4):
            at = 3 * (4 * p + m)
            out_ref[at : at + 2] = g_pairs[2 * m : 2 * m + 2]
            out_ref[at + 2] = c_pairs[p]


def fold(parts, upper, rest):
    return pl.pallas_call(
        fold_kernel,
        out_shape=jax.ShapeDtypeStruct((192, 2, 128), F32),
        in_specs=[VMEM] * 3,
        out_specs=VMEM,
        compiler_params=PARAMS,
        name="fold",
    )(parts, upper, rest)


def finish_kernel(x_ref, out_ref):
    sums = [jnp.zeros((64, 128), F32), jnp.zeros((64, 128), F32)]
    for m in range(4):
        rows = [x_ref[3 * (4 * p + m) : 3 * (4 * p + m) + 2] for p in range(16)]
        rows = jnp.concatenate(rows, axis=0).reshape(64, 128)
        c = x_ref[3 * m + 2]
        for p in range(1, 16):
            c = c + x_ref[3 * (4 * p + m) + 2]
        sums = [sums[j] + rows * c[j : j + 1, :] for j in range(2)]
    total = jnp.sum(jnp.concatenate(sums, axis=0).T, axis=0, keepdims=True)
    out_ref[0:1, :] = total[:, 0:64]
    out_ref[1:2, :] = total[:, 64:128]


def finish(parts):
    return pl.pallas_call(
        finish_kernel,
        out_shape=jax.ShapeDtypeStruct((2, 64), F32),
        in_specs=[VMEM] * 1,
        out_specs=VMEM,
        compiler_params=PARAMS,
        name="finish",
    )(parts)


def shards(test_basis, deim_basis, trial_basis, jacobian, neighbours, counts, sample_inverse):
    jac, nbr, count = jacobian.transpose(2, 1, 0), neighbours.T, counts.reshape(1, 1)
    g_part, own = prepare(test_basis.swapaxes(0, 1), deim_basis.swapaxes(0, 1), jac, nbr, count)
    groups, group = lax.axis_size(ROWS), lax.axis_size(GROUP)
    across = [(i - 1, i) for i in range(group, groups, group)]
    across += [(target, source) for source, target in across]
    edge = lax.ppermute(own, ROWS, across)
    g_group = lax.all_to_all(g_part, GROUP, 0, 0, tiled=True)
    trial = trial_basis.swapaxes(0, 1)
    mine, upper, rest = own_part(own, trial, sample_inverse)
    sent = sample(g_group, nbr, edge, mine, trial)
    parts = lax.all_to_all(sent, "zh", 0, 0, tiled=True)
    pieces = lax.all_to_all(fold(parts, upper, rest), CUBE, 0, 0, tiled=True)
    return finish(pieces).T


def solution(mesh):
    split = Mesh(mesh.devices.reshape(8, 2, 4, 2, 4), ("zh", "zl", "x", "c", "y"))
    placed = (
        P(ROWS, None, None),
        P(ROWS, None, "y"),
        P(ROWS, None, None),
        P(ROWS, None, None),
        P(ROWS, None),
        P(ROWS),
        P("y", None),
    )
    return jax.shard_map(
        shards, mesh=split, in_specs=placed, out_specs=P("y", ROWS), check_vma=False
    )
```

```python
import jax
import jax.numpy as jnp
from jax import lax
from jax.experimental import pallas as pl
from jax.experimental.pallas import tpu as pltpu
from jax.sharding import Mesh
from jax.sharding import PartitionSpec as P

ROWS = ("zh", "zl", "x", "c")
GROUP = ("zl", "x", "c")
CUBE = ("zl", "x", "c", "y")
F32 = jnp.float32
BF16 = jnp.bfloat16
NC, NB = 5, 7
NBR, CNT = 40, 47
LOW_CNT, OWN_CNT, RANK, G_EXP, B_EXP, GROUP_CNT = 96, 97, 98, 99, 100, 112
TOP = 32000.0


VMEM = pl.BlockSpec(memory_space=pltpu.VMEM)
HBM = pl.BlockSpec(memory_space=pltpu.HBM)
PARAMS = pltpu.CompilerParams(vmem_limit_bytes=12 * 1024 * 1024)


def lanes(shape):
    return lax.broadcasted_iota(jnp.int32, shape, len(shape) - 1)


def exponent(x):
    top = jnp.max(jnp.abs(x), axis=(0, 1), keepdims=True)
    return jnp.floor(-jnp.log2(jnp.maximum(top, 1e-30)))


def coded(x, exp):
    code = jnp.floor(jnp.sqrt(jnp.sqrt(jnp.abs(x * jnp.exp2(exp)))) * TOP + 0.5)
    return jnp.where(x < 0.0, -code, code)


def decoded(code):
    root = code * (1.0 / TOP)
    square = root * root
    return square * square * jnp.where(code < 0.0, -1.0, 1.0)


def to_i16(x):
    return x.astype(jnp.int32).astype(jnp.int16)


def from_i16(x):
    return x.astype(jnp.int32).astype(F32)


def table_of(jac_ref, nbr_ref, count):
    blank = jnp.zeros((1, 16), F32)
    rows = []
    for j in range(NC):
        rows += [jac_ref[j], blank]
    rows += [nbr_ref[...].astype(F32), jnp.broadcast_to(count, (1, 16))]
    table = jnp.concatenate(rows + [jnp.zeros((80, 16), F32)], axis=0)
    table = jnp.concatenate([table, jnp.zeros((128, 112), F32)], axis=1)
    return table.T[0:16, :]


def prepare_kernel(
    v_hbm,
    d_hbm,
    jac_hbm,
    nbr_hbm,
    count_hbm,
    g_ref,
    table_ref,
    v_ref,
    d_ref,
    jac_ref,
    nbr_ref,
    count_ref,
    sems,
):
    small = [
        pltpu.make_async_copy(jac_hbm, jac_ref, sems.at[2 * NC]),
        pltpu.make_async_copy(nbr_hbm, nbr_ref, sems.at[2 * NC + 1]),
        pltpu.make_async_copy(count_hbm, count_ref, sems.at[2 * NC + 2]),
    ]
    v_copies = [
        pltpu.make_async_copy(v_hbm.at[j], v_ref.at[j], sems.at[j]) for j in range(NC)
    ]
    d_copies = [
        pltpu.make_async_copy(d_hbm.at[j], d_ref.at[j], sems.at[NC + j]) for j in range(NC)
    ]
    for copy in small:
        copy.start()
    for j in range(NC):
        v_copies[j].start()
        d_copies[j].start()
    for copy in small:
        copy.wait()
    count = count_ref[0, 0].astype(F32)
    table = table_of(jac_ref, nbr_ref, count)
    table_ref[...] = table
    packed = table[0:8, :] + pltpu.roll(table[8:16, :], 64, 1)
    packed = packed + jnp.where(lanes((8, 128)) >= GROUP_CNT, count, 0.0)
    packed = packed.reshape(4, 2, 128)
    acc = jnp.zeros((128, 256), F32)
    for j in range(NC):
        v_copies[j].wait()
        d_copies[j].wait()
        acc = acc + lax.dot_general(
            d_ref[j], v_ref[j], (((0,), (0,)), ((), ())), preferred_element_type=F32
        )
    pairs = acc.T.reshape(128, 2, 128)
    for p in range(16):
        for m in range(4):
            at = 32 * m + 2 * p
            g_ref[12 * p + 2 * m : 12 * p + 2 * m + 2] = pairs[at : at + 2]
        g_ref[12 * p + 8 : 12 * p + 12] = packed


def prepare(test, deim, jac, nbr, counts):
    return pl.pallas_call(
        prepare_kernel,
        in_specs=[HBM, HBM, HBM, HBM, HBM],
        out_specs=[VMEM, VMEM],
        out_shape=[
            jax.ShapeDtypeStruct((192, 2, 128), F32),
            jax.ShapeDtypeStruct((16, 128), F32),
        ],
        scratch_shapes=[
            pltpu.VMEM(test.shape, BF16),
            pltpu.VMEM(deim.shape, BF16),
            pltpu.VMEM((NC, NB, 16), F32),
            pltpu.VMEM((NB, 16), jnp.int32),
            pltpu.SMEM((1, 1), jnp.int32),
            pltpu.SemaphoreType.DMA((2 * NC + 3,)),
        ],
        name="prepare",
    )(test, deim, jac, nbr, counts)


def halves(x):
    upper = x.astype(BF16)
    return upper, (x - upper.astype(F32)).astype(BF16)


def alive(rows):
    slot = lax.broadcasted_iota(jnp.int32, (16, 128), 0).astype(F32)
    dead = (lanes((16, 128)) < NBR) & (slot >= rows[:, CNT : CNT + 1])
    return jnp.where(dead, 0.0, rows)


def weights(table, cell, j):
    weight = jnp.zeros((16, 128), F32)
    for n in range(NB):
        hit = cell == table[:, NBR + n : NBR + n + 1]
        weight = weight + jnp.where(hit, table[:, 8 * j + n : 8 * j + n + 1], 0.0)
    return weight


def own_kernel(table_ref, u_ref, s_ref, edge_ref, sums_ref, upper_ref, rest_ref):
    table = table_ref[...]
    edge_ref[...] = table
    rank = jnp.floor(table[0:1, NBR : NBR + 1] * (1.0 / 512.0))
    own = alive(table)
    cell = lanes((16, 128)).astype(F32) + rank * 512.0
    sums = jnp.zeros((32, 256), F32)
    for j in range(NC):
        parts = [weights(own, cell + 128.0 * part, j) for part in range(4)]
        pieces = halves(jnp.concatenate(parts, axis=1))
        sums = sums + jnp.dot(
            jnp.concatenate(pieces, axis=0), u_ref[j], preferred_element_type=F32
        )
    sums_ref[...] = sums[0:16, :] + sums[16:32, :]
    upper_ref[...], rest_ref[...] = halves(s_ref[...])


def own_part(table, trial, inverse):
    return pl.pallas_call(
        own_kernel,
        out_shape=[
            jax.ShapeDtypeStruct((16, 128), F32),
            jax.ShapeDtypeStruct((16, 256), F32),
            jax.ShapeDtypeStruct(inverse.shape, BF16),
            jax.ShapeDtypeStruct(inverse.shape, BF16),
        ],
        in_specs=[VMEM] * 3,
        out_specs=[VMEM] * 4,
        compiler_params=PARAMS,
        name="own_part",
    )(table, trial, inverse)


def sample_kernel(x_ref, nbr_ref, edge_ref, own_ref, u_ref, out_ref):
    rank = jnp.floor(nbr_ref[0:1, 0:1].astype(F32) * (1.0 / 512.0))
    place = rank - 16.0 * jnp.floor(rank * 0.0625)
    lane = lanes((1, 128))
    total = jnp.zeros((8, 2, 128), F32)
    blank = jnp.zeros((4, 2, 128), F32)
    near = [blank, blank, blank]
    extra = jnp.zeros((1, 128), F32)
    for p in range(16):
        total = total + x_ref[12 * p : 12 * p + 8]
        packed = x_ref[12 * p + 8 : 12 * p + 12]
        near = [
            near[k] + jnp.where((place == p + 1 - k)[None], packed, 0.0) for k in range(3)
        ]
        extra = extra + jnp.where(lane == GROUP_CNT + p, packed[0, 0:1, :], 0.0)
    total = total.reshape(16, 128)
    tables = []
    for k, edge in ((0, 0.0), (1, None), (2, 15.0)):
        rows = near[k].reshape(8, 128)
        rows = jnp.concatenate([rows, pltpu.roll(rows, 64, 1)], axis=0)
        if edge is not None:
            rows = jnp.where(place == edge, edge_ref[...], rows)
        if k < 2:
            extra = extra + jnp.where(lane == LOW_CNT + k, rows[0:1, CNT : CNT + 1], 0.0)
        tables.append(alive(rows))
    cell = lanes((16, 128)).astype(F32) + rank * 512.0
    low = jnp.zeros((32, 256), F32)
    high = jnp.zeros((32, 256), F32)
    for j in range(NC):
        pieces = halves(weights(tables[0], cell, j))
        low = low + jnp.dot(
            jnp.concatenate(pieces, axis=0), u_ref[j, 0:128, :], preferred_element_type=F32
        )
        pieces = halves(weights(tables[2], cell + 384.0, j))
        high = high + jnp.dot(
            jnp.concatenate(pieces, axis=0), u_ref[j, 384:512, :], preferred_element_type=F32
        )
    rows = jnp.concatenate(
        [low[0:16, :] + low[16:32, :], own_ref[...], high[0:16, :] + high[16:32, :]], axis=0
    )
    b_exp, g_exp = exponent(rows), exponent(total)
    rows = jnp.concatenate([coded(rows, b_exp), jnp.zeros((80, 256), F32)], axis=0)
    extra = extra + jnp.where(lane == RANK, rank, 0.0)
    extra = extra + jnp.where(lane == B_EXP, b_exp, 0.0) + jnp.where(lane == G_EXP, g_exp, 0.0)
    cols = rows.T
    code = coded(total, g_exp)
    for z in range(8):
        left = cols[32 * z : 32 * z + 16, :]
        right = pltpu.roll(cols[32 * z + 16 : 32 * z + 32, :], 48, 1)
        out_ref[z] = to_i16(jnp.concatenate([code, left + right + extra], axis=0))


def sample(g_parts, nbr, edge, own, trial):
    return pl.pallas_call(
        sample_kernel,
        out_shape=jax.ShapeDtypeStruct((8, 32, 128), jnp.int16),
        in_specs=[VMEM] * 5,
        out_specs=VMEM,
        compiler_params=PARAMS,
        name="sample",
    )(g_parts, nbr, edge, own, trial)


def fold_kernel(x_ref, upper_ref, rest_ref, out_ref):
    blocks = [from_i16(x_ref[z]) for z in range(8)]
    info = jnp.concatenate([block[16:17, :] for block in blocks], axis=0)
    lane = lanes((8, 128))

    def column(k):
        return jnp.sum(jnp.where(lane == k, info, 0.0), axis=1, keepdims=True)

    g_scale = jnp.exp2(-column(G_EXP))
    b_scale = jnp.exp2(-column(B_EXP))
    total = jnp.zeros((16, 128), F32)
    for z in range(8):
        total = total + decoded(blocks[z][0:16, :]) * g_scale[z : z + 1, :]
    rank = column(RANK)
    place = rank - 16.0 * jnp.floor(rank * 0.0625)
    is_count = (lane >= GROUP_CNT) & (lane < GROUP_CNT + 16)
    counts = jnp.where(is_count, info, 0.0)
    before = lax.broadcasted_iota(jnp.int32, (8, 8), 1) < lax.broadcasted_iota(
        jnp.int32, (8, 8), 0
    )
    lower = jnp.dot(before.astype(F32), counts, preferred_element_type=F32)
    ahead = (lane - GROUP_CNT).astype(F32) < place
    lower = lower + jnp.where(ahead, counts, 0.0)
    offset = jnp.sum(lower, axis=1, keepdims=True)
    shift = jnp.where(lane < 16, -column(LOW_CNT), jnp.where(lane < 32, 0.0, column(OWN_CNT)))
    ids = jnp.where(lane < 48, offset + shift + (lane % 16).astype(F32), -1.0)
    at = lanes((1, 128))
    mode = lax.broadcasted_iota(jnp.int32, (512, 128), 0).astype(F32)
    sampled = jnp.zeros((64, 512), F32)
    for z in range(0, 8, 2):
        here, there = (
            decoded(blocks[k][16:32, :]) * b_scale[k : k + 1, :] for k in (z, z + 1)
        )
        first = jnp.where(at < 48, here, jnp.where(at < 96, pltpu.roll(there, 48, 1), 0.0))
        second = jnp.where(at < 48, pltpu.roll(here, 80, 1), jnp.where(at < 96, there, 0.0))
        row = jnp.where(at < 48, ids[z : z + 1, :], pltpu.roll(ids[z + 1 : z + 2, :], 48, 1))
        hot = jnp.where(mode == row, 1.0, 0.0).astype(BF16)
        pieces = halves(jnp.concatenate([first, second], axis=0))
        sampled = sampled + lax.dot_general(
            jnp.concatenate(pieces, axis=0),
            hot,
            (((1,), (1,)), ((), ())),
            preferred_element_type=F32,
        )
    sampled = sampled[0:32, :] + sampled[32:64, :]
    upper, rest = halves(sampled)
    c = lax.dot_general(
        jnp.concatenate([upper, rest], axis=0),
        upper_ref[...],
        (((1,), (1,)), ((), ())),
        preferred_element_type=F32,
    )
    c = (c[0:32, :] + c[32:64, :]) + lax.dot_general(
        upper, rest_ref[...], (((1,), (1,)), ((), ())), preferred_element_type=F32
    )
    g_pairs = total.reshape(8, 2, 128)
    c_pairs = c.reshape(16, 2, 128)
    for p in range(16):
        for m in range(4):
            at = 3 * (4 * p + m)
            out_ref[at : at + 2] = g_pairs[2 * m : 2 * m + 2]
            out_ref[at + 2] = c_pairs[p]


def fold(parts, upper, rest):
    return pl.pallas_call(
        fold_kernel,
        out_shape=jax.ShapeDtypeStruct((192, 2, 128), F32),
        in_specs=[VMEM] * 3,
        out_specs=VMEM,
        compiler_params=PARAMS,
        name="fold",
    )(parts, upper, rest)


def finish_kernel(x_ref, out_ref):
    sums = [jnp.zeros((64, 128), F32), jnp.zeros((64, 128), F32)]
    for m in range(4):
        rows = [x_ref[3 * (4 * p + m) : 3 * (4 * p + m) + 2] for p in range(16)]
        rows = jnp.concatenate(rows, axis=0).reshape(64, 128)
        c = x_ref[3 * m + 2]
        for p in range(1, 16):
            c = c + x_ref[3 * (4 * p + m) + 2]
        sums = [sums[j] + rows * c[j : j + 1, :] for j in range(2)]
    total = jnp.sum(jnp.concatenate(sums, axis=0).T, axis=0, keepdims=True)
    out_ref[0:1, :] = total[:, 0:64]
    out_ref[1:2, :] = total[:, 64:128]


def finish(parts):
    return pl.pallas_call(
        finish_kernel,
        out_shape=jax.ShapeDtypeStruct((2, 64), F32),
        in_specs=[VMEM] * 1,
        out_specs=VMEM,
        compiler_params=PARAMS,
        name="finish",
    )(parts)


def shards(test_basis, deim_basis, trial_basis, jacobian, neighbours, counts, sample_inverse):
    jac, nbr, count = jacobian.transpose(2, 1, 0), neighbours.T, counts.reshape(1, 1)
    g_part, own = prepare(test_basis.swapaxes(0, 1), deim_basis.swapaxes(0, 1), jac, nbr, count)
    groups, group = lax.axis_size(ROWS), lax.axis_size(GROUP)
    across = [(i - 1, i) for i in range(group, groups, group)]
    across += [(target, source) for source, target in across]
    g_group = lax.all_to_all(g_part, GROUP, 0, 0, tiled=True)
    trial = trial_basis.swapaxes(0, 1)
    table, mine, upper, rest = own_part(own, trial, sample_inverse)
    edge = lax.ppermute(table, ROWS, across)
    sent = sample(g_group, nbr, edge, mine, trial)
    parts = lax.all_to_all(sent, "zh", 0, 0, tiled=True)
    pieces = lax.all_to_all(fold(parts, upper, rest), CUBE, 0, 0, tiled=True)
    return finish(pieces).T


def solution(mesh):
    split = Mesh(mesh.devices.reshape(8, 2, 4, 2, 4), ("zh", "zl", "x", "c", "y"))
    placed = (
        P(ROWS, None, None),
        P(ROWS, None, "y"),
        P(ROWS, None, None),
        P(ROWS, None, None),
        P(ROWS, None),
        P(ROWS),
        P("y", None),
    )
    return jax.shard_map(
        shards, mesh=split, in_specs=placed, out_specs=P("y", ROWS), check_vma=False
    )
```

```python
import jax
import jax.numpy as jnp
from jax import lax
from jax.experimental import pallas as pl
from jax.experimental.pallas import tpu as pltpu
from jax.sharding import Mesh
from jax.sharding import PartitionSpec as P

ROWS = ("zh", "zl", "x", "c")
GROUP = ("zl", "x", "c")
CUBE = ("zl", "x", "c", "y")
F32 = jnp.float32
BF16 = jnp.bfloat16
NC, NB = 5, 7
NBR, CNT = 40, 47
LOW_CNT, OWN_CNT, RANK, G_EXP, B_EXP, GROUP_CNT = 96, 97, 98, 99, 100, 112
TOP = 32000.0


VMEM = pl.BlockSpec(memory_space=pltpu.VMEM)
HBM = pl.BlockSpec(memory_space=pltpu.HBM)
PARAMS = pltpu.CompilerParams(vmem_limit_bytes=12 * 1024 * 1024)


def lanes(shape):
    return lax.broadcasted_iota(jnp.int32, shape, len(shape) - 1)


def exponent(x):
    top = jnp.max(jnp.abs(x), axis=(0, 1), keepdims=True)
    return jnp.floor(-jnp.log2(jnp.maximum(top, 1e-30)))


def coded(x, exp):
    code = jnp.floor(jnp.sqrt(jnp.sqrt(jnp.abs(x * jnp.exp2(exp)))) * TOP + 0.5)
    return jnp.where(x < 0.0, -code, code)


def decoded(code):
    root = code * (1.0 / TOP)
    square = root * root
    return square * square * jnp.where(code < 0.0, -1.0, 1.0)


def to_i16(x):
    return x.astype(jnp.int32).astype(jnp.int16)


def from_i16(x):
    return x.astype(jnp.int32).astype(F32)


def table_of(jac_ref, nbr_ref, count):
    blank = jnp.zeros((1, 16), F32)
    rows = []
    for j in range(NC):
        rows += [jac_ref[j], blank]
    rows += [nbr_ref[...].astype(F32), jnp.broadcast_to(count, (1, 16))]
    table = jnp.concatenate(rows + [jnp.zeros((80, 16), F32)], axis=0)
    table = jnp.concatenate([table, jnp.zeros((128, 112), F32)], axis=1)
    return table.T[0:16, :]


def prepare_kernel(
    v_hbm,
    d_hbm,
    jac_hbm,
    nbr_hbm,
    count_hbm,
    g_ref,
    table_ref,
    v_ref,
    d_ref,
    jac_ref,
    nbr_ref,
    count_ref,
    sems,
):
    small = [
        pltpu.make_async_copy(jac_hbm, jac_ref, sems.at[2 * NC]),
        pltpu.make_async_copy(nbr_hbm, nbr_ref, sems.at[2 * NC + 1]),
        pltpu.make_async_copy(count_hbm, count_ref, sems.at[2 * NC + 2]),
    ]
    v_copies = [
        pltpu.make_async_copy(v_hbm.at[j], v_ref.at[j], sems.at[j]) for j in range(NC)
    ]
    d_copies = [
        pltpu.make_async_copy(d_hbm.at[j], d_ref.at[j], sems.at[NC + j]) for j in range(NC)
    ]
    for copy in small:
        copy.start()
    for j in range(NC):
        v_copies[j].start()
        d_copies[j].start()
    for copy in small:
        copy.wait()
    count = count_ref[0, 0].astype(F32)
    table = table_of(jac_ref, nbr_ref, count)
    table_ref[...] = table
    packed = table[0:8, :] + pltpu.roll(table[8:16, :], 64, 1)
    packed = packed + jnp.where(lanes((8, 128)) >= GROUP_CNT, count, 0.0)
    packed = packed.reshape(4, 2, 128)
    acc = jnp.zeros((128, 256), F32)
    for j in range(NC):
        v_copies[j].wait()
        d_copies[j].wait()
        acc = acc + lax.dot_general(
            d_ref[j], v_ref[j], (((0,), (0,)), ((), ())), preferred_element_type=F32
        )
    pairs = acc.T.reshape(128, 2, 128)
    for p in range(16):
        for m in range(4):
            at = 32 * m + 2 * p
            g_ref[12 * p + 2 * m : 12 * p + 2 * m + 2] = pairs[at : at + 2]
        g_ref[12 * p + 8 : 12 * p + 12] = packed


def prepare(test, deim, jac, nbr, counts):
    return pl.pallas_call(
        prepare_kernel,
        in_specs=[HBM, HBM, HBM, HBM, HBM],
        out_specs=[VMEM, VMEM],
        out_shape=[
            jax.ShapeDtypeStruct((192, 2, 128), F32),
            jax.ShapeDtypeStruct((16, 128), F32),
        ],
        scratch_shapes=[
            pltpu.VMEM(test.shape, BF16),
            pltpu.VMEM(deim.shape, BF16),
            pltpu.VMEM((NC, NB, 16), F32),
            pltpu.VMEM((NB, 16), jnp.int32),
            pltpu.SMEM((1, 1), jnp.int32),
            pltpu.SemaphoreType.DMA((2 * NC + 3,)),
        ],
        name="prepare",
    )(test, deim, jac, nbr, counts)


def halves(x):
    upper = x.astype(BF16)
    return upper, (x - upper.astype(F32)).astype(BF16)


def alive(rows):
    slot = lax.broadcasted_iota(jnp.int32, (16, 128), 0).astype(F32)
    dead = (lanes((16, 128)) < NBR) & (slot >= rows[:, CNT : CNT + 1])
    return jnp.where(dead, 0.0, rows)


def weights(table, cell, j):
    weight = jnp.zeros((16, 128), F32)
    for n in range(NB):
        hit = cell == table[:, NBR + n : NBR + n + 1]
        weight = weight + jnp.where(hit, table[:, 8 * j + n : 8 * j + n + 1], 0.0)
    return weight


def sample_kernel(x_ref, nbr_ref, edge_ref, u_ref, out_ref):
    rank = jnp.floor(nbr_ref[0:1, 0:1].astype(F32) * (1.0 / 512.0))
    place = rank - 16.0 * jnp.floor(rank * 0.0625)
    lane = lanes((1, 128))
    total = jnp.zeros((8, 2, 128), F32)
    blank = jnp.zeros((4, 2, 128), F32)
    near = [blank, blank, blank]
    extra = jnp.zeros((1, 128), F32)
    for p in range(16):
        total = total + x_ref[12 * p : 12 * p + 8]
        packed = x_ref[12 * p + 8 : 12 * p + 12]
        near = [
            near[k] + jnp.where((place == p + 1 - k)[None], packed, 0.0) for k in range(3)
        ]
        extra = extra + jnp.where(lane == GROUP_CNT + p, packed[0, 0:1, :], 0.0)
    total = total.reshape(16, 128)
    tables = []
    for k, edge in ((0, 0.0), (1, None), (2, 15.0)):
        rows = near[k].reshape(8, 128)
        rows = jnp.concatenate([rows, pltpu.roll(rows, 64, 1)], axis=0)
        if edge is not None:
            rows = jnp.where(place == edge, edge_ref[...], rows)
        if k < 2:
            extra = extra + jnp.where(lane == LOW_CNT + k, rows[0:1, CNT : CNT + 1], 0.0)
        tables.append(alive(rows))
    cell = lanes((16, 128)).astype(F32) + rank * 512.0
    zero = jnp.zeros((16, 384), F32)
    sums = jnp.zeros((96, 256), F32)
    for j in range(NC):
        own = [weights(tables[1], cell + 128.0 * part, j) for part in range(4)]
        rows = [
            jnp.concatenate([weights(tables[0], cell, j), zero], axis=1),
            jnp.concatenate(own, axis=1),
            jnp.concatenate([zero, weights(tables[2], cell + 384.0, j)], axis=1),
        ]
        pieces = halves(jnp.concatenate(rows, axis=0))
        sums = sums + jnp.dot(
            jnp.concatenate(pieces, axis=0), u_ref[j], preferred_element_type=F32
        )
    rows = sums[0:48, :] + sums[48:96, :]
    b_exp, g_exp = exponent(rows), exponent(total)
    rows = jnp.concatenate([coded(rows, b_exp), jnp.zeros((80, 256), F32)], axis=0)
    extra = extra + jnp.where(lane == RANK, rank, 0.0)
    extra = extra + jnp.where(lane == B_EXP, b_exp, 0.0) + jnp.where(lane == G_EXP, g_exp, 0.0)
    cols = rows.T
    code = coded(total, g_exp)
    for z in range(8):
        left = cols[32 * z : 32 * z + 16, :]
        right = pltpu.roll(cols[32 * z + 16 : 32 * z + 32, :], 48, 1)
        out_ref[z] = to_i16(jnp.concatenate([code, left + right + extra], axis=0))


def sample(g_parts, nbr, edge, trial):
    return pl.pallas_call(
        sample_kernel,
        out_shape=jax.ShapeDtypeStruct((8, 32, 128), jnp.int16),
        in_specs=[VMEM] * 4,
        out_specs=VMEM,
        compiler_params=PARAMS,
        name="sample",
    )(g_parts, nbr, edge, trial)


def fold_kernel(x_ref, s_ref, out_ref):
    s_upper, s_rest = halves(s_ref[...])
    blocks = [from_i16(x_ref[z]) for z in range(8)]
    info = jnp.concatenate([block[16:17, :] for block in blocks], axis=0)
    lane = lanes((8, 128))

    def column(k):
        return jnp.sum(jnp.where(lane == k, info, 0.0), axis=1, keepdims=True)

    g_scale = jnp.exp2(-column(G_EXP))
    b_scale = jnp.exp2(-column(B_EXP))
    total = jnp.zeros((16, 128), F32)
    for z in range(8):
        total = total + decoded(blocks[z][0:16, :]) * g_scale[z : z + 1, :]
    rank = column(RANK)
    place = rank - 16.0 * jnp.floor(rank * 0.0625)
    is_count = (lane >= GROUP_CNT) & (lane < GROUP_CNT + 16)
    counts = jnp.where(is_count, info, 0.0)
    before = lax.broadcasted_iota(jnp.int32, (8, 8), 1) < lax.broadcasted_iota(
        jnp.int32, (8, 8), 0
    )
    lower = jnp.dot(before.astype(F32), counts, preferred_element_type=F32)
    ahead = (lane - GROUP_CNT).astype(F32) < place
    lower = lower + jnp.where(ahead, counts, 0.0)
    offset = jnp.sum(lower, axis=1, keepdims=True)
    shift = jnp.where(lane < 16, -column(LOW_CNT), jnp.where(lane < 32, 0.0, column(OWN_CNT)))
    ids = jnp.where(lane < 48, offset + shift + (lane % 16).astype(F32), -1.0)
    at = lanes((1, 128))
    mode = lax.broadcasted_iota(jnp.int32, (512, 128), 0).astype(F32)
    sampled = jnp.zeros((64, 512), F32)
    for z in range(0, 8, 2):
        here, there = (
            decoded(blocks[k][16:32, :]) * b_scale[k : k + 1, :] for k in (z, z + 1)
        )
        first = jnp.where(at < 48, here, jnp.where(at < 96, pltpu.roll(there, 48, 1), 0.0))
        second = jnp.where(at < 48, pltpu.roll(here, 80, 1), jnp.where(at < 96, there, 0.0))
        row = jnp.where(at < 48, ids[z : z + 1, :], pltpu.roll(ids[z + 1 : z + 2, :], 48, 1))
        hot = jnp.where(mode == row, 1.0, 0.0).astype(BF16)
        pieces = halves(jnp.concatenate([first, second], axis=0))
        sampled = sampled + lax.dot_general(
            jnp.concatenate(pieces, axis=0),
            hot,
            (((1,), (1,)), ((), ())),
            preferred_element_type=F32,
        )
    sampled = sampled[0:32, :] + sampled[32:64, :]
    upper, rest = halves(sampled)
    c = lax.dot_general(
        jnp.concatenate([upper, rest], axis=0),
        s_upper,
        (((1,), (1,)), ((), ())),
        preferred_element_type=F32,
    )
    c = (c[0:32, :] + c[32:64, :]) + lax.dot_general(
        upper, s_rest, (((1,), (1,)), ((), ())), preferred_element_type=F32
    )
    g_pairs = total.reshape(8, 2, 128)
    c_pairs = c.reshape(16, 2, 128)
    for p in range(16):
        for m in range(4):
            at = 3 * (4 * p + m)
            out_ref[at : at + 2] = g_pairs[2 * m : 2 * m + 2]
            out_ref[at + 2] = c_pairs[p]


def fold(parts, inverse):
    return pl.pallas_call(
        fold_kernel,
        out_shape=jax.ShapeDtypeStruct((192, 2, 128), F32),
        in_specs=[VMEM] * 2,
        out_specs=VMEM,
        compiler_params=PARAMS,
        name="fold",
    )(parts, inverse)


def finish_kernel(x_ref, out_ref):
    sums = [jnp.zeros((64, 128), F32), jnp.zeros((64, 128), F32)]
    for m in range(4):
        rows = [x_ref[3 * (4 * p + m) : 3 * (4 * p + m) + 2] for p in range(16)]
        rows = jnp.concatenate(rows, axis=0).reshape(64, 128)
        c = x_ref[3 * m + 2]
        for p in range(1, 16):
            c = c + x_ref[3 * (4 * p + m) + 2]
        sums = [sums[j] + rows * c[j : j + 1, :] for j in range(2)]
    total = jnp.sum(jnp.concatenate(sums, axis=0).T, axis=0, keepdims=True)
    out_ref[0:1, :] = total[:, 0:64]
    out_ref[1:2, :] = total[:, 64:128]


def finish(parts):
    return pl.pallas_call(
        finish_kernel,
        out_shape=jax.ShapeDtypeStruct((2, 64), F32),
        in_specs=[VMEM] * 1,
        out_specs=VMEM,
        compiler_params=PARAMS,
        name="finish",
    )(parts)


def shards(test_basis, deim_basis, trial_basis, jacobian, neighbours, counts, sample_inverse):
    jac, nbr, count = jacobian.transpose(2, 1, 0), neighbours.T, counts.reshape(1, 1)
    g_part, own = prepare(test_basis.swapaxes(0, 1), deim_basis.swapaxes(0, 1), jac, nbr, count)
    groups, group = lax.axis_size(ROWS), lax.axis_size(GROUP)
    across = [(i - 1, i) for i in range(group, groups, group)]
    across += [(target, source) for source, target in across]
    edge = lax.ppermute(own, ROWS, across)
    g_group = lax.all_to_all(g_part, GROUP, 0, 0, tiled=True)
    sent = sample(g_group, nbr, edge, trial_basis.swapaxes(0, 1))
    parts = lax.all_to_all(sent, "zh", 0, 0, tiled=True)
    pieces = lax.all_to_all(fold(parts, sample_inverse), CUBE, 0, 0, tiled=True)
    return finish(pieces).T


def solution(mesh):
    split = Mesh(mesh.devices.reshape(8, 2, 4, 2, 4), ("zh", "zl", "x", "c", "y"))
    placed = (
        P(ROWS, None, None),
        P(ROWS, None, "y"),
        P(ROWS, None, None),
        P(ROWS, None, None),
        P(ROWS, None),
        P(ROWS),
        P("y", None),
    )
    return jax.shard_map(
        shards, mesh=split, in_specs=placed, out_specs=P("y", ROWS), check_vma=False
    )
```

```python
import jax
import jax.numpy as jnp
from jax import lax
from jax.experimental import pallas as pl
from jax.experimental.pallas import tpu as pltpu
from jax.sharding import Mesh
from jax.sharding import PartitionSpec as P

ROWS = ("zh", "zl", "x", "c")
GROUP = ("zl", "x", "c")
CUBE = ("zl", "x", "c", "y")
F32 = jnp.float32
BF16 = jnp.bfloat16
NC, NB = 5, 7
NBR, CNT = 40, 47
LOW_CNT, OWN_CNT, RANK, G_EXP, B_EXP, GROUP_CNT = 96, 97, 98, 99, 100, 112
TOP = 32000.0


VMEM = pl.BlockSpec(memory_space=pltpu.VMEM)
HBM = pl.BlockSpec(memory_space=pltpu.HBM)
PARAMS = pltpu.CompilerParams(vmem_limit_bytes=12 * 1024 * 1024)


def lanes(shape):
    return lax.broadcasted_iota(jnp.int32, shape, len(shape) - 1)


def exponent(x):
    top = jnp.max(jnp.abs(x), axis=(0, 1), keepdims=True)
    return jnp.floor(-jnp.log2(jnp.maximum(top, 1e-30)))


def coded(x, exp):
    code = jnp.floor(jnp.sqrt(jnp.sqrt(jnp.abs(x * jnp.exp2(exp)))) * TOP + 0.5)
    return jnp.where(x < 0.0, -code, code)


def decoded(code):
    root = code * (1.0 / TOP)
    square = root * root
    return square * square * jnp.where(code < 0.0, -1.0, 1.0)


def to_i16(x):
    return x.astype(jnp.int32).astype(jnp.int16)


def from_i16(x):
    return x.astype(jnp.int32).astype(F32)


def table_of(jac_ref, nbr_ref, count):
    blank = jnp.zeros((1, 16), F32)
    rows = []
    for j in range(NC):
        rows += [jac_ref[j], blank]
    rows += [nbr_ref[...].astype(F32), jnp.broadcast_to(count, (1, 16))]
    table = jnp.concatenate(rows + [jnp.zeros((80, 16), F32)], axis=0)
    table = jnp.concatenate([table, jnp.zeros((128, 112), F32)], axis=1)
    return table.T[0:16, :]


def prepare_kernel(
    v_hbm,
    d_hbm,
    jac_hbm,
    nbr_hbm,
    count_hbm,
    g_ref,
    table_ref,
    v_ref,
    d_ref,
    jac_ref,
    nbr_ref,
    count_ref,
    sems,
):
    small = [
        pltpu.make_async_copy(jac_hbm, jac_ref, sems.at[2 * NC]),
        pltpu.make_async_copy(nbr_hbm, nbr_ref, sems.at[2 * NC + 1]),
        pltpu.make_async_copy(count_hbm, count_ref, sems.at[2 * NC + 2]),
    ]
    v_copies = [
        pltpu.make_async_copy(v_hbm.at[j], v_ref.at[j], sems.at[j]) for j in range(NC)
    ]
    d_copies = [
        pltpu.make_async_copy(d_hbm.at[j], d_ref.at[j], sems.at[NC + j]) for j in range(NC)
    ]
    for copy in small:
        copy.start()
    for j in range(NC):
        v_copies[j].start()
        d_copies[j].start()
    for copy in small:
        copy.wait()
    count = count_ref[0, 0].astype(F32)
    table = table_of(jac_ref, nbr_ref, count)
    table_ref[...] = table
    packed = table[0:8, :] + pltpu.roll(table[8:16, :], 64, 1)
    packed = packed + jnp.where(lanes((8, 128)) >= GROUP_CNT, count, 0.0)
    packed = packed.reshape(4, 2, 128)
    acc = jnp.zeros((128, 256), F32)
    for j in range(NC):
        v_copies[j].wait()
        d_copies[j].wait()
        acc = acc + lax.dot_general(
            d_ref[j], v_ref[j], (((0,), (0,)), ((), ())), preferred_element_type=F32
        )
    pairs = acc.T.reshape(128, 2, 128)
    for p in range(16):
        for m in range(4):
            at = 32 * m + 2 * p
            g_ref[12 * p + 2 * m : 12 * p + 2 * m + 2] = pairs[at : at + 2]
        g_ref[12 * p + 8 : 12 * p + 12] = packed


def prepare(test, deim, jac, nbr, counts):
    return pl.pallas_call(
        prepare_kernel,
        in_specs=[HBM, HBM, HBM, HBM, HBM],
        out_specs=[VMEM, VMEM],
        out_shape=[
            jax.ShapeDtypeStruct((192, 2, 128), F32),
            jax.ShapeDtypeStruct((16, 128), F32),
        ],
        scratch_shapes=[
            pltpu.VMEM(test.shape, BF16),
            pltpu.VMEM(deim.shape, BF16),
            pltpu.VMEM((NC, NB, 16), F32),
            pltpu.VMEM((NB, 16), jnp.int32),
            pltpu.SMEM((1, 1), jnp.int32),
            pltpu.SemaphoreType.DMA((2 * NC + 3,)),
        ],
        name="prepare",
    )(test, deim, jac, nbr, counts)


def halves(x):
    upper = x.astype(BF16)
    return upper, (x - upper.astype(F32)).astype(BF16)


def alive(rows):
    slot = lax.broadcasted_iota(jnp.int32, (16, 128), 0).astype(F32)
    dead = (lanes((16, 128)) < NBR) & (slot >= rows[:, CNT : CNT + 1])
    return jnp.where(dead, 0.0, rows)


def weights(table, cell, j):
    weight = jnp.zeros((16, 128), F32)
    for n in range(NB):
        hit = cell == table[:, NBR + n : NBR + n + 1]
        weight = weight + jnp.where(hit, table[:, 8 * j + n : 8 * j + n + 1], 0.0)
    return weight


def own_kernel(jac_ref, nbr_ref, u_ref, s_ref, sums_ref, upper_ref, rest_ref):
    table = table_of(jac_ref, nbr_ref, 0.0)
    rank = jnp.floor(table[0:1, NBR : NBR + 1] * (1.0 / 512.0))
    cell = lanes((16, 128)).astype(F32) + rank * 512.0
    sums = jnp.zeros((32, 256), F32)
    for j in range(NC):
        parts = [weights(table, cell + 128.0 * part, j) for part in range(4)]
        pieces = halves(jnp.concatenate(parts, axis=1))
        sums = sums + jnp.dot(
            jnp.concatenate(pieces, axis=0), u_ref[j], preferred_element_type=F32
        )
    sums_ref[...] = sums[0:16, :] + sums[16:32, :]
    upper_ref[...], rest_ref[...] = halves(s_ref[...])


def own_part(jac, nbr, trial, inverse):
    return pl.pallas_call(
        own_kernel,
        out_shape=[
            jax.ShapeDtypeStruct((16, 256), F32),
            jax.ShapeDtypeStruct(inverse.shape, BF16),
            jax.ShapeDtypeStruct(inverse.shape, BF16),
        ],
        in_specs=[VMEM] * 4,
        out_specs=[VMEM] * 3,
        compiler_params=PARAMS,
        name="own_part",
    )(jac, nbr, trial, inverse)


def sample_kernel(x_ref, nbr_ref, edge_ref, own_ref, u_ref, out_ref):
    rank = jnp.floor(nbr_ref[0:1, 0:1].astype(F32) * (1.0 / 512.0))
    place = rank - 16.0 * jnp.floor(rank * 0.0625)
    lane = lanes((1, 128))
    total = jnp.zeros((8, 2, 128), F32)
    blank = jnp.zeros((4, 2, 128), F32)
    near = [blank, blank, blank]
    extra = jnp.zeros((1, 128), F32)
    for p in range(16):
        total = total + x_ref[12 * p : 12 * p + 8]
        packed = x_ref[12 * p + 8 : 12 * p + 12]
        near = [
            near[k] + jnp.where((place == p + 1 - k)[None], packed, 0.0) for k in range(3)
        ]
        extra = extra + jnp.where(lane == GROUP_CNT + p, packed[0, 0:1, :], 0.0)
    total = total.reshape(16, 128)
    tables = []
    for k, edge in ((0, 0.0), (1, None), (2, 15.0)):
        rows = near[k].reshape(8, 128)
        rows = jnp.concatenate([rows, pltpu.roll(rows, 64, 1)], axis=0)
        if edge is not None:
            rows = jnp.where(place == edge, edge_ref[...], rows)
        if k < 2:
            extra = extra + jnp.where(lane == LOW_CNT + k, rows[0:1, CNT : CNT + 1], 0.0)
        tables.append(rows)
    cell = lanes((16, 128)).astype(F32) + rank * 512.0
    low_table, high_table = alive(tables[0]), alive(tables[2])
    slot = lax.broadcasted_iota(jnp.int32, (16, 256), 0).astype(F32)
    own = jnp.where(slot < tables[1][:, CNT : CNT + 1], own_ref[...], 0.0)
    low = jnp.zeros((32, 256), F32)
    high = jnp.zeros((32, 256), F32)
    for j in range(NC):
        pieces = halves(weights(low_table, cell, j))
        low = low + jnp.dot(
            jnp.concatenate(pieces, axis=0), u_ref[j, 0:128, :], preferred_element_type=F32
        )
        pieces = halves(weights(high_table, cell + 384.0, j))
        high = high + jnp.dot(
            jnp.concatenate(pieces, axis=0), u_ref[j, 384:512, :], preferred_element_type=F32
        )
    rows = jnp.concatenate(
        [low[0:16, :] + low[16:32, :], own, high[0:16, :] + high[16:32, :]], axis=0
    )
    b_exp, g_exp = exponent(rows), exponent(total)
    rows = jnp.concatenate([coded(rows, b_exp), jnp.zeros((80, 256), F32)], axis=0)
    extra = extra + jnp.where(lane == RANK, rank, 0.0)
    extra = extra + jnp.where(lane == B_EXP, b_exp, 0.0) + jnp.where(lane == G_EXP, g_exp, 0.0)
    cols = rows.T
    code = coded(total, g_exp)
    for z in range(8):
        left = cols[32 * z : 32 * z + 16, :]
        right = pltpu.roll(cols[32 * z + 16 : 32 * z + 32, :], 48, 1)
        out_ref[z] = to_i16(jnp.concatenate([code, left + right + extra], axis=0))


def sample(g_parts, nbr, edge, own, trial):
    return pl.pallas_call(
        sample_kernel,
        out_shape=jax.ShapeDtypeStruct((8, 32, 128), jnp.int16),
        in_specs=[VMEM] * 5,
        out_specs=VMEM,
        compiler_params=PARAMS,
        name="sample",
    )(g_parts, nbr, edge, own, trial)


def fold_kernel(x_ref, upper_ref, rest_ref, out_ref):
    blocks = [from_i16(x_ref[z]) for z in range(8)]
    info = jnp.concatenate([block[16:17, :] for block in blocks], axis=0)
    lane = lanes((8, 128))

    def column(k):
        return jnp.sum(jnp.where(lane == k, info, 0.0), axis=1, keepdims=True)

    g_scale = jnp.exp2(-column(G_EXP))
    b_scale = jnp.exp2(-column(B_EXP))
    total = jnp.zeros((16, 128), F32)
    for z in range(8):
        total = total + decoded(blocks[z][0:16, :]) * g_scale[z : z + 1, :]
    rank = column(RANK)
    place = rank - 16.0 * jnp.floor(rank * 0.0625)
    is_count = (lane >= GROUP_CNT) & (lane < GROUP_CNT + 16)
    counts = jnp.where(is_count, info, 0.0)
    before = lax.broadcasted_iota(jnp.int32, (8, 8), 1) < lax.broadcasted_iota(
        jnp.int32, (8, 8), 0
    )
    lower = jnp.dot(before.astype(F32), counts, preferred_element_type=F32)
    ahead = (lane - GROUP_CNT).astype(F32) < place
    lower = lower + jnp.where(ahead, counts, 0.0)
    offset = jnp.sum(lower, axis=1, keepdims=True)
    shift = jnp.where(lane < 16, -column(LOW_CNT), jnp.where(lane < 32, 0.0, column(OWN_CNT)))
    ids = jnp.where(lane < 48, offset + shift + (lane % 16).astype(F32), -1.0)
    at = lanes((1, 128))
    mode = lax.broadcasted_iota(jnp.int32, (512, 128), 0).astype(F32)
    sampled = jnp.zeros((64, 512), F32)
    for z in range(0, 8, 2):
        here, there = (
            decoded(blocks[k][16:32, :]) * b_scale[k : k + 1, :] for k in (z, z + 1)
        )
        first = jnp.where(at < 48, here, jnp.where(at < 96, pltpu.roll(there, 48, 1), 0.0))
        second = jnp.where(at < 48, pltpu.roll(here, 80, 1), jnp.where(at < 96, there, 0.0))
        row = jnp.where(at < 48, ids[z : z + 1, :], pltpu.roll(ids[z + 1 : z + 2, :], 48, 1))
        hot = jnp.where(mode == row, 1.0, 0.0).astype(BF16)
        pieces = halves(jnp.concatenate([first, second], axis=0))
        sampled = sampled + lax.dot_general(
            jnp.concatenate(pieces, axis=0),
            hot,
            (((1,), (1,)), ((), ())),
            preferred_element_type=F32,
        )
    sampled = sampled[0:32, :] + sampled[32:64, :]
    upper, rest = halves(sampled)
    c = lax.dot_general(
        jnp.concatenate([upper, rest], axis=0),
        upper_ref[...],
        (((1,), (1,)), ((), ())),
        preferred_element_type=F32,
    )
    c = (c[0:32, :] + c[32:64, :]) + lax.dot_general(
        upper, rest_ref[...], (((1,), (1,)), ((), ())), preferred_element_type=F32
    )
    g_pairs = total.reshape(8, 2, 128)
    c_pairs = c.reshape(16, 2, 128)
    for p in range(16):
        for m in range(4):
            at = 3 * (4 * p + m)
            out_ref[at : at + 2] = g_pairs[2 * m : 2 * m + 2]
            out_ref[at + 2] = c_pairs[p]


def fold(parts, upper, rest):
    return pl.pallas_call(
        fold_kernel,
        out_shape=jax.ShapeDtypeStruct((192, 2, 128), F32),
        in_specs=[VMEM] * 3,
        out_specs=VMEM,
        compiler_params=PARAMS,
        name="fold",
    )(parts, upper, rest)


def finish_kernel(x_ref, out_ref):
    sums = [jnp.zeros((64, 128), F32), jnp.zeros((64, 128), F32)]
    for m in range(4):
        rows = [x_ref[3 * (4 * p + m) : 3 * (4 * p + m) + 2] for p in range(16)]
        rows = jnp.concatenate(rows, axis=0).reshape(64, 128)
        c = x_ref[3 * m + 2]
        for p in range(1, 16):
            c = c + x_ref[3 * (4 * p + m) + 2]
        sums = [sums[j] + rows * c[j : j + 1, :] for j in range(2)]
    total = jnp.sum(jnp.concatenate(sums, axis=0).T, axis=0, keepdims=True)
    out_ref[0:1, :] = total[:, 0:64]
    out_ref[1:2, :] = total[:, 64:128]


def finish(parts):
    return pl.pallas_call(
        finish_kernel,
        out_shape=jax.ShapeDtypeStruct((2, 64), F32),
        in_specs=[VMEM] * 1,
        out_specs=VMEM,
        compiler_params=PARAMS,
        name="finish",
    )(parts)


def shards(test_basis, deim_basis, trial_basis, jacobian, neighbours, counts, sample_inverse):
    jac, nbr, count = jacobian.transpose(2, 1, 0), neighbours.T, counts.reshape(1, 1)
    g_part, own = prepare(test_basis.swapaxes(0, 1), deim_basis.swapaxes(0, 1), jac, nbr, count)
    groups, group = lax.axis_size(ROWS), lax.axis_size(GROUP)
    across = [(i - 1, i) for i in range(group, groups, group)]
    across += [(target, source) for source, target in across]
    edge = lax.ppermute(own, ROWS, across)
    g_group = lax.all_to_all(g_part, GROUP, 0, 0, tiled=True)
    trial = trial_basis.swapaxes(0, 1)
    mine, upper, rest = own_part(jac, nbr, trial, sample_inverse)
    sent = sample(g_group, nbr, edge, mine, trial)
    parts = lax.all_to_all(sent, "zh", 0, 0, tiled=True)
    pieces = lax.all_to_all(fold(parts, upper, rest), CUBE, 0, 0, tiled=True)
    return finish(pieces).T


def solution(mesh):
    split = Mesh(mesh.devices.reshape(8, 2, 4, 2, 4), ("zh", "zl", "x", "c", "y"))
    placed = (
        P(ROWS, None, None),
        P(ROWS, None, "y"),
        P(ROWS, None, None),
        P(ROWS, None, None),
        P(ROWS, None),
        P(ROWS),
        P("y", None),
    )
    return jax.shard_map(
        shards, mesh=split, in_specs=placed, out_specs=P("y", ROWS), check_vma=False
    )
```

```python
import jax
import jax.numpy as jnp
from jax import lax
from jax.experimental import pallas as pl
from jax.experimental.pallas import tpu as pltpu
from jax.sharding import Mesh
from jax.sharding import PartitionSpec as P

ROWS = ("zh", "zl", "x", "c")
GROUP = ("zl", "x", "c")
CUBE = ("zl", "x", "c", "y")
F32 = jnp.float32
BF16 = jnp.bfloat16
NC, NB = 5, 7
NBR, CNT = 40, 47
LOW_CNT, OWN_CNT, RANK, G_EXP, B_EXP, GROUP_CNT = 96, 97, 98, 99, 100, 112
TOP = 32000.0


VMEM = pl.BlockSpec(memory_space=pltpu.VMEM)
HBM = pl.BlockSpec(memory_space=pltpu.HBM)
PARAMS = pltpu.CompilerParams(vmem_limit_bytes=12 * 1024 * 1024)


def lanes(shape):
    return lax.broadcasted_iota(jnp.int32, shape, len(shape) - 1)


def exponent(x):
    top = jnp.max(jnp.abs(x), axis=(0, 1), keepdims=True)
    return jnp.floor(-jnp.log2(jnp.maximum(top, 1e-37)))


def coded(x, exp):
    code = jnp.floor(jnp.sqrt(jnp.sqrt(jnp.abs(x * jnp.exp2(exp)))) * TOP + 0.5)
    return jnp.where(x < 0.0, -code, code)


def decoded(code):
    root = code * (1.0 / TOP)
    square = root * root
    return square * square * jnp.where(code < 0.0, -1.0, 1.0)


def to_i16(x):
    return x.astype(jnp.int32).astype(jnp.int16)


def from_i16(x):
    return x.astype(jnp.int32).astype(F32)


def table_of(jac_ref, nbr_ref, count):
    blank = jnp.zeros((1, 16), F32)
    rows = []
    for j in range(NC):
        rows += [jac_ref[j], blank]
    rows += [nbr_ref[...].astype(F32), jnp.broadcast_to(count, (1, 16))]
    table = jnp.concatenate(rows + [jnp.zeros((80, 16), F32)], axis=0)
    table = jnp.concatenate([table, jnp.zeros((128, 112), F32)], axis=1)
    return table.T[0:16, :]


def prepare_kernel(
    v_hbm,
    d_hbm,
    jac_hbm,
    nbr_hbm,
    count_hbm,
    g_ref,
    table_ref,
    v_ref,
    d_ref,
    jac_ref,
    nbr_ref,
    count_ref,
    sems,
):
    small = [
        pltpu.make_async_copy(jac_hbm, jac_ref, sems.at[2 * NC]),
        pltpu.make_async_copy(nbr_hbm, nbr_ref, sems.at[2 * NC + 1]),
        pltpu.make_async_copy(count_hbm, count_ref, sems.at[2 * NC + 2]),
    ]
    v_copies = [
        pltpu.make_async_copy(v_hbm.at[j], v_ref.at[j], sems.at[j]) for j in range(NC)
    ]
    d_copies = [
        pltpu.make_async_copy(d_hbm.at[j], d_ref.at[j], sems.at[NC + j]) for j in range(NC)
    ]
    for copy in small:
        copy.start()
    for j in range(NC):
        v_copies[j].start()
        d_copies[j].start()
    for copy in small:
        copy.wait()
    count = count_ref[0, 0].astype(F32)
    table = table_of(jac_ref, nbr_ref, count)
    table_ref[...] = table
    packed = table[0:8, :] + pltpu.roll(table[8:16, :], 64, 1)
    packed = packed + jnp.where(lanes((8, 128)) >= GROUP_CNT, count, 0.0)
    packed = packed.reshape(4, 2, 128)
    acc = jnp.zeros((128, 256), F32)
    for j in range(NC):
        v_copies[j].wait()
        d_copies[j].wait()
        acc = acc + lax.dot_general(
            d_ref[j], v_ref[j], (((0,), (0,)), ((), ())), preferred_element_type=F32
        )
    pairs = acc.T.reshape(128, 2, 128)
    for p in range(16):
        for m in range(4):
            at = 32 * m + 2 * p
            g_ref[12 * p + 2 * m : 12 * p + 2 * m + 2] = pairs[at : at + 2]
        g_ref[12 * p + 8 : 12 * p + 12] = packed


def prepare(test, deim, jac, nbr, counts):
    return pl.pallas_call(
        prepare_kernel,
        in_specs=[HBM, HBM, HBM, HBM, HBM],
        out_specs=[VMEM, VMEM],
        out_shape=[
            jax.ShapeDtypeStruct((192, 2, 128), F32),
            jax.ShapeDtypeStruct((16, 128), F32),
        ],
        scratch_shapes=[
            pltpu.VMEM(test.shape, BF16),
            pltpu.VMEM(deim.shape, BF16),
            pltpu.VMEM((NC, NB, 16), F32),
            pltpu.VMEM((NB, 16), jnp.int32),
            pltpu.SMEM((1, 1), jnp.int32),
            pltpu.SemaphoreType.DMA((2 * NC + 3,)),
        ],
        name="prepare",
    )(test, deim, jac, nbr, counts)


def halves(x):
    upper = x.astype(BF16)
    return upper, (x - upper.astype(F32)).astype(BF16)


def alive(rows):
    slot = lax.broadcasted_iota(jnp.int32, (16, 128), 0).astype(F32)
    dead = (lanes((16, 128)) < NBR) & (slot >= rows[:, CNT : CNT + 1])
    return jnp.where(dead, 0.0, rows)


def weights(table, cell, j):
    weight = jnp.zeros((16, 128), F32)
    for n in range(NB):
        hit = cell == table[:, NBR + n : NBR + n + 1]
        weight = weight + jnp.where(hit, table[:, 8 * j + n : 8 * j + n + 1], 0.0)
    return weight


def own_kernel(jac_ref, nbr_ref, u_ref, s_ref, sums_ref, upper_ref, rest_ref):
    table = table_of(jac_ref, nbr_ref, 0.0)
    rank = jnp.floor(table[0:1, NBR : NBR + 1] * (1.0 / 512.0))
    cell = lanes((16, 128)).astype(F32) + rank * 512.0
    sums = jnp.zeros((32, 256), F32)
    for j in range(NC):
        parts = [weights(table, cell + 128.0 * part, j) for part in range(4)]
        pieces = halves(jnp.concatenate(parts, axis=1))
        sums = sums + jnp.dot(
            jnp.concatenate(pieces, axis=0), u_ref[j], preferred_element_type=F32
        )
    sums_ref[...] = sums[0:16, :] + sums[16:32, :]
    upper_ref[...], rest_ref[...] = halves(s_ref[...])


def own_part(jac, nbr, trial, inverse):
    return pl.pallas_call(
        own_kernel,
        out_shape=[
            jax.ShapeDtypeStruct((16, 256), F32),
            jax.ShapeDtypeStruct(inverse.shape, BF16),
            jax.ShapeDtypeStruct(inverse.shape, BF16),
        ],
        in_specs=[VMEM] * 4,
        out_specs=[VMEM] * 3,
        compiler_params=PARAMS,
        name="own_part",
    )(jac, nbr, trial, inverse)


def sample_kernel(x_ref, nbr_ref, edge_ref, own_ref, u_ref, out_ref):
    rank = jnp.floor(nbr_ref[0:1, 0:1].astype(F32) * (1.0 / 512.0))
    place = rank - 16.0 * jnp.floor(rank * 0.0625)
    lane = lanes((1, 128))
    total = jnp.zeros((8, 2, 128), F32)
    blank = jnp.zeros((4, 2, 128), F32)
    near = [blank, blank, blank]
    extra = jnp.zeros((1, 128), F32)
    for p in range(16):
        total = total + x_ref[12 * p : 12 * p + 8]
        packed = x_ref[12 * p + 8 : 12 * p + 12]
        near = [
            near[k] + jnp.where((place == p + 1 - k)[None], packed, 0.0) for k in range(3)
        ]
        extra = extra + jnp.where(lane == GROUP_CNT + p, packed[0, 0:1, :], 0.0)
    total = total.reshape(16, 128)
    tables = []
    for k, edge in ((0, 0.0), (1, None), (2, 15.0)):
        rows = near[k].reshape(8, 128)
        rows = jnp.concatenate([rows, pltpu.roll(rows, 64, 1)], axis=0)
        if edge is not None:
            rows = jnp.where(place == edge, edge_ref[...], rows)
        if k < 2:
            extra = extra + jnp.where(lane == LOW_CNT + k, rows[0:1, CNT : CNT + 1], 0.0)
        tables.append(rows)
    cell = lanes((16, 128)).astype(F32) + rank * 512.0
    low_table, high_table = alive(tables[0]), alive(tables[2])
    slot = lax.broadcasted_iota(jnp.int32, (16, 256), 0).astype(F32)
    own = jnp.where(slot < tables[1][:, CNT : CNT + 1], own_ref[...], 0.0)
    low = jnp.zeros((32, 256), F32)
    high = jnp.zeros((32, 256), F32)
    for j in range(NC):
        pieces = halves(weights(low_table, cell, j))
        low = low + jnp.dot(
            jnp.concatenate(pieces, axis=0), u_ref[j, 0:128, :], preferred_element_type=F32
        )
        pieces = halves(weights(high_table, cell + 384.0, j))
        high = high + jnp.dot(
            jnp.concatenate(pieces, axis=0), u_ref[j, 384:512, :], preferred_element_type=F32
        )
    rows = jnp.concatenate(
        [low[0:16, :] + low[16:32, :], own, high[0:16, :] + high[16:32, :]], axis=0
    )
    b_exp, g_exp = exponent(rows), exponent(total)
    rows = jnp.concatenate([coded(rows, b_exp), jnp.zeros((80, 256), F32)], axis=0)
    extra = extra + jnp.where(lane == RANK, rank, 0.0)
    extra = extra + jnp.where(lane == B_EXP, b_exp, 0.0) + jnp.where(lane == G_EXP, g_exp, 0.0)
    cols = rows.T
    code = coded(total, g_exp)
    for z in range(8):
        left = cols[32 * z : 32 * z + 16, :]
        right = pltpu.roll(cols[32 * z + 16 : 32 * z + 32, :], 48, 1)
        out_ref[z] = to_i16(jnp.concatenate([code, left + right + extra], axis=0))


def sample(g_parts, nbr, edge, own, trial):
    return pl.pallas_call(
        sample_kernel,
        out_shape=jax.ShapeDtypeStruct((8, 32, 128), jnp.int16),
        in_specs=[VMEM] * 5,
        out_specs=VMEM,
        compiler_params=PARAMS,
        name="sample",
    )(g_parts, nbr, edge, own, trial)


def fold_kernel(x_ref, upper_ref, rest_ref, out_ref):
    blocks = [from_i16(x_ref[z]) for z in range(8)]
    info = jnp.concatenate([block[16:17, :] for block in blocks], axis=0)
    lane = lanes((8, 128))

    def column(k):
        return jnp.sum(jnp.where(lane == k, info, 0.0), axis=1, keepdims=True)

    g_scale = jnp.exp2(-column(G_EXP))
    b_scale = jnp.exp2(-column(B_EXP))
    total = jnp.zeros((16, 128), F32)
    for z in range(8):
        total = total + decoded(blocks[z][0:16, :]) * g_scale[z : z + 1, :]
    rank = column(RANK)
    place = rank - 16.0 * jnp.floor(rank * 0.0625)
    is_count = (lane >= GROUP_CNT) & (lane < GROUP_CNT + 16)
    counts = jnp.where(is_count, info, 0.0)
    before = lax.broadcasted_iota(jnp.int32, (8, 8), 1) < lax.broadcasted_iota(
        jnp.int32, (8, 8), 0
    )
    lower = jnp.dot(before.astype(F32), counts, preferred_element_type=F32)
    ahead = (lane - GROUP_CNT).astype(F32) < place
    lower = lower + jnp.where(ahead, counts, 0.0)
    offset = jnp.sum(lower, axis=1, keepdims=True)
    shift = jnp.where(lane < 16, -column(LOW_CNT), jnp.where(lane < 32, 0.0, column(OWN_CNT)))
    ids = jnp.where(lane < 48, offset + shift + (lane % 16).astype(F32), -1.0)
    at = lanes((1, 128))
    mode = lax.broadcasted_iota(jnp.int32, (512, 128), 0).astype(F32)
    sampled = jnp.zeros((64, 512), F32)
    for z in range(0, 8, 2):
        here, there = (
            decoded(blocks[k][16:32, :]) * b_scale[k : k + 1, :] for k in (z, z + 1)
        )
        first = jnp.where(at < 48, here, jnp.where(at < 96, pltpu.roll(there, 48, 1), 0.0))
        second = jnp.where(at < 48, pltpu.roll(here, 80, 1), jnp.where(at < 96, there, 0.0))
        row = jnp.where(at < 48, ids[z : z + 1, :], pltpu.roll(ids[z + 1 : z + 2, :], 48, 1))
        hot = jnp.where(mode == row, 1.0, 0.0).astype(BF16)
        pieces = halves(jnp.concatenate([first, second], axis=0))
        sampled = sampled + lax.dot_general(
            jnp.concatenate(pieces, axis=0),
            hot,
            (((1,), (1,)), ((), ())),
            preferred_element_type=F32,
        )
    sampled = sampled[0:32, :] + sampled[32:64, :]
    upper, rest = halves(sampled)
    c = lax.dot_general(
        jnp.concatenate([upper, rest], axis=0),
        upper_ref[...],
        (((1,), (1,)), ((), ())),
        preferred_element_type=F32,
    )
    c = (c[0:32, :] + c[32:64, :]) + lax.dot_general(
        upper, rest_ref[...], (((1,), (1,)), ((), ())), preferred_element_type=F32
    )
    g_pairs = total.reshape(8, 2, 128)
    c_pairs = c.reshape(16, 2, 128)
    for p in range(16):
        for m in range(4):
            at = 3 * (4 * p + m)
            out_ref[at : at + 2] = g_pairs[2 * m : 2 * m + 2]
            out_ref[at + 2] = c_pairs[p]


def fold(parts, upper, rest):
    return pl.pallas_call(
        fold_kernel,
        out_shape=jax.ShapeDtypeStruct((192, 2, 128), F32),
        in_specs=[VMEM] * 3,
        out_specs=VMEM,
        compiler_params=PARAMS,
        name="fold",
    )(parts, upper, rest)


def finish_kernel(x_ref, out_ref):
    sums = [jnp.zeros((64, 128), F32), jnp.zeros((64, 128), F32)]
    for m in range(4):
        rows = [x_ref[3 * (4 * p + m) : 3 * (4 * p + m) + 2] for p in range(16)]
        rows = jnp.concatenate(rows, axis=0).reshape(64, 128)
        c = x_ref[3 * m + 2]
        for p in range(1, 16):
            c = c + x_ref[3 * (4 * p + m) + 2]
        sums = [sums[j] + rows * c[j : j + 1, :] for j in range(2)]
    total = jnp.sum(jnp.concatenate(sums, axis=0).T, axis=0, keepdims=True)
    out_ref[0:1, :] = total[:, 0:64]
    out_ref[1:2, :] = total[:, 64:128]


def finish(parts):
    return pl.pallas_call(
        finish_kernel,
        out_shape=jax.ShapeDtypeStruct((2, 64), F32),
        in_specs=[VMEM] * 1,
        out_specs=VMEM,
        compiler_params=PARAMS,
        name="finish",
    )(parts)


def shards(test_basis, deim_basis, trial_basis, jacobian, neighbours, counts, sample_inverse):
    jac, nbr, count = jacobian.transpose(2, 1, 0), neighbours.T, counts.reshape(1, 1)
    g_part, own = prepare(test_basis.swapaxes(0, 1), deim_basis.swapaxes(0, 1), jac, nbr, count)
    groups, group = lax.axis_size(ROWS), lax.axis_size(GROUP)
    across = [(i - 1, i) for i in range(group, groups, group)]
    across += [(target, source) for source, target in across]
    edge = lax.ppermute(own, ROWS, across)
    g_group = lax.all_to_all(g_part, GROUP, 0, 0, tiled=True)
    trial = trial_basis.swapaxes(0, 1)
    mine, upper, rest = own_part(jac, nbr, trial, sample_inverse)
    sent = sample(g_group, nbr, edge, mine, trial)
    parts = lax.all_to_all(sent, "zh", 0, 0, tiled=True)
    pieces = lax.all_to_all(fold(parts, upper, rest), CUBE, 0, 0, tiled=True)
    return finish(pieces).T


def solution(mesh):
    split = Mesh(mesh.devices.reshape(8, 2, 4, 2, 4), ("zh", "zl", "x", "c", "y"))
    placed = (
        P(ROWS, None, None),
        P(ROWS, None, "y"),
        P(ROWS, None, None),
        P(ROWS, None, None),
        P(ROWS, None),
        P(ROWS),
        P("y", None),
    )
    return jax.shard_map(
        shards, mesh=split, in_specs=placed, out_specs=P("y", ROWS), check_vma=False
    )
```

```python
import jax
import jax.numpy as jnp
from jax import lax
from jax.experimental import pallas as pl
from jax.experimental.pallas import tpu as pltpu
from jax.sharding import Mesh
from jax.sharding import PartitionSpec as P

ROWS = ("zh", "zl", "x", "c")
GROUP = ("zl", "x", "c")
CUBE = ("zl", "x", "c", "y")
F32 = jnp.float32
BF16 = jnp.bfloat16
NC, NB = 5, 7
NBR, CNT = 40, 47
LOW_CNT, OWN_CNT, RANK, G_EXP, B_EXP, GROUP_CNT = 96, 97, 98, 99, 100, 112
TOP = 32000.0


VMEM = pl.BlockSpec(memory_space=pltpu.VMEM)
HBM = pl.BlockSpec(memory_space=pltpu.HBM)
PARAMS = pltpu.CompilerParams(vmem_limit_bytes=12 * 1024 * 1024)


def lanes(shape):
    return lax.broadcasted_iota(jnp.int32, shape, len(shape) - 1)


def exponent(x):
    top = jnp.max(jnp.abs(x), axis=(0, 1), keepdims=True)
    return jnp.floor(-jnp.log2(jnp.maximum(top, 1e-30)))


def coded(x, exp):
    code = jnp.floor(jnp.sqrt(jnp.sqrt(jnp.abs(x * jnp.exp2(exp)))) * TOP + 0.5)
    return jnp.where(x < 0.0, -code, code)


def decoded(code):
    root = code * (1.0 / TOP)
    square = root * root
    return square * square * jnp.where(code < 0.0, -1.0, 1.0)


def to_i16(x):
    return x.astype(jnp.int32).astype(jnp.int16)


def from_i16(x):
    return x.astype(jnp.int32).astype(F32)


def table_of(jac_ref, nbr_ref, count):
    blank = jnp.zeros((1, 16), F32)
    rows = []
    for j in range(NC):
        rows += [jac_ref[j], blank]
    rows += [nbr_ref[...].astype(F32), jnp.broadcast_to(count, (1, 16))]
    table = jnp.concatenate(rows + [jnp.zeros((80, 16), F32)], axis=0)
    table = jnp.concatenate([table, jnp.zeros((128, 112), F32)], axis=1)
    return table.T[0:16, :]


def prepare_kernel(
    v_hbm,
    d_hbm,
    jac_hbm,
    nbr_hbm,
    count_hbm,
    g_ref,
    table_ref,
    v_ref,
    d_ref,
    jac_ref,
    nbr_ref,
    count_ref,
    sems,
):
    small = [
        pltpu.make_async_copy(jac_hbm, jac_ref, sems.at[2 * NC]),
        pltpu.make_async_copy(nbr_hbm, nbr_ref, sems.at[2 * NC + 1]),
        pltpu.make_async_copy(count_hbm, count_ref, sems.at[2 * NC + 2]),
    ]
    v_copies = [
        pltpu.make_async_copy(v_hbm.at[j], v_ref.at[j], sems.at[j]) for j in range(NC)
    ]
    d_copies = [
        pltpu.make_async_copy(d_hbm.at[j], d_ref.at[j], sems.at[NC + j]) for j in range(NC)
    ]
    for copy in small:
        copy.start()
    for j in range(NC):
        v_copies[j].start()
        d_copies[j].start()
    for copy in small:
        copy.wait()
    count = count_ref[0, 0].astype(F32)
    table = table_of(jac_ref, nbr_ref, count)
    packed = table[0:8, :] + pltpu.roll(table[8:16, :], 64, 1)
    packed = packed + jnp.where(lanes((8, 128)) >= GROUP_CNT, count, 0.0)
    table_ref[...] = packed
    packed = packed.reshape(4, 2, 128)
    acc = jnp.zeros((128, 256), F32)
    for j in range(NC):
        v_copies[j].wait()
        d_copies[j].wait()
        acc = acc + lax.dot_general(
            d_ref[j], v_ref[j], (((0,), (0,)), ((), ())), preferred_element_type=F32
        )
    pairs = acc.T.reshape(128, 2, 128)
    for p in range(16):
        for m in range(4):
            at = 32 * m + 2 * p
            g_ref[12 * p + 2 * m : 12 * p + 2 * m + 2] = pairs[at : at + 2]
        g_ref[12 * p + 8 : 12 * p + 12] = packed


def prepare(test, deim, jac, nbr, counts):
    return pl.pallas_call(
        prepare_kernel,
        in_specs=[HBM, HBM, HBM, HBM, HBM],
        out_specs=[VMEM, VMEM],
        out_shape=[
            jax.ShapeDtypeStruct((192, 2, 128), F32),
            jax.ShapeDtypeStruct((8, 128), F32),
        ],
        scratch_shapes=[
            pltpu.VMEM(test.shape, BF16),
            pltpu.VMEM(deim.shape, BF16),
            pltpu.VMEM((NC, NB, 16), F32),
            pltpu.VMEM((NB, 16), jnp.int32),
            pltpu.SMEM((1, 1), jnp.int32),
            pltpu.SemaphoreType.DMA((2 * NC + 3,)),
        ],
        name="prepare",
    )(test, deim, jac, nbr, counts)


def halves(x):
    upper = x.astype(BF16)
    return upper, (x - upper.astype(F32)).astype(BF16)


def alive(rows):
    slot = lax.broadcasted_iota(jnp.int32, (16, 128), 0).astype(F32)
    dead = (lanes((16, 128)) < NBR) & (slot >= rows[:, CNT : CNT + 1])
    return jnp.where(dead, 0.0, rows)


def weights(table, cell, j):
    weight = jnp.zeros((16, 128), F32)
    for n in range(NB):
        hit = cell == table[:, NBR + n : NBR + n + 1]
        weight = weight + jnp.where(hit, table[:, 8 * j + n : 8 * j + n + 1], 0.0)
    return weight


def own_kernel(jac_ref, nbr_ref, u_ref, s_ref, sums_ref, upper_ref, rest_ref):
    table = table_of(jac_ref, nbr_ref, 0.0)
    rank = jnp.floor(table[0:1, NBR : NBR + 1] * (1.0 / 512.0))
    cell = lanes((16, 128)).astype(F32) + rank * 512.0
    sums = jnp.zeros((32, 256), F32)
    for j in range(NC):
        parts = [weights(table, cell + 128.0 * part, j) for part in range(4)]
        pieces = halves(jnp.concatenate(parts, axis=1))
        sums = sums + jnp.dot(
            jnp.concatenate(pieces, axis=0), u_ref[j], preferred_element_type=F32
        )
    sums_ref[...] = sums[0:16, :] + sums[16:32, :]
    upper_ref[...], rest_ref[...] = halves(s_ref[...])


def own_part(jac, nbr, trial, inverse):
    return pl.pallas_call(
        own_kernel,
        out_shape=[
            jax.ShapeDtypeStruct((16, 256), F32),
            jax.ShapeDtypeStruct(inverse.shape, BF16),
            jax.ShapeDtypeStruct(inverse.shape, BF16),
        ],
        in_specs=[VMEM] * 4,
        out_specs=[VMEM] * 3,
        compiler_params=PARAMS,
        name="own_part",
    )(jac, nbr, trial, inverse)


def sample_kernel(x_ref, nbr_ref, edge_ref, own_ref, u_ref, out_ref):
    rank = jnp.floor(nbr_ref[0:1, 0:1].astype(F32) * (1.0 / 512.0))
    place = rank - 16.0 * jnp.floor(rank * 0.0625)
    lane = lanes((1, 128))
    total = jnp.zeros((8, 2, 128), F32)
    blank = jnp.zeros((4, 2, 128), F32)
    near = [blank, blank, blank]
    extra = jnp.zeros((1, 128), F32)
    for p in range(16):
        total = total + x_ref[12 * p : 12 * p + 8]
        packed = x_ref[12 * p + 8 : 12 * p + 12]
        near = [
            near[k] + jnp.where((place == p + 1 - k)[None], packed, 0.0) for k in range(3)
        ]
        extra = extra + jnp.where(lane == GROUP_CNT + p, packed[0, 0:1, :], 0.0)
    total = total.reshape(16, 128)
    tables = []
    for k, edge in ((0, 0.0), (1, None), (2, 15.0)):
        rows = near[k].reshape(8, 128)
        if edge is not None:
            rows = jnp.where(place == edge, edge_ref[...], rows)
        rows = jnp.concatenate([rows, pltpu.roll(rows, 64, 1)], axis=0)
        if k < 2:
            extra = extra + jnp.where(lane == LOW_CNT + k, rows[0:1, CNT : CNT + 1], 0.0)
        tables.append(rows)
    cell = lanes((16, 128)).astype(F32) + rank * 512.0
    low_table, high_table = alive(tables[0]), alive(tables[2])
    slot = lax.broadcasted_iota(jnp.int32, (16, 256), 0).astype(F32)
    own = jnp.where(slot < tables[1][:, CNT : CNT + 1], own_ref[...], 0.0)
    low = jnp.zeros((32, 256), F32)
    high = jnp.zeros((32, 256), F32)
    for j in range(NC):
        pieces = halves(weights(low_table, cell, j))
        low = low + jnp.dot(
            jnp.concatenate(pieces, axis=0), u_ref[j, 0:128, :], preferred_element_type=F32
        )
        pieces = halves(weights(high_table, cell + 384.0, j))
        high = high + jnp.dot(
            jnp.concatenate(pieces, axis=0), u_ref[j, 384:512, :], preferred_element_type=F32
        )
    rows = jnp.concatenate(
        [low[0:16, :] + low[16:32, :], own, high[0:16, :] + high[16:32, :]], axis=0
    )
    b_exp, g_exp = exponent(rows), exponent(total)
    rows = jnp.concatenate([coded(rows, b_exp), jnp.zeros((80, 256), F32)], axis=0)
    extra = extra + jnp.where(lane == RANK, rank, 0.0)
    extra = extra + jnp.where(lane == B_EXP, b_exp, 0.0) + jnp.where(lane == G_EXP, g_exp, 0.0)
    cols = rows.T
    code = coded(total, g_exp)
    for z in range(8):
        left = cols[32 * z : 32 * z + 16, :]
        right = pltpu.roll(cols[32 * z + 16 : 32 * z + 32, :], 48, 1)
        out_ref[z] = to_i16(jnp.concatenate([code, left + right + extra], axis=0))


def sample(g_parts, nbr, edge, own, trial):
    return pl.pallas_call(
        sample_kernel,
        out_shape=jax.ShapeDtypeStruct((8, 32, 128), jnp.int16),
        in_specs=[VMEM] * 5,
        out_specs=VMEM,
        compiler_params=PARAMS,
        name="sample",
    )(g_parts, nbr, edge, own, trial)


def fold_kernel(x_ref, upper_ref, rest_ref, out_ref):
    blocks = [from_i16(x_ref[z]) for z in range(8)]
    info = jnp.concatenate([block[16:17, :] for block in blocks], axis=0)
    lane = lanes((8, 128))

    def column(k):
        return jnp.sum(jnp.where(lane == k, info, 0.0), axis=1, keepdims=True)

    g_scale = jnp.exp2(-column(G_EXP))
    b_scale = jnp.exp2(-column(B_EXP))
    total = jnp.zeros((16, 128), F32)
    for z in range(8):
        total = total + decoded(blocks[z][0:16, :]) * g_scale[z : z + 1, :]
    rank = column(RANK)
    place = rank - 16.0 * jnp.floor(rank * 0.0625)
    is_count = (lane >= GROUP_CNT) & (lane < GROUP_CNT + 16)
    counts = jnp.where(is_count, info, 0.0)
    before = lax.broadcasted_iota(jnp.int32, (8, 8), 1) < lax.broadcasted_iota(
        jnp.int32, (8, 8), 0
    )
    lower = jnp.dot(before.astype(F32), counts, preferred_element_type=F32)
    ahead = (lane - GROUP_CNT).astype(F32) < place
    lower = lower + jnp.where(ahead, counts, 0.0)
    offset = jnp.sum(lower, axis=1, keepdims=True)
    shift = jnp.where(lane < 16, -column(LOW_CNT), jnp.where(lane < 32, 0.0, column(OWN_CNT)))
    ids = jnp.where(lane < 48, offset + shift + (lane % 16).astype(F32), -1.0)
    at = lanes((1, 128))
    mode = lax.broadcasted_iota(jnp.int32, (512, 128), 0).astype(F32)
    sampled = jnp.zeros((64, 512), F32)
    for z in range(0, 8, 2):
        here, there = (
            decoded(blocks[k][16:32, :]) * b_scale[k : k + 1, :] for k in (z, z + 1)
        )
        first = jnp.where(at < 48, here, jnp.where(at < 96, pltpu.roll(there, 48, 1), 0.0))
        second = jnp.where(at < 48, pltpu.roll(here, 80, 1), jnp.where(at < 96, there, 0.0))
        row = jnp.where(at < 48, ids[z : z + 1, :], pltpu.roll(ids[z + 1 : z + 2, :], 48, 1))
        hot = jnp.where(mode == row, 1.0, 0.0).astype(BF16)
        pieces = halves(jnp.concatenate([first, second], axis=0))
        sampled = sampled + lax.dot_general(
            jnp.concatenate(pieces, axis=0),
            hot,
            (((1,), (1,)), ((), ())),
            preferred_element_type=F32,
        )
    sampled = sampled[0:32, :] + sampled[32:64, :]
    upper, rest = halves(sampled)
    c = lax.dot_general(
        jnp.concatenate([upper, rest], axis=0),
        upper_ref[...],
        (((1,), (1,)), ((), ())),
        preferred_element_type=F32,
    )
    c = (c[0:32, :] + c[32:64, :]) + lax.dot_general(
        upper, rest_ref[...], (((1,), (1,)), ((), ())), preferred_element_type=F32
    )
    g_pairs = total.reshape(8, 2, 128)
    c_pairs = c.reshape(16, 2, 128)
    for p in range(16):
        for m in range(4):
            at = 3 * (4 * p + m)
            out_ref[at : at + 2] = g_pairs[2 * m : 2 * m + 2]
            out_ref[at + 2] = c_pairs[p]


def fold(parts, upper, rest):
    return pl.pallas_call(
        fold_kernel,
        out_shape=jax.ShapeDtypeStruct((192, 2, 128), F32),
        in_specs=[VMEM] * 3,
        out_specs=VMEM,
        compiler_params=PARAMS,
        name="fold",
    )(parts, upper, rest)


def finish_kernel(x_ref, out_ref):
    sums = [jnp.zeros((64, 128), F32), jnp.zeros((64, 128), F32)]
    for m in range(4):
        rows = [x_ref[3 * (4 * p + m) : 3 * (4 * p + m) + 2] for p in range(16)]
        rows = jnp.concatenate(rows, axis=0).reshape(64, 128)
        c = x_ref[3 * m + 2]
        for p in range(1, 16):
            c = c + x_ref[3 * (4 * p + m) + 2]
        sums = [sums[j] + rows * c[j : j + 1, :] for j in range(2)]
    total = jnp.sum(jnp.concatenate(sums, axis=0).T, axis=0, keepdims=True)
    out_ref[0:1, :] = total[:, 0:64]
    out_ref[1:2, :] = total[:, 64:128]


def finish(parts):
    return pl.pallas_call(
        finish_kernel,
        out_shape=jax.ShapeDtypeStruct((2, 64), F32),
        in_specs=[VMEM] * 1,
        out_specs=VMEM,
        compiler_params=PARAMS,
        name="finish",
    )(parts)


def shards(test_basis, deim_basis, trial_basis, jacobian, neighbours, counts, sample_inverse):
    jac, nbr, count = jacobian.transpose(2, 1, 0), neighbours.T, counts.reshape(1, 1)
    g_part, own = prepare(test_basis.swapaxes(0, 1), deim_basis.swapaxes(0, 1), jac, nbr, count)
    groups, group = lax.axis_size(ROWS), lax.axis_size(GROUP)
    across = [(i - 1, i) for i in range(group, groups, group)]
    across += [(target, source) for source, target in across]
    edge = lax.ppermute(own, ROWS, across)
    g_group = lax.all_to_all(g_part, GROUP, 0, 0, tiled=True)
    trial = trial_basis.swapaxes(0, 1)
    mine, upper, rest = own_part(jac, nbr, trial, sample_inverse)
    sent = sample(g_group, nbr, edge, mine, trial)
    parts = lax.all_to_all(sent, "zh", 0, 0, tiled=True)
    pieces = lax.all_to_all(fold(parts, upper, rest), CUBE, 0, 0, tiled=True)
    return finish(pieces).T


def solution(mesh):
    split = Mesh(mesh.devices.reshape(8, 2, 4, 2, 4), ("zh", "zl", "x", "c", "y"))
    placed = (
        P(ROWS, None, None),
        P(ROWS, None, "y"),
        P(ROWS, None, None),
        P(ROWS, None, None),
        P(ROWS, None),
        P(ROWS),
        P("y", None),
    )
    return jax.shard_map(
        shards, mesh=split, in_specs=placed, out_specs=P("y", ROWS), check_vma=False
    )
```

```python
import jax
import jax.numpy as jnp
from jax import lax
from jax.experimental import pallas as pl
from jax.experimental.pallas import tpu as pltpu
from jax.sharding import Mesh
from jax.sharding import PartitionSpec as P

ROWS = ("zh", "zl", "x", "c")
GROUP = ("zl", "x", "c")
CUBE = ("y", "zl", "x", "c")
F32 = jnp.float32
BF16 = jnp.bfloat16
NC, NB = 5, 7
NBR, CNT = 40, 47
LOW_CNT, OWN_CNT, RANK, G_EXP, B_EXP, GROUP_CNT = 96, 97, 98, 99, 100, 112
TOP = 32000.0


VMEM = pl.BlockSpec(memory_space=pltpu.VMEM)
HBM = pl.BlockSpec(memory_space=pltpu.HBM)
PARAMS = pltpu.CompilerParams(vmem_limit_bytes=12 * 1024 * 1024)


def lanes(shape):
    return lax.broadcasted_iota(jnp.int32, shape, len(shape) - 1)


def exponent(x):
    top = jnp.max(jnp.abs(x), axis=(0, 1), keepdims=True)
    return jnp.floor(-jnp.log2(jnp.maximum(top, 1e-37)))


def coded(x, exp):
    code = jnp.floor(jnp.sqrt(jnp.sqrt(jnp.abs(x * jnp.exp2(exp)))) * TOP + 0.5)
    return jnp.where(x < 0.0, -code, code)


def decoded(code):
    root = code * (1.0 / TOP)
    square = root * root
    return square * square * jnp.where(code < 0.0, -1.0, 1.0)


def to_i16(x):
    return x.astype(jnp.int32).astype(jnp.int16)


def from_i16(x):
    return x.astype(jnp.int32).astype(F32)


def table_of(jac_ref, nbr_ref, count):
    blank = jnp.zeros((1, 16), F32)
    rows = []
    for j in range(NC):
        rows += [jac_ref[j], blank]
    rows += [nbr_ref[...].astype(F32), jnp.broadcast_to(count, (1, 16))]
    table = jnp.concatenate(rows + [jnp.zeros((80, 16), F32)], axis=0)
    table = jnp.concatenate([table, jnp.zeros((128, 112), F32)], axis=1)
    return table.T[0:16, :]


def prepare_kernel(
    v_hbm,
    d_hbm,
    jac_hbm,
    nbr_hbm,
    count_hbm,
    g_ref,
    table_ref,
    v_ref,
    d_ref,
    jac_ref,
    nbr_ref,
    count_ref,
    sems,
):
    small = [
        pltpu.make_async_copy(jac_hbm, jac_ref, sems.at[2 * NC]),
        pltpu.make_async_copy(nbr_hbm, nbr_ref, sems.at[2 * NC + 1]),
        pltpu.make_async_copy(count_hbm, count_ref, sems.at[2 * NC + 2]),
    ]
    v_copies = [
        pltpu.make_async_copy(v_hbm.at[j], v_ref.at[j], sems.at[j]) for j in range(NC)
    ]
    d_copies = [
        pltpu.make_async_copy(d_hbm.at[j], d_ref.at[j], sems.at[NC + j]) for j in range(NC)
    ]
    for copy in small:
        copy.start()
    for j in range(NC):
        v_copies[j].start()
        d_copies[j].start()
    for copy in small:
        copy.wait()
    count = count_ref[0, 0].astype(F32)
    table = table_of(jac_ref, nbr_ref, count)
    packed = table[0:8, :] + pltpu.roll(table[8:16, :], 64, 1)
    packed = packed + jnp.where(lanes((8, 128)) >= GROUP_CNT, count, 0.0)
    table_ref[...] = packed
    packed = packed.reshape(4, 2, 128)
    acc = jnp.zeros((128, 256), F32)
    for j in range(NC):
        v_copies[j].wait()
        d_copies[j].wait()
        acc = acc + lax.dot_general(
            d_ref[j], v_ref[j], (((0,), (0,)), ((), ())), preferred_element_type=F32
        )
    pairs = acc.T.reshape(128, 2, 128)
    for p in range(16):
        for m in range(4):
            at = 32 * m + 2 * p
            g_ref[12 * p + 2 * m : 12 * p + 2 * m + 2] = pairs[at : at + 2]
        g_ref[12 * p + 8 : 12 * p + 12] = packed


def prepare(test, deim, jac, nbr, counts):
    return pl.pallas_call(
        prepare_kernel,
        in_specs=[HBM, HBM, HBM, HBM, HBM],
        out_specs=[VMEM, VMEM],
        out_shape=[
            jax.ShapeDtypeStruct((192, 2, 128), F32),
            jax.ShapeDtypeStruct((8, 128), F32),
        ],
        scratch_shapes=[
            pltpu.VMEM(test.shape, BF16),
            pltpu.VMEM(deim.shape, BF16),
            pltpu.VMEM((NC, NB, 16), F32),
            pltpu.VMEM((NB, 16), jnp.int32),
            pltpu.SMEM((1, 1), jnp.int32),
            pltpu.SemaphoreType.DMA((2 * NC + 3,)),
        ],
        name="prepare",
    )(test, deim, jac, nbr, counts)


def halves(x):
    upper = x.astype(BF16)
    return upper, (x - upper.astype(F32)).astype(BF16)


def alive(rows):
    slot = lax.broadcasted_iota(jnp.int32, (16, 128), 0).astype(F32)
    dead = (lanes((16, 128)) < NBR) & (slot >= rows[:, CNT : CNT + 1])
    return jnp.where(dead, 0.0, rows)


def weights(table, cell, j):
    weight = jnp.zeros((16, 128), F32)
    for n in range(NB):
        hit = cell == table[:, NBR + n : NBR + n + 1]
        weight = weight + jnp.where(hit, table[:, 8 * j + n : 8 * j + n + 1], 0.0)
    return weight


def own_kernel(jac_ref, nbr_ref, u_ref, s_ref, sums_ref, upper_ref, rest_ref):
    table = table_of(jac_ref, nbr_ref, 0.0)
    rank = jnp.floor(table[0:1, NBR : NBR + 1] * (1.0 / 512.0))
    cell = lanes((16, 128)).astype(F32) + rank * 512.0
    sums = jnp.zeros((32, 256), F32)
    for j in range(NC):
        parts = [weights(table, cell + 128.0 * part, j) for part in range(4)]
        pieces = halves(jnp.concatenate(parts, axis=1))
        sums = sums + jnp.dot(
            jnp.concatenate(pieces, axis=0), u_ref[j], preferred_element_type=F32
        )
    sums_ref[...] = sums[0:16, :] + sums[16:32, :]
    upper_ref[...], rest_ref[...] = halves(s_ref[...])


def own_part(jac, nbr, trial, inverse):
    return pl.pallas_call(
        own_kernel,
        out_shape=[
            jax.ShapeDtypeStruct((16, 256), F32),
            jax.ShapeDtypeStruct(inverse.shape, BF16),
            jax.ShapeDtypeStruct(inverse.shape, BF16),
        ],
        in_specs=[VMEM] * 4,
        out_specs=[VMEM] * 3,
        compiler_params=PARAMS,
        name="own_part",
    )(jac, nbr, trial, inverse)


def sample_kernel(x_ref, nbr_ref, edge_ref, own_ref, u_ref, out_ref):
    rank = jnp.floor(nbr_ref[0:1, 0:1].astype(F32) * (1.0 / 512.0))
    place = rank - 16.0 * jnp.floor(rank * 0.0625)
    lane = lanes((1, 128))
    total = jnp.zeros((8, 2, 128), F32)
    blank = jnp.zeros((4, 2, 128), F32)
    near = [blank, blank, blank]
    extra = jnp.zeros((1, 128), F32)
    for p in range(16):
        total = total + x_ref[12 * p : 12 * p + 8]
        packed = x_ref[12 * p + 8 : 12 * p + 12]
        near = [
            near[k] + jnp.where((place == p + 1 - k)[None], packed, 0.0) for k in range(3)
        ]
        extra = extra + jnp.where(lane == GROUP_CNT + p, packed[0, 0:1, :], 0.0)
    total = total.reshape(16, 128)
    tables = []
    for k, edge in ((0, 0.0), (1, None), (2, 15.0)):
        rows = near[k].reshape(8, 128)
        if edge is not None:
            rows = jnp.where(place == edge, edge_ref[...], rows)
        rows = jnp.concatenate([rows, pltpu.roll(rows, 64, 1)], axis=0)
        if k < 2:
            extra = extra + jnp.where(lane == LOW_CNT + k, rows[0:1, CNT : CNT + 1], 0.0)
        tables.append(rows)
    cell = lanes((16, 128)).astype(F32) + rank * 512.0
    low_table, high_table = alive(tables[0]), alive(tables[2])
    slot = lax.broadcasted_iota(jnp.int32, (16, 256), 0).astype(F32)
    own = jnp.where(slot < tables[1][:, CNT : CNT + 1], own_ref[...], 0.0)
    low = jnp.zeros((32, 256), F32)
    high = jnp.zeros((32, 256), F32)
    for j in range(NC):
        pieces = halves(weights(low_table, cell, j))
        low = low + jnp.dot(
            jnp.concatenate(pieces, axis=0), u_ref[j, 0:128, :], preferred_element_type=F32
        )
        pieces = halves(weights(high_table, cell + 384.0, j))
        high = high + jnp.dot(
            jnp.concatenate(pieces, axis=0), u_ref[j, 384:512, :], preferred_element_type=F32
        )
    rows = jnp.concatenate(
        [low[0:16, :] + low[16:32, :], own, high[0:16, :] + high[16:32, :]], axis=0
    )
    b_exp, g_exp = exponent(rows), exponent(total)
    rows = jnp.concatenate([coded(rows, b_exp), jnp.zeros((80, 256), F32)], axis=0)
    extra = extra + jnp.where(lane == RANK, rank, 0.0)
    extra = extra + jnp.where(lane == B_EXP, b_exp, 0.0) + jnp.where(lane == G_EXP, g_exp, 0.0)
    cols = rows.T
    code = coded(total, g_exp)
    for z in range(8):
        left = cols[32 * z : 32 * z + 16, :]
        right = pltpu.roll(cols[32 * z + 16 : 32 * z + 32, :], 48, 1)
        out_ref[z] = to_i16(jnp.concatenate([code, left + right + extra], axis=0))


def sample(g_parts, nbr, edge, own, trial):
    return pl.pallas_call(
        sample_kernel,
        out_shape=jax.ShapeDtypeStruct((8, 32, 128), jnp.int16),
        in_specs=[VMEM] * 5,
        out_specs=VMEM,
        compiler_params=PARAMS,
        name="sample",
    )(g_parts, nbr, edge, own, trial)


def fold_kernel(x_ref, upper_ref, rest_ref, out_ref):
    blocks = [from_i16(x_ref[z]) for z in range(8)]
    info = jnp.concatenate([block[16:17, :] for block in blocks], axis=0)
    lane = lanes((8, 128))

    def column(k):
        return jnp.sum(jnp.where(lane == k, info, 0.0), axis=1, keepdims=True)

    g_scale = jnp.exp2(-column(G_EXP))
    b_scale = jnp.exp2(-column(B_EXP))
    total = jnp.zeros((16, 128), F32)
    for z in range(8):
        total = total + decoded(blocks[z][0:16, :]) * g_scale[z : z + 1, :]
    rank = column(RANK)
    place = rank - 16.0 * jnp.floor(rank * 0.0625)
    is_count = (lane >= GROUP_CNT) & (lane < GROUP_CNT + 16)
    counts = jnp.where(is_count, info, 0.0)
    before = lax.broadcasted_iota(jnp.int32, (8, 8), 1) < lax.broadcasted_iota(
        jnp.int32, (8, 8), 0
    )
    lower = jnp.dot(before.astype(F32), counts, preferred_element_type=F32)
    ahead = (lane - GROUP_CNT).astype(F32) < place
    lower = lower + jnp.where(ahead, counts, 0.0)
    offset = jnp.sum(lower, axis=1, keepdims=True)
    shift = jnp.where(lane < 16, -column(LOW_CNT), jnp.where(lane < 32, 0.0, column(OWN_CNT)))
    ids = jnp.where(lane < 48, offset + shift + (lane % 16).astype(F32), -1.0)
    at = lanes((1, 128))
    mode = lax.broadcasted_iota(jnp.int32, (512, 128), 0).astype(F32)
    sampled = jnp.zeros((64, 512), F32)
    for z in range(0, 8, 2):
        here, there = (
            decoded(blocks[k][16:32, :]) * b_scale[k : k + 1, :] for k in (z, z + 1)
        )
        first = jnp.where(at < 48, here, jnp.where(at < 96, pltpu.roll(there, 48, 1), 0.0))
        second = jnp.where(at < 48, pltpu.roll(here, 80, 1), jnp.where(at < 96, there, 0.0))
        row = jnp.where(at < 48, ids[z : z + 1, :], pltpu.roll(ids[z + 1 : z + 2, :], 48, 1))
        hot = jnp.where(mode == row, 1.0, 0.0).astype(BF16)
        pieces = halves(jnp.concatenate([first, second], axis=0))
        sampled = sampled + lax.dot_general(
            jnp.concatenate(pieces, axis=0),
            hot,
            (((1,), (1,)), ((), ())),
            preferred_element_type=F32,
        )
    sampled = sampled[0:32, :] + sampled[32:64, :]
    upper, rest = halves(sampled)
    c = lax.dot_general(
        jnp.concatenate([upper, rest], axis=0),
        upper_ref[...],
        (((1,), (1,)), ((), ())),
        preferred_element_type=F32,
    )
    c = (c[0:32, :] + c[32:64, :]) + lax.dot_general(
        upper, rest_ref[...], (((1,), (1,)), ((), ())), preferred_element_type=F32
    )
    g_pairs = total.reshape(8, 2, 128)
    c_pairs = c.reshape(16, 2, 128)
    for p in range(16):
        for m in range(4):
            at = 3 * (16 * m + p)
            out_ref[at : at + 2] = g_pairs[2 * m : 2 * m + 2]
            out_ref[at + 2] = c_pairs[p]


def fold(parts, upper, rest):
    return pl.pallas_call(
        fold_kernel,
        out_shape=jax.ShapeDtypeStruct((192, 2, 128), F32),
        in_specs=[VMEM] * 3,
        out_specs=VMEM,
        compiler_params=PARAMS,
        name="fold",
    )(parts, upper, rest)


def finish_kernel(x_ref, out_ref):
    sums = [jnp.zeros((64, 128), F32), jnp.zeros((64, 128), F32)]
    for m in range(4):
        rows = [x_ref[3 * (16 * m + p) : 3 * (16 * m + p) + 2] for p in range(16)]
        rows = jnp.concatenate(rows, axis=0).reshape(64, 128)
        c = x_ref[48 * m + 2]
        for p in range(1, 16):
            c = c + x_ref[3 * (16 * m + p) + 2]
        sums = [sums[j] + rows * c[j : j + 1, :] for j in range(2)]
    total = jnp.sum(jnp.concatenate(sums, axis=0).T, axis=0, keepdims=True)
    out_ref[0:1, :] = total[:, 0:64]
    out_ref[1:2, :] = total[:, 64:128]


def finish(parts):
    return pl.pallas_call(
        finish_kernel,
        out_shape=jax.ShapeDtypeStruct((2, 64), F32),
        in_specs=[VMEM] * 1,
        out_specs=VMEM,
        compiler_params=PARAMS,
        name="finish",
    )(parts)


def shards(test_basis, deim_basis, trial_basis, jacobian, neighbours, counts, sample_inverse):
    jac, nbr, count = jacobian.transpose(2, 1, 0), neighbours.T, counts.reshape(1, 1)
    g_part, own = prepare(test_basis.swapaxes(0, 1), deim_basis.swapaxes(0, 1), jac, nbr, count)
    groups, group = lax.axis_size(ROWS), lax.axis_size(GROUP)
    across = [(i - 1, i) for i in range(group, groups, group)]
    across += [(target, source) for source, target in across]
    edge = lax.ppermute(own, ROWS, across)
    g_group = lax.all_to_all(g_part, GROUP, 0, 0, tiled=True)
    trial = trial_basis.swapaxes(0, 1)
    mine, upper, rest = own_part(jac, nbr, trial, sample_inverse)
    sent = sample(g_group, nbr, edge, mine, trial)
    parts = lax.all_to_all(sent, "zh", 0, 0, tiled=True)
    pieces = lax.all_to_all(fold(parts, upper, rest), CUBE, 0, 0, tiled=True)
    return finish(pieces).T


def solution(mesh):
    split = Mesh(mesh.devices.reshape(8, 2, 4, 2, 4), ("zh", "zl", "x", "c", "y"))
    placed = (
        P(ROWS, None, None),
        P(ROWS, None, "y"),
        P(ROWS, None, None),
        P(ROWS, None, None),
        P(ROWS, None),
        P(ROWS),
        P("y", None),
    )
    return jax.shard_map(
        shards, mesh=split, in_specs=placed, out_specs=P("y", ROWS), check_vma=False
    )
```
